32 devices in a mesh: rows: 8 (over z, x), pos: 4 (over y, core).
Axes of the slice: x: 2, y: 2, z: 4, core: 2. Of those that a mesh axis runs over, the one named last changes fastest.
Arguments:
- tokens: bfloat16 [24, 640, 768], P('rows', 'pos'), may hold values from -6 to 6
- segments: int32 [24, 640], P('rows'), may hold values from 0 to 7, as said below
- w_query: bfloat16 [768, 768], replicated, may hold values from -0.21875 to 0.21875
- b_query: bfloat16 [768], replicated, may hold values from -3 to 3
- w_key: bfloat16 [768, 768], replicated, may hold values from -0.21875 to 0.21875
- w_value: bfloat16 [768, 768], replicated, may hold values from -0.21875 to 0.21875
- b_value: bfloat16 [768], replicated, may hold values from -3 to 3
- w_out: bfloat16 [768, 768], replicated, may hold values from -0.875 to 0.875
- b_out: bfloat16 [768], replicated, may hold values from -3 to 3
- gain_one: bfloat16 [768], replicated, may hold values from 0.5 to 1.5
- shift_one: bfloat16 [768], replicated, may hold values from -3 to 3
- w_up: bfloat16 [768, 3072], replicated, may hold values from -0.21875 to 0.21875
- b_up: bfloat16 [3072], replicated, may hold values from -3 to 3
- w_down: bfloat16 [3072, 768], replicated, may hold values from -0.109375 to 0.109375
- b_down: bfloat16 [768], replicated, may hold values from -3 to 3
- gain_two: bfloat16 [768], replicated, may hold values from 0.5 to 1.5
- shift_two: bfloat16 [768], replicated, may hold values from -3 to 3
- cotangent: bfloat16 [24, 640, 768], P('rows', 'pos'), may hold values from -6 to 6
Outputs:
- result: bfloat16 [24, 640, 768], P('rows', 'pos')
- grad_tokens: float32 [24, 640, 768], P('rows', 'pos')
- grad_w_query: float32 [768, 768], replicated
- grad_b_query: float32 [768], replicated
- grad_w_key: float32 [768, 768], replicated
- grad_w_value: float32 [768, 768], replicated
- grad_b_value: float32 [768], replicated
- grad_w_out: float32 [768, 768], replicated
- grad_b_out: float32 [768], replicated
- grad_gain_one: float32 [768], replicated
- grad_shift_one: float32 [768], replicated
- grad_w_up: float32 [768, 3072], replicated
- grad_b_up: float32 [3072], replicated
- grad_w_down: float32 [3072, 768], replicated
- grad_b_down: float32 [768], replicated
- grad_gain_two: float32 [768], replicated
- grad_shift_two: float32 [768], replicated
The draws below stay inside these ranges and needn't reach their ends.
Inputs may be any that keep to these rules, and one draw needn't show every extreme that they name: `segments`: each row's segment numbers start at 0, never fall, and rise by at most one from a position to the next.
All inputs are finite; a program needn't handle non-finite values.
Results may differ from the reference program's by a relative error of at most 0.014.
Values may be sent and summed in bfloat16 or wider, within the bound.
A program may use at most 192 MiB of HBM per device.

```python
import jax
import jax.numpy as jnp
from jax import lax

D = 768
HEADS = 12
HEAD_DIM = 64
FF = 3072
ROW_LEN = 640
SEGS = 8
R_DEV = 3
ROWS = 24


def draw_segments(key, part):
    key = jax.random.fold_in(key, 11)
    key_cuts, key_count, key_whole = jax.random.split(key, 3)
    row_keys = jax.random.split(key_cuts, ROWS)

    def pick_cuts(row_key):
        return jax.random.permutation(row_key, ROW_LEN - 1)[:SEGS - 1] + 1
    cut_pos = jax.vmap(pick_cuts)(row_keys).astype(jnp.int32)
    counts = jax.random.randint(key_count, (ROWS, 1), 0, SEGS)
    whole_row = jax.random.randint(key_whole, (), 0, ROWS)
    row_ids = jnp.arange(ROWS)[:, None]
    counts = jnp.where(row_ids == whole_row, 0, counts)
    counts = jnp.where(row_ids == (whole_row + 1) % ROWS, SEGS - 1, counts)
    active = jnp.arange(SEGS - 1)[None, :] < counts
    cut_pos = jnp.where(active, cut_pos, ROW_LEN)
    places = jnp.arange(ROW_LEN)
    hits = (places[None, :, None] >= cut_pos[:, None, :]).astype(jnp.int32)
    return jnp.sum(hits, axis=-1).astype(jnp.int32)


def shard_levels(stream_key, extent, cuts, smallest, largest):
    def one(axis_at, parts):
        draws = jax.random.uniform(jax.random.fold_in(jax.random.fold_in(stream_key, 6), axis_at), (parts,), jnp.float32, smallest / len(cuts), largest / len(cuts))
        return jnp.repeat(jnp.exp(draws), extent[axis_at] // parts).reshape((-1,) + (1,) * (len(extent) - axis_at - 1))

    level = one(*cuts[0])
    for cut in cuts[1:]:
        level = level * one(*cut)
    return level


def gaussian(key, shape, spread, most, pieces=(), dtype=jnp.bfloat16):
    array = spread * jax.random.normal(key, shape, jnp.float32)
    if pieces:
        array = array * shard_levels(key, shape, pieces, -0.22, 0.18)
    return jnp.clip(array, -most, most).astype(dtype)


def setup_inputs(seed: int = 0) -> dict:
    seeds = jax.random.split(jax.random.key(seed), 19)
    return {
        "tokens": gaussian(seeds[0], (ROWS, ROW_LEN, D), 1.0, 6.0, ((0, 8), (1, 4))),
        "segments": draw_segments(jax.random.fold_in(seeds[18], 71), 0),
        "w_query": gaussian(seeds[2], (D, D), D ** -0.5, 0.21875),
        "b_query": gaussian(seeds[3], (D,), 0.5, 3.0),
        "w_key": gaussian(seeds[4], (D, D), D ** -0.5, 0.21875),
        "w_value": gaussian(seeds[5], (D, D), D ** -0.5, 0.21875),
        "b_value": gaussian(seeds[6], (D,), 0.5, 3.0),
        "w_out": gaussian(seeds[7], (D, D), (D // 16) ** -0.5, 0.875),
        "b_out": gaussian(seeds[8], (D,), 0.5, 3.0),
        "gain_one": jnp.clip(1.0 + 0.1 * jax.random.normal(seeds[9], (D,), jnp.float32), 0.5, 1.5).astype(jnp.bfloat16),
        "shift_one": gaussian(seeds[10], (D,), 0.5, 3.0),
        "w_up": gaussian(seeds[11], (D, FF), D ** -0.5, 0.21875),
        "b_up": gaussian(seeds[12], (FF,), 0.5, 3.0),
        "w_down": gaussian(seeds[13], (FF, D), FF ** -0.5, 0.109375),
        "b_down": gaussian(seeds[14], (D,), 0.5, 3.0),
        "gain_two": jnp.clip(1.0 + 0.1 * jax.random.normal(seeds[15], (D,), jnp.float32), 0.5, 1.5).astype(jnp.bfloat16),
        "shift_two": gaussian(seeds[16], (D,), 0.5, 3.0),
        "cotangent": gaussian(seeds[17], (ROWS, ROW_LEN, D), 1.0, 6.0, ((0, 8), (1, 4))),
    }


@jax.custom_vjp
def low(v):
    return lax.optimization_barrier(v.astype(jnp.bfloat16)).astype(jnp.float32)

@jax.custom_vjp
def low_back(v):
    return v

def low_keep(v):
    return (low(v), None)

def low_pass(kept, grad):
    return (grad,)

def back_keep(v):
    return (v, None)

def back_low(kept, grad):
    return (low(grad),)
low.defvjp(low_keep, low_pass)
low_back.defvjp(back_keep, back_low)
HIGH = lax.Precision.HIGHEST
EPS = 1e-05
MASKED = -1000000000.0

def layer_norm(v, gain, shift):
    mean_row = lax.optimization_barrier(jnp.mean(v, axis=-1, keepdims=True))
    centred = v - mean_row
    variance = lax.optimization_barrier(jnp.mean(centred * centred, axis=-1, keepdims=True))
    return centred * lax.rsqrt(variance + EPS) * gain + shift

def project(a, w):
    return jnp.einsum('gld,de->gle', a, w, precision=HIGH)

def block_forward(block_tokens, block_segs, params):
    w_query, b_query, w_key, w_value, b_value, w_out, b_out, gain_one, shift_one, w_up, b_up, w_down, b_down, gain_two, shift_two = params
    group_rows, length, feature_width = block_tokens.shape
    split = (group_rows, length, HEADS, HEAD_DIM)
    queries = low(low_back(project(block_tokens, w_query) + b_query)).reshape(split)
    key_rows = low(low_back(project(block_tokens, w_key))).reshape(split)
    value_rows = low(low_back(project(block_tokens, w_value) + b_value)).reshape(split)
    raw_scores = jnp.einsum('gqhd,gkhd->ghqk', queries, key_rows, precision=HIGH) * HEAD_DIM ** (-0.5)
    raw_scores = low_back(raw_scores)
    same_doc = (block_segs[:, :, None] == block_segs[:, None, :])[:, None]
    scores = jnp.where(same_doc, raw_scores, MASKED)
    row_top = lax.optimization_barrier(jnp.max(scores, axis=-1, keepdims=True))
    exponent = jnp.exp(scores - row_top)
    prob_rows = low(exponent / lax.optimization_barrier(jnp.sum(exponent, axis=-1, keepdims=True)))
    heads_mixed = jnp.einsum('ghqk,gkhd->gqhd', prob_rows, value_rows, precision=HIGH)
    heads_mixed = low(low_back(heads_mixed.reshape(group_rows, length, feature_width)))
    attended = low_back(project(heads_mixed, w_out) + b_out)
    normed = layer_norm(block_tokens + attended, gain_one, shift_one)
    upper_in = low_back(project(low(normed), w_up) + b_up)
    active = low(jax.nn.gelu(upper_in, approximate=False))
    down_out = low_back(project(active, w_down) + b_down)
    return layer_norm(normed + down_out, gain_two, shift_two)

def reference(tokens, segments, w_query, b_query, w_key, w_value, b_value, w_out, b_out, gain_one, shift_one, w_up, b_up, w_down, b_down, gain_two, shift_two, cotangent):
    params = tuple((p.astype(jnp.float32) for p in (w_query, b_query, w_key, w_value, b_value, w_out, b_out, gain_one, shift_one, w_up, b_up, w_down, b_down, gain_two, shift_two)))
    tokens_full = tokens.astype(jnp.float32)
    segs_grouped = segments.reshape(ROWS // R_DEV, R_DEV, ROW_LEN)

    def forward(tokens_in, weights):
        grouped = tokens_in.reshape(ROWS // R_DEV, R_DEV, ROW_LEN, D)

        def per_block(pair):
            return block_forward(pair[0], pair[1], weights)
        outputs = lax.map(jax.checkpoint(per_block), (grouped, segs_grouped))
        return outputs.reshape(ROWS, ROW_LEN, D)
    output, puller = jax.vjp(forward, tokens_full, params)
    grad_in, grads = puller(cotangent.astype(jnp.float32))
    return (output.astype(jnp.bfloat16), grad_in, grads[0], grads[1], grads[2], grads[3], grads[4], grads[5], grads[6], grads[7], grads[8], grads[9], grads[10], grads[11], grads[12], grads[13], grads[14])
```

```python
from functools import partial

import jax
import jax.numpy as jnp
from jax import lax
from jax.experimental import pallas as pl
from jax.experimental.pallas import tpu as pltpu
from jax.sharding import PartitionSpec as P

HEADS = 12
HEAD_DIM = 64


EPS = 1e-05
MASKED = -1000000000.0


def layer_norm(v, gain, shift):
    mean_row = jnp.mean(v, axis=-1, keepdims=True)
    centred = v - mean_row
    variance = jnp.mean(centred * centred, axis=-1, keepdims=True)
    return centred * lax.rsqrt(variance + EPS) * gain + shift


def tokens_dot(a, w):
    return jnp.einsum("rpd,de->rpe", a, w, preferred_element_type=jnp.float32)


def weight_grad(a, g):
    return jnp.einsum("rpd,rpe->de", a, g, preferred_element_type=jnp.float32)


def back_dot(g, w):
    return jnp.einsum("rpe,de->rpd", g, w, preferred_element_type=jnp.float32)


def token_sum(g):
    return jnp.sum(g.astype(jnp.float32), axis=(0, 1))


def split_heads(a):
    return a.reshape(a.shape[0], HEADS, HEAD_DIM)


def row_scores(query_row, key_row, same_row):
    raw_scores = jnp.einsum(
        "qhd,khd->hqk",
        split_heads(query_row),
        split_heads(key_row),
        preferred_element_type=jnp.float32,
    ) * HEAD_DIM ** (-0.5)
    return jnp.where(same_row[None], raw_scores, MASKED)


def attend_row(piece):
    query_row, key_row, value_row, same_row = piece
    scores = row_scores(query_row, key_row, same_row)
    row_top = jnp.max(scores, axis=-1, keepdims=True)
    exponent = jnp.exp(scores - row_top)
    row_total = jnp.sum(exponent, axis=-1, keepdims=True)
    log_total = row_top + jnp.log(row_total)
    prob_low = (exponent / row_total).astype(jnp.bfloat16)
    mixed = jnp.einsum(
        "hqk,khd->qhd", prob_low, split_heads(value_row), preferred_element_type=jnp.float32
    )
    mixed = mixed.reshape(query_row.shape[0], query_row.shape[1]).astype(jnp.bfloat16)
    return (mixed, log_total)


def score_grads(query_row, key_row, value_row, grad_row, same_row, log_total):
    prob_again = jnp.exp(row_scores(query_row, key_row, same_row) - log_total)
    grad_probs = jnp.einsum(
        "qhd,khd->hqk",
        split_heads(grad_row),
        split_heads(value_row),
        preferred_element_type=jnp.float32,
    )
    return (prob_again, grad_probs)


def attend_back(piece):
    query_row, key_row, value_row, grad_row, same_row, log_total = piece
    prob_again, grad_probs = score_grads(
        query_row, key_row, value_row, grad_row, same_row, log_total
    )
    row_inner = jnp.sum(grad_probs * prob_again, axis=-1, keepdims=True)
    grad_scores = (prob_again * (grad_probs - row_inner)).astype(jnp.bfloat16)
    grad_query = jnp.einsum(
        "hqk,khd->qhd", grad_scores, split_heads(key_row), preferred_element_type=jnp.float32
    ) * HEAD_DIM ** (-0.5)
    grad_query = grad_query.reshape(query_row.shape[0], query_row.shape[1]).astype(jnp.bfloat16)
    key_terms = jnp.einsum(
        "hqk,qhd->khd", grad_scores, split_heads(query_row), preferred_element_type=jnp.float32
    ) * HEAD_DIM ** (-0.5)
    value_terms = jnp.einsum(
        "hqk,qhd->khd",
        prob_again.astype(jnp.bfloat16),
        split_heads(grad_row),
        preferred_element_type=jnp.float32,
    )
    key_terms = key_terms.reshape(key_row.shape[0], key_row.shape[1])
    value_terms = value_terms.reshape(key_row.shape[0], key_row.shape[1])
    return (grad_query, key_terms, value_terms)


MESH = pl.DeviceIdType.MESH


def flip(value, bit):
    return value + bit - 2 * bit * lax.rem(lax.div(value, bit), 2)


def bit_of(value, bit):
    return lax.rem(lax.div(value, bit), 2)


def axis_bits(size):
    assert size & (size - 1) == 0
    return [1 << i for i in range(size.bit_length() - 1)]


class Place:
    def __init__(self):
        self.row = lax.axis_index("rows")
        self.pos = lax.axis_index("pos")

    def partner(self, link):
        axis, bit = link
        if axis == "r":
            return (flip(self.row, bit), self.pos)
        return (self.row, flip(self.pos, bit))

    def side(self, link):
        axis, bit = link
        return bit_of(self.row if axis == "r" else self.pos, bit)


def window(ref, row0, rows, col0, cols):
    return ref.at[pl.ds(row0, rows), pl.ds(col0, cols)]


def plan_splits(rows, cols, links):
    kinds = []
    for _ in links:
        if (rows // 2) % 16 == 0:
            rows //= 2
            kinds.append("rows")
        elif (cols // 2) % 128 == 0:
            cols //= 2
            kinds.append("cols")
        else:
            kinds.append("whole")
    return kinds


def add_into(dst, left, right, rows):
    step = 16 if rows % 48 else 48

    @pl.loop(0, rows // step)
    def _(i):
        at = pl.ds(pl.multiple_of(i * step, step), step)
        dst[at, :] = (
            left[at, :].astype(jnp.float32) + right[at, :].astype(jnp.float32)
        ).astype(dst.dtype)


class Chunk:
    def __init__(self, place, index, links, src, out, total, landing, send_sem, recv_sem, copy_sem):
        self.place, self.index, self.links = place, index, links
        self.src, self.out, self.total = src, out, total
        self.send_sem, self.recv_sem, self.copy_sem = send_sem, recv_sem, copy_sem
        rows, cols = src.shape
        self.kinds = plan_splits(rows, cols, links)
        self.landing = landing
        self.row0, self.col0, self.rows, self.cols = 0, 0, rows, cols
        self.trail, self.sent, self.recv = [], [], None
        self.land_row = 0
        self.step_no = 0

    def steps(self):
        return 2 * len(self.links) + 1

    def halves(self, kind, side):
        rows, cols = self.rows, self.cols
        if kind == "rows":
            rows //= 2
            keep = (self.row0 + side * rows, self.col0)
            give = (self.row0 + (1 - side) * rows, self.col0)
        elif kind == "cols":
            cols //= 2
            keep = (self.row0, self.col0 + side * cols)
            give = (self.row0, self.col0 + (1 - side) * cols)
        else:
            keep = give = (self.row0, self.col0)
        return keep, give, rows, cols

    def at(self, ref, place, rows, cols):
        row0, col0 = place
        if not isinstance(row0, int):
            row0 = pl.multiple_of(row0, 16)
        if not isinstance(col0, int):
            col0 = pl.multiple_of(col0, 128)
        return window(ref, row0, rows, col0, cols)

    def send(self, link, src, dst):
        slot = len(self.sent)
        copy = pltpu.make_async_remote_copy(
            src_ref=src,
            dst_ref=dst,
            send_sem=self.send_sem.at[self.index, slot],
            recv_sem=self.recv_sem.at[self.index, slot],
            device_id=self.place.partner(link),
            device_id_type=MESH,
        )
        copy.start()
        self.sent.append(copy)
        self.recv = copy

    def start_reduce(self, number):
        link, kind = self.links[number], self.kinds[number]
        keep, give, rows, cols = self.halves(kind, self.place.side(link))
        base = self.src if number == 0 else self.total
        land = window(self.landing, self.land_row, rows, 0, cols)
        self.send(link, self.at(base, give, rows, cols), land)
        self.pending = (kind, keep, rows, cols, base, land)
        self.land_row += rows

    def finish_reduce(self):
        kind, keep, rows, cols, base, land = self.pending
        self.recv.wait_recv()
        if kind == "whole":
            self.sent[-1].wait_send()
        add_into(
            self.at(self.total, keep, rows, cols), self.at(base, keep, rows, cols), land, rows
        )
        self.trail.append((kind, self.row0, self.col0, self.rows, self.cols))
        (self.row0, self.col0), self.rows, self.cols = keep, rows, cols

    def held(self, ref):
        return self.at(ref, (self.row0, self.col0), self.rows, self.cols)

    def start_gather(self, number):
        if self.kinds[number] == "whole":
            return
        here = self.held(self.out)
        self.send(self.links[number], here, here)

    def finish_gather(self, number):
        kind, self.row0, self.col0, self.rows, self.cols = self.trail.pop()
        if kind != "whole":
            self.recv.wait_recv()

    def advance(self):
        count, now = len(self.links), self.step_no
        if now > 0 and now <= count:
            self.finish_reduce()
        elif now > count:
            self.finish_gather(2 * count - now)
        if now < count:
            self.start_reduce(now)
        elif now < 2 * count:
            if now == count:
                own = pltpu.make_async_copy(
                    self.held(self.total), self.held(self.out), self.copy_sem.at[self.index]
                )
                own.start()
                own.wait()
            self.start_gather(2 * count - 1 - now)
        else:
            for index, copy in enumerate(self.sent):
                if not (index < count and self.kinds[index] == "whole"):
                    copy.wait_send()
        self.step_no += 1


def landing_rows(rows, cols, links):
    total = 0
    for kind in plan_splits(rows, cols, links):
        if kind == "rows":
            rows //= 2
        total += rows
    return total


def greet(place, links):
    barrier = pltpu.get_barrier_semaphore()
    for link in links:
        pl.semaphore_signal(barrier, inc=1, device_id=place.partner(link), device_id_type=MESH)
    pl.semaphore_wait(barrier, len(links))


def sum_kernel(orders, *refs):
    count = len(orders)
    (q_in, k_in, v_in, o_in, up_in, down_in, small_in) = refs[:7]
    (q_out, k_out, v_out, o_out, up_out, down_out, small_out) = refs[7:14]
    total, landing, small_land, send_sem, recv_sem, copy_sem, small_sem = refs[14:]
    place = Place()
    links = orders[0]
    greet(place, links)
    width = q_in.shape[0]
    blocks = [(down_in, down_out, j * width, 0) for j in range(4)]
    blocks += [(up_in, up_out, 0, j * width) for j in range(4)]
    blocks += [(a, b, 0, 0) for a, b in ((o_in, o_out), (q_in, q_out), (k_in, k_out), (v_in, v_out))]
    chunks = [
        Chunk(
            place,
            index,
            orders[index],
            window(src, row0, width, col0, width),
            window(out, row0, width, col0, width),
            total.at[index],
            landing.at[index],
            send_sem,
            recv_sem,
            copy_sem,
        )
        for index, (src, out, row0, col0) in enumerate(blocks)
    ]
    small_out[...] = small_in[...]
    for wave in range(chunks[0].steps()):
        small = None
        if wave < len(links):
            small = pltpu.make_async_remote_copy(
                src_ref=small_out,
                dst_ref=small_land.at[wave],
                send_sem=small_sem.at[0, wave],
                recv_sem=small_sem.at[1, wave],
                device_id=place.partner(links[wave]),
                device_id_type=MESH,
            )
            small.start()
        for chunk in chunks:
            chunk.advance()
        if small is not None:
            small.wait()
            small_out[...] += small_land[wave]


def sum_gradients(mesh_shape, blocks, small):
    row_bits = [("r", bit) for bit in axis_bits(mesh_shape["rows"])]
    pos_bits = [("p", bit) for bit in axis_bits(mesh_shape["pos"])]
    one = [pos_bits[0], row_bits[0], *pos_bits[1:], *row_bits[1:]]
    two = [*pos_bits, *row_bits]
    orders = [one if index % 2 == 0 else two for index in range(12)]
    width = blocks[0].shape[0]
    steps = len(one)
    vmem = pl.BlockSpec(memory_space=pltpu.VMEM)
    hbm = pl.BlockSpec(memory_space=pl.ANY)
    return pl.pallas_call(
        partial(sum_kernel, orders),
        out_shape=[jax.ShapeDtypeStruct(b.shape, b.dtype) for b in blocks]
        + [jax.ShapeDtypeStruct(small.shape, small.dtype)],
        in_specs=[vmem] * 7,
        out_specs=[hbm] * 6 + [vmem],
        scratch_shapes=[
            pltpu.VMEM((12, width, width), jnp.bfloat16),
            pltpu.VMEM((12, landing_rows(width, width, one), width), jnp.bfloat16),
            pltpu.VMEM((steps, *small.shape), jnp.float32),
            pltpu.SemaphoreType.DMA((12, 2 * steps)),
            pltpu.SemaphoreType.DMA((12, 2 * steps)),
            pltpu.SemaphoreType.DMA((12,)),
            pltpu.SemaphoreType.DMA((2, steps)),
        ],
        compiler_params=pltpu.CompilerParams(
            collective_id=0, has_side_effects=True, vmem_limit_bytes=60 * 2**20
        ),
        name="sum_gradients",
    )(*blocks, small)


def on_device(
    mesh_shape,
    tokens,
    segments,
    w_query,
    b_query,
    w_key,
    w_value,
    b_value,
    w_out,
    b_out,
    gain_one,
    shift_one,
    w_up,
    b_up,
    w_down,
    b_down,
    gain_two,
    shift_two,
    cotangent,
):
    rows_n, part_len, feature_width = tokens.shape
    first_pos = lax.axis_index("pos") * part_len
    seg_here = lax.dynamic_slice_in_dim(segments, first_pos, part_len, 1)
    same_doc = seg_here[:, :, None] == segments[:, None, :]
    gain_onef = gain_one.astype(jnp.float32)
    shift_onef = shift_one.astype(jnp.float32)
    gain_twof = gain_two.astype(jnp.float32)
    shift_twof = shift_two.astype(jnp.float32)
    queries = (tokens_dot(tokens, w_query) + b_query).astype(jnp.bfloat16)
    key_part = tokens_dot(tokens, w_key).astype(jnp.bfloat16)
    value_part = (tokens_dot(tokens, w_value) + b_value).astype(jnp.bfloat16)
    key_rows, value_rows = (
        lax.all_gather(key_part, "pos", axis=1, tiled=True),
        lax.all_gather(value_part, "pos", axis=1, tiled=True),
    )
    heads_mixed, log_total = lax.map(attend_row, (queries, key_rows, value_rows, same_doc))
    attended = tokens_dot(heads_mixed, w_out) + b_out
    resid_one = tokens.astype(jnp.float32) + attended
    normed, pull_one = jax.vjp(layer_norm, resid_one, gain_onef, shift_onef)
    normed_low = normed.astype(jnp.bfloat16)
    upper_in = tokens_dot(normed_low, w_up) + b_up
    active, pull_gelu = jax.vjp(partial(jax.nn.gelu, approximate=False), upper_in)
    active = active.astype(jnp.bfloat16)
    down_out = tokens_dot(active, w_down) + b_down
    resid_two = normed + down_out
    result, pull_two = jax.vjp(layer_norm, resid_two, gain_twof, shift_twof)
    grad_two, grad_gain_two, grad_shift_two = pull_two(cotangent.astype(jnp.float32))
    grad_down = grad_two.astype(jnp.bfloat16)
    grad_w_down = weight_grad(active, grad_down)
    grad_b_down = token_sum(grad_down)
    (grad_upper,) = pull_gelu(back_dot(grad_down, w_down))
    grad_upper = grad_upper.astype(jnp.bfloat16)
    grad_w_up = weight_grad(normed_low, grad_upper)
    grad_b_up = token_sum(grad_upper)
    grad_normed = grad_two + back_dot(grad_upper, w_up)
    grad_one, grad_gain_one, grad_shift_one = pull_one(grad_normed)
    grad_attend = grad_one.astype(jnp.bfloat16)
    grad_w_out = weight_grad(heads_mixed, grad_attend)
    grad_b_out = token_sum(grad_attend)
    grad_mixed = back_dot(grad_attend, w_out).astype(jnp.bfloat16)
    key_back_rows, value_back_rows = (key_rows, value_rows)
    grad_query, key_terms, value_terms = lax.map(
        attend_back, (queries, key_back_rows, value_back_rows, grad_mixed, same_doc, log_total)
    )
    grad_keys, grad_values = (
        lax.psum_scatter(
            key_terms.astype(jnp.bfloat16), "pos", scatter_dimension=1, tiled=True
        ).astype(jnp.float32),
        lax.psum_scatter(
            value_terms.astype(jnp.bfloat16), "pos", scatter_dimension=1, tiled=True
        ).astype(jnp.float32),
    )
    grad_keys = grad_keys.astype(jnp.bfloat16)
    grad_values = grad_values.astype(jnp.bfloat16)
    grad_w_query = weight_grad(tokens, grad_query)
    grad_b_query = token_sum(grad_query)
    grad_w_key = weight_grad(tokens, grad_keys)
    grad_w_value = weight_grad(tokens, grad_values)
    grad_b_value = token_sum(grad_values)
    grad_tokens = (
        grad_one
        + back_dot(grad_query, w_query)
        + back_dot(grad_keys, w_key)
        + back_dot(grad_values, w_value)
    )
    small = jnp.concatenate(
        [
            grad_b_query,
            grad_b_value,
            grad_b_out,
            grad_gain_one,
            grad_shift_one,
            grad_b_down,
            grad_gain_two,
            grad_shift_two,
            grad_b_up,
        ]
    ).reshape(12, feature_width)
    low = jnp.bfloat16
    blocks = [
        g.astype(low)
        for g in (grad_w_query, grad_w_key, grad_w_value, grad_w_out, grad_w_up, grad_w_down)
    ]
    *blocks, small = sum_gradients(mesh_shape, blocks, jnp.pad(small, ((0, 4), (0, 0))))
    grad_w_query, grad_w_key, grad_w_value, grad_w_out, grad_w_up, grad_w_down = (
        b.astype(jnp.float32) for b in blocks
    )
    (
        grad_b_query,
        grad_b_value,
        grad_b_out,
        grad_gain_one,
        grad_shift_one,
        grad_b_down,
        grad_gain_two,
        grad_shift_two,
    ) = (small[i] for i in range(8))
    grad_b_up = small[8:12].reshape(-1)
    return (
        result.astype(jnp.bfloat16),
        grad_tokens,
        grad_w_query,
        grad_b_query,
        grad_w_key,
        grad_w_value,
        grad_b_value,
        grad_w_out,
        grad_b_out,
        grad_gain_one,
        grad_shift_one,
        grad_w_up,
        grad_b_up,
        grad_w_down,
        grad_b_down,
        grad_gain_two,
        grad_shift_two,
    )


def solution(mesh):
    return jax.shard_map(
        partial(on_device, dict(mesh.shape)),
        mesh=mesh,
        in_specs=(
            P("rows", "pos", None),
            P("rows", None),
            P(),
            P(),
            P(),
            P(),
            P(),
            P(),
            P(),
            P(),
            P(),
            P(),
            P(),
            P(),
            P(),
            P(),
            P(),
            P("rows", "pos", None),
        ),
        out_specs=(
            P("rows", "pos", None),
            P("rows", "pos", None),
            P(),
            P(),
            P(),
            P(),
            P(),
            P(),
            P(),
            P(),
            P(),
            P(),
            P(),
            P(),
            P(),
            P(),
            P(),
        ),
        check_vma=False,
    )
```

```python
from functools import partial

import jax
import jax.numpy as jnp
from jax import lax
from jax.experimental import pallas as pl
from jax.experimental.pallas import tpu as pltpu
from jax.sharding import PartitionSpec as P

HEADS = 12
HEAD_DIM = 64
EPS = 1e-05
MASKED = -1000000000.0
SCALE = HEAD_DIM ** (-0.5)
LANES = 128
VMEM_LIMIT = 60 * 2**20
MESH = pl.DeviceIdType.MESH
LOW = jnp.bfloat16
F32 = jnp.float32


def flip(value, bit):
    return value + bit - 2 * bit * lax.rem(lax.div(value, bit), 2)


def bit_of(value, bit):
    return lax.rem(lax.div(value, bit), 2)


def axis_bits(size):
    assert size & (size - 1) == 0
    return [1 << i for i in range(size.bit_length() - 1)]


def dot(a, b):
    return jnp.dot(a, b, preferred_element_type=F32)


def dot_nt(a, b):
    return lax.dot_general(a, b, (((1,), (1,)), ((), ())), preferred_element_type=F32)


def dot_tn(a, b):
    return lax.dot_general(a, b, (((0,), (0,)), ((), ())), preferred_element_type=F32)


class Place:
    def __init__(self):
        self.row = lax.axis_index("rows")
        self.pos = lax.axis_index("pos")

    def partner(self, link):
        axis, bit = link
        if axis == "r":
            return (flip(self.row, bit), self.pos)
        return (self.row, flip(self.pos, bit))

    def side(self, link):
        axis, bit = link
        return bit_of(self.row if axis == "r" else self.pos, bit)


def remote(src, dst, sems, index, device):
    send_sem, recv_sem = sems
    return pltpu.make_async_remote_copy(
        src_ref=src,
        dst_ref=dst,
        send_sem=send_sem.at[index],
        recv_sem=recv_sem.at[index],
        device_id=device,
        device_id_type=MESH,
    )


def greet(devices):
    barrier = pltpu.get_barrier_semaphore()
    for device in devices:
        pl.semaphore_signal(barrier, inc=1, device_id=device, device_id_type=MESH)
    pl.semaphore_wait(barrier, len(devices))


def rows_at(ref, start, size):
    return ref.at[pl.ds(pl.multiple_of(start, 16), size)]


def forward_kernel(
    rows_n, x_in, w_in, b_in, seg_wide, seg_row, x_turned, qkv, lse, mixed, *scratch
):
    x_all, blend, lse_cols, x_send, x_recv, o_send, o_recv, own_sem = scratch
    place = Place()
    me = place.pos
    mate, across = flip(me, 1), flip(me, 2)
    far = flip(mate, 2)
    peers = [mate, across, far]
    part = x_in.shape[0] // rows_n
    length = 4 * part
    width = w_in.shape[1] // 3
    heads = width // HEAD_DIM
    greet([(place.row, peer) for peer in peers])
    x_sems, o_sems = (x_send, x_recv), (o_send, o_recv)

    def x_spot(r, owner):
        return rows_at(x_all, r * length + owner * part, part)

    to_across, to_mate, passed, own = [], [], [], []
    for r in range(rows_n):
        src = x_in.at[pl.ds(r * part, part)]
        to_across.append(remote(src, x_spot(r, me), x_sems, (0, r), (place.row, across)))
        to_mate.append(remote(src, x_spot(r, me), x_sems, (1, r), (place.row, mate)))
        passed.append(
            remote(x_spot(r, across), x_spot(r, across), x_sems, (2, r), (place.row, mate))
        )
        own.append(pltpu.make_async_copy(src, x_spot(r, me), own_sem.at[r]))
        to_across[r].start()
        to_mate[r].start()
        own[r].start()
    is_query = lax.broadcasted_iota(jnp.int32, (1, 3 * width), 1) < width
    scale = jnp.where(is_query, SCALE, 1.0)
    out_copies = []
    for r in range(rows_n):
        to_across[r].wait_recv()
        passed[r].start()
        to_mate[r].wait_recv()
        own[r].wait()
        passed[r].wait_recv()
        base = r * length
        x_row = x_all[base : base + length, :]
        made = ((dot(x_row, w_in[...]) + b_in[...]) * scale).astype(LOW)
        for index in range(3 * heads):
            qkv[index, base : base + length, :] = made[:, index * HEAD_DIM : (index + 1) * HEAD_DIM]

        @pl.loop(0, length // LANES)
        def _(block):
            here = pl.ds(pl.multiple_of(base + block * LANES, LANES), LANES)
            local = pl.ds(pl.multiple_of(block * LANES, LANES), LANES)
            seg_q = seg_wide[r, local, :]
            same = jnp.concatenate([seg_q] * (length // LANES), axis=1) == seg_row[r : r + 1, :]
            for head in range(heads):
                query = qkv[head, here, :]
                key = qkv[heads + head, base : base + length, :]
                value = qkv[2 * heads + head, base : base + length, :]
                scores = jnp.where(same, dot_nt(query, key), MASKED)
                top = jnp.max(scores, axis=-1, keepdims=True)
                power = jnp.exp(scores - top)
                total = jnp.sum(power, axis=-1, keepdims=True)
                out = dot(power.astype(LOW), value) / total
                blend[here, head * HEAD_DIM : (head + 1) * HEAD_DIM] = out.astype(LOW)
                column = r * heads + head
                lse_cols[local, column : column + 1] = top + jnp.log(total)

        for index, peer in enumerate(peers):
            copy = remote(
                rows_at(blend, base + peer * part, part),
                mixed.at[me, pl.ds(r * part, part)],
                o_sems,
                (index, r),
                (place.row, peer),
            )
            copy.start()
            out_copies.append(copy)
        mixed[me, r * part : (r + 1) * part, :] = blend[
            pl.ds(pl.multiple_of(base + me * part, 16), part), :
        ]
    lse[...] = jnp.transpose(lse_cols[...])[: lse.shape[0], :]
    half = x_turned.shape[0]
    for r in range(rows_n):
        base = r * length
        block = x_all[base : base + length, pl.ds(pl.multiple_of(bit_of(me, 1) * half, LANES), half)]
        x_turned[:, base : base + length] = jnp.transpose(block)
    for copy in to_across + to_mate + passed:
        copy.wait_send()
    for copy in out_copies:
        copy.wait()


def attend_forward(x_rows, w_own, b_own, seg_wide, seg_row, rows_n):
    tokens_n, features = x_rows.shape
    length = seg_row.shape[1]
    every = rows_n * length
    width = w_own.shape[1] // 3
    vmem = pl.BlockSpec(memory_space=pltpu.VMEM)
    dma = pltpu.SemaphoreType.DMA
    return pl.pallas_call(
        partial(forward_kernel, rows_n),
        out_shape=[
            jax.ShapeDtypeStruct((features // 2, every), LOW),
            jax.ShapeDtypeStruct((3 * width // HEAD_DIM, every, HEAD_DIM), LOW),
            jax.ShapeDtypeStruct((16, length), F32),
            jax.ShapeDtypeStruct((4, tokens_n, width), LOW),
        ],
        in_specs=[vmem] * 5,
        out_specs=[vmem] * 4,
        scratch_shapes=[
            pltpu.VMEM((every, features), LOW),
            pltpu.VMEM((every, width), LOW),
            pltpu.VMEM((length, LANES), F32),
            dma((3, rows_n)),
            dma((3, rows_n)),
            dma((3, rows_n)),
            dma((3, rows_n)),
            dma((rows_n,)),
        ],
        compiler_params=pltpu.CompilerParams(
            collective_id=1, has_side_effects=True, vmem_limit_bytes=VMEM_LIMIT
        ),
        cost_estimate=pl.CostEstimate(
            flops=10**10, bytes_accessed=10**7, transcendentals=4 * 10**6
        ),
        name="attend_forward",
    )(x_rows, w_own, b_own, seg_wide, seg_row)


def plan_splits(rows, cols, links):
    kinds = []
    for _ in links:
        if (rows // 2) % 16 == 0:
            rows //= 2
            kinds.append("rows")
        elif (cols // 2) % LANES == 0:
            cols //= 2
            kinds.append("cols")
        else:
            kinds.append("whole")
    return kinds


def shrink(rows, cols, kind):
    return (rows // 2 if kind == "rows" else rows, cols // 2 if kind == "cols" else cols)


def landing_shape(rows, cols, kinds, skip):
    total, widest = 0, 0
    for number, kind in enumerate(kinds):
        rows, cols = shrink(rows, cols, kind)
        if number >= skip:
            total, widest = total + rows, max(widest, cols)
    return total, widest


def add_into(dst, left, right, rows):
    step = 16 if rows % 48 else 48

    @pl.loop(0, rows // step)
    def _(i):
        at = pl.ds(pl.multiple_of(i * step, step), step)
        dst[at, :] = (left[at, :].astype(F32) + right[at, :].astype(F32)).astype(dst.dtype)


def window(ref, row0, rows, col0, cols):
    if not isinstance(row0, int):
        row0 = pl.multiple_of(row0, 16)
    if not isinstance(col0, int):
        col0 = pl.multiple_of(col0, LANES)
    return ref.at[pl.ds(row0, rows), pl.ds(col0, cols)]


class Chunk:
    def __init__(self, place, links, kinds, skip, give, out, total, landing, sems):
        send_sem, recv_sem, copy_sem = sems
        self.reduces, self.gathers, self.moment, self.gave = [], [], 0, False
        row0, col0 = 0, 0
        rows, cols = out.shape
        corner, landed, slot, trail = None, 0, 0, []
        for number, (link, kind) in enumerate(zip(links, kinds)):
            side = place.side(link)
            rows, cols = shrink(rows, cols, kind)
            keep = other = (row0, col0)
            if kind == "rows":
                keep, other = (row0 + side * rows, col0), (row0 + (1 - side) * rows, col0)
            elif kind == "cols":
                keep, other = (row0, col0 + side * cols), (row0, col0 + (1 - side) * cols)
            row0, col0 = keep
            trail.append((link, kind, keep, rows, cols))
            if number == max(skip - 1, 0):
                corner = keep
            if number < skip:
                continue

            def held(at):
                return window(total, at[0] - corner[0], rows, at[1] - corner[1], cols)

            land = window(landing, landed, rows, 0, cols)
            landed += rows
            src = give if number == 0 else held(other)
            copy = remote(src, land, (send_sem, recv_sem), slot, place.partner(link))
            slot += 1
            self.reduces.append((copy, held(keep), land, kind == "whole"))
        mine = window(out, row0, rows, col0, cols)
        self.own = pltpu.make_async_copy(held((row0, col0)), mine, copy_sem)
        for link, kind, keep, rows, cols in trail[::-1]:
            if kind == "whole":
                self.gathers.append(None)
                continue
            here = window(out, keep[0], rows, keep[1], cols)
            self.gathers.append(remote(here, here, (send_sem, recv_sem), slot, place.partner(link)))
            slot += 1

    def done(self):
        return self.moment > len(self.reduces) + len(self.gathers)

    def advance(self):
        count, now = len(self.reduces), self.moment
        if 0 < now <= count:
            copy, keep, land, whole = self.reduces[now - 1]
            copy.wait_recv()
            if whole:
                copy.wait_send()
            add_into(keep, keep, land, land.shape[0])
        elif now > count and self.gathers[now - count - 1] is not None:
            self.gathers[now - count - 1].wait_recv()
        if now < count:
            self.reduces[now][0].start()
        elif now < count + len(self.gathers):
            if now == count:
                self.own.start()
                self.own.wait()
            if self.gathers[now - count] is not None:
                self.gathers[now - count].start()
        else:
            for index, (copy, _, _, whole) in enumerate(self.reduces):
                if not whole and not (index == 0 and self.gave):
                    copy.wait_send()
            for copy in self.gathers:
                if copy is not None:
                    copy.wait_send()
        self.moment += 1


TAIL_STEEP = 0.24
TAIL = (
    0.09575598852910579,
    0.09547705164870551,
    0.093198719112773,
    0.06193635630868121,
    0.1216760657292812,
    -0.06984360139735674,
    0.1555215658230106,
    -0.05372215169653546,
)
TILE = 256
BAND = 48
SLOTS = 4


def gelu_and_slope(u):
    bell = jnp.exp(u * u * -0.5)
    t = 1.0 / (1.0 + TAIL_STEEP * jnp.abs(u))
    f = TAIL[-1]
    for coefficient in TAIL[-2::-1]:
        f = f * t + coefficient
    below = f * t * bell
    phi = jnp.where(u > 0, 1.0 - below, below)
    return u * phi, phi + u * (bell * 0.3989422804014327)


def fold(v):
    return jnp.sum(v.reshape(v.shape[0] // 8, 8, v.shape[1]), axis=0)


def bands(n, init, body):
    def step(i, carry):
        return body(pl.ds(pl.multiple_of(i * BAND, BAND), BAND), carry)

    return lax.fori_loop(0, n // BAND, step, init)


def rest_kernel(rows_n, orders, late_order, lags, *refs):
    (x_in, mixed, cot, vecs, up_bias, lse, seg_wide, seg_row) = refs[:8]
    (qkv_in, turned_in, w_out_in, w_up_in, w_down_in, w_own_in, w_mate_in) = refs[8:15]
    (q_out, k_out, v_out, o_out, up_out, down_out, result, dx_out, small_out) = refs[15:24]
    (d_give, d_all, chip, dx_give, dx_land, gives, total, late_total, landing, late_land) = refs[24:34]
    (small_land, send_sem, recv_sem, copy_sem, small_send, small_recv) = refs[34:40]
    (d_send, d_recv, g_send, g_recv, dx_send, dx_recv, load_sem) = refs[40:47]
    place = Place()
    me = place.pos
    mate, across = flip(me, 1), flip(me, 2)
    peers = [across, flip(mate, 2), mate]
    core = bit_of(me, 1)
    tokens_n, features = x_in.shape
    part = tokens_n // rows_n
    length = 4 * part
    width = d_all.shape[1]
    heads = width // HEAD_DIM
    inner_n = up_bias.shape[1]
    half = features // 2
    quarters = inner_n // features
    links = late_order
    ticks = [0]
    outs = [window(down_out, j * features, features, 0, features) for j in range(inner_n // features)]
    outs += [window(up_out, 0, features, j * features, features) for j in range(inner_n // features)]
    outs += [o_out]
    chunks = [
        Chunk(
            place,
            orders[index],
            plan_splits(features, features, orders[index]),
            0,
            gives.at[index % SLOTS],
            out,
            total.at[index],
            landing.at[index],
            (send_sem.at[index], recv_sem.at[index], copy_sem.at[index]),
        )
        for index, out in enumerate(outs)
    ]
    late = []
    for index, out in enumerate((q_out, k_out, v_out)):
        number = len(chunks) + index
        late.append(
            Chunk(
                place,
                late_order,
                ["rows", "cols"] + plan_splits(half, half, late_order[2:]),
                2,
                None,
                out,
                late_total.at[index],
                late_land.at[index],
                (send_sem.at[number], recv_sem.at[number], copy_sem.at[number]),
            )
        )
    mine, other = chip.at[core], chip.at[1 - core]
    d_copies, g_copies, dx_copies = {}, [], []
    for r in range(rows_n):
        at = pl.ds(r * part, part)
        row = pl.ds(r * length, length)
        for index, peer in enumerate(peers):
            d_copies[index, r] = remote(
                d_give.at[peer, at],
                rows_at(d_all, r * length + me * part, part),
                (d_send, d_recv),
                (index, r),
                (place.row, peer),
            )
        g_copies.append(
            remote(mine.at[row], mine.at[row], (g_send, g_recv), r, (place.row, mate))
        )
        dx_copies.append(
            remote(dx_give.at[at], dx_land.at[at], (dx_send, dx_recv), r, (place.row, across))
        )
    born = []

    def tick():
        for chunk, when, lag in zip(chunks, born, lags):
            if ticks[0] >= when + lag and not chunk.done():
                chunk.advance()
        ticks[0] += 1

    def new_chunk(give, keep):
        index = len(born)
        chunk = chunks[index]
        if index >= SLOTS:
            chunks[index - SLOTS].reduces[0][0].wait_send()
            chunks[index - SLOTS].gave = True
        gives[index % SLOTS] = give().astype(LOW)
        chunk.advance()
        total[index] = keep().astype(LOW)
        born.append(ticks[0])

    greet([place.partner(link) for link in links] + [(place.row, flip(mate, 2))])
    give_at = pl.ds(pl.multiple_of((1 - core) * half, LANES), half)
    keep_at = pl.ds(pl.multiple_of(core * half, LANES), half)
    small_out[...] = jnp.zeros_like(small_out)

    def dense(w_out, w_up, w_down, joined, hat, spread_one, low, turned, active, slope, d_low, d_up):
        acc = dx_out
        loads = []
        for index, (src, dst) in enumerate(((w_out_in, w_out), (w_up_in, w_up), (w_down_in, w_down))):
            loads.append(pltpu.make_async_copy(src, dst, load_sem.at[index]))
            loads[-1].start()
        for group in range(4):
            joined[:, group * width : (group + 1) * width] = mixed[group]
        gain_one, shift_one = vecs[1:2, :], vecs[2:3, :]
        gain_two, shift_two = vecs[4:5, :], vecs[5:6, :]
        loads[0].wait()
        acc[...] = dot(joined[...], w_out[...])

        def norm_one(at, carry):
            v = x_in[at, :].astype(F32) + (acc[at, :] + vecs[0:1, :])
            centred = v - jnp.mean(v, axis=-1, keepdims=True)
            over = lax.rsqrt(jnp.mean(centred * centred, axis=-1, keepdims=True) + EPS)
            v = centred * over
            hat[at, :] = v
            spread_one[at, :] = jnp.broadcast_to(over, (BAND, LANES))
            low[at, :] = (v * gain_one + shift_one).astype(LOW)
            return carry

        bands(tokens_n, 0, norm_one)
        loads[1].wait()

        @pl.loop(0, inner_n // TILE)
        def _(tile):
            cols = pl.ds(pl.multiple_of(tile * TILE, TILE), TILE)
            u = dot(low[...], w_up[:, cols]) + up_bias[:, cols]
            for band in range(tokens_n // BAND):
                at = slice(band * BAND, (band + 1) * BAND)
                g, s = gelu_and_slope(u[at])
                active[at, cols] = g.astype(LOW)
                slope[at, cols] = s

        loads[2].wait()

        @pl.loop(0, features // TILE)
        def _(tile):
            cols = pl.ds(pl.multiple_of(tile * TILE, TILE), TILE)
            acc[:, cols] = dot(active[...], w_down[:, cols])

        def norm_two(at, carry):
            d_gain, d_shift, d_bias = carry
            v = hat[at, :] * gain_one + shift_one + (acc[at, :] + vecs[3:4, :])
            centred = v - jnp.mean(v, axis=-1, keepdims=True)
            over = lax.rsqrt(jnp.mean(centred * centred, axis=-1, keepdims=True) + EPS)
            v = centred * over
            result[at, :] = (v * gain_two + shift_two).astype(LOW)
            d = cot[at, :].astype(F32)
            d_gain += fold(d * v)
            d_shift += fold(d)
            d = d * gain_two
            d = d - jnp.mean(d, axis=-1, keepdims=True) - v * jnp.mean(d * v, axis=-1, keepdims=True)
            d = d * over
            acc[at, :] = d
            d = d.astype(LOW)
            d_low[at, :] = d
            return d_gain, d_shift, d_bias + fold(d.astype(F32))

        blank = jnp.zeros((8, features), F32)
        d_gain, d_shift, d_bias = bands(tokens_n, (blank, blank, blank), norm_two)
        for index, value in ((3, d_bias), (4, d_gain), (5, d_shift)):
            small_out[index : index + 1, :] = jnp.sum(value, axis=0, keepdims=True)

        for quarter in range(quarters):
            first = quarter * features

            def some_down(side):
                at = pl.ds(pl.multiple_of(first + side * half, LANES), half)
                return dot_tn(active[:, at], d_low[...])

            new_chunk(
                lambda: some_down(1 - core),
                lambda: some_down(core),
            )
        turned[...] = jnp.transpose(low[...])
        tick()
        for quarter in range(quarters):
            first = quarter * features

            @pl.loop(0, features // TILE)
            def _(tile):
                rows = pl.ds(pl.multiple_of(first + tile * TILE, TILE), TILE)
                cols = pl.ds(pl.multiple_of(tile * TILE, TILE), TILE)
                d = (dot_nt(d_low[...], w_down[rows, :]) * slope[:, rows]).astype(LOW)
                d_up[:, cols] = d
                small_out[12 + quarter : 13 + quarter, cols] = jnp.sum(
                    d.astype(F32), axis=0, keepdims=True
                )

            new_chunk(
                lambda: dot(turned[give_at, :], d_up[...]),
                lambda: dot(turned[keep_at, :], d_up[...]),
            )
            acc[...] += dot_nt(d_up[...], w_up[:, first : first + features])
            tick()

        def norm_back(at, carry):
            d_gain, d_shift, d_bias = carry
            v, d = hat[at, :], acc[at, :]
            d_gain += fold(d * v)
            d_shift += fold(d)
            d = d * gain_one
            d = d - jnp.mean(d, axis=-1, keepdims=True) - v * jnp.mean(d * v, axis=-1, keepdims=True)
            d = d * spread_one[at, 0:1]
            acc[at, :] = d
            d = d.astype(LOW)
            d_low[at, :] = d
            return d_gain, d_shift, d_bias + fold(d.astype(F32))

        d_gain, d_shift, d_bias = bands(tokens_n, (blank, blank, blank), norm_back)
        for index, value in ((0, d_bias), (1, d_gain), (2, d_shift)):
            small_out[index : index + 1, :] = jnp.sum(value, axis=0, keepdims=True)
        for group in range(4):
            at = slice(group * width, (group + 1) * width)
            d_give[group] = dot_nt(d_low[...], w_out[at, :]).astype(LOW)
        for r in range(rows_n):
            for index in range(3):
                d_copies[index, r].start()
        new_chunk(
            lambda: dot_tn(joined[:, give_at], d_low[...]),
            lambda: dot_tn(joined[:, keep_at], d_low[...]),
        )
        tick()

    square = (tokens_n, features)
    pl.run_scoped(
        dense,
        pltpu.VMEM((features, features), LOW),
        pltpu.VMEM((features, inner_n), LOW),
        pltpu.VMEM((inner_n, features), LOW),
        pltpu.VMEM(square, LOW),
        pltpu.VMEM(square, F32),
        pltpu.VMEM((tokens_n, LANES), F32),
        pltpu.VMEM(square, LOW),
        pltpu.VMEM((features, tokens_n), LOW),
        pltpu.VMEM((tokens_n, inner_n), LOW),
        pltpu.VMEM((tokens_n, inner_n), F32),
        pltpu.VMEM(square, LOW),
        pltpu.VMEM(square, LOW),
    )

    def attention(qkv, x_turned, w_own, w_mate, d_heads, prob, d_score):
        loads = []
        for index, (src, dst) in enumerate(
            ((qkv_in, qkv), (turned_in, x_turned), (w_own_in, w_own), (w_mate_in, w_mate))
        ):
            loads.append(pltpu.make_async_copy(src, dst, load_sem.at[index]))
            loads[-1].start()
        for load in loads:
            load.wait()
        for r in range(rows_n):
            base = r * length
            own_rows = pl.ds(pl.multiple_of(base + me * part, 16), part)
            d_all[own_rows, :] = d_give[me, r * part : (r + 1) * part, :]
            for index in range(3):
                d_copies[index, r].wait_recv()
            d_row = d_all[base : base + length, :]
            for head in range(heads):
                d_heads[head] = d_row[:, head * HEAD_DIM : (head + 1) * HEAD_DIM]

            @pl.loop(0, length // LANES)
            def _(block):
                here = pl.ds(pl.multiple_of(base + block * LANES, LANES), LANES)
                local = pl.ds(pl.multiple_of(block * LANES, LANES), LANES)
                same = seg_wide[r] == seg_row[r : r + 1, local]
                for head in range(heads):
                    query = qkv[head, here, :]
                    key = qkv[heads + head, base : base + length, :]
                    value = qkv[2 * heads + head, base : base + length, :]
                    log_total = lse[r * heads + head : r * heads + head + 1, local]
                    p = jnp.exp(jnp.where(same, dot_nt(key, query) - log_total, MASKED))
                    dp = dot_nt(value, d_heads[head, local, :])
                    inner = jnp.sum(dp * p, axis=0, keepdims=True)
                    prob[head, :, local] = p.astype(LOW)
                    d_score[head, :, local] = (p * (dp - inner)).astype(LOW)

            tick()
            for head in range(heads):
                query = qkv[head, base : base + length, :]
                key = qkv[heads + head, base : base + length, :]
                ds = d_score[head]
                at = slice(base, base + length)
                left = head * HEAD_DIM
                dq = dot_tn(ds, key) * SCALE
                mine[at, left : left + HEAD_DIM] = dq.astype(LOW)
                left += width
                mine[at, left : left + HEAD_DIM] = dot(ds, query).astype(LOW)
                left += width
                mine[at, left : left + HEAD_DIM] = dot(prob[head], d_heads[head]).astype(LOW)
            g_copies[r].start()
            tick()

        def dx_of(r, owner):
            at = pl.ds(pl.multiple_of(r * length + owner * part, 16), part)
            return dot_nt(mine[at, :], w_own[...]) + dot_nt(other[at, :], w_mate[...])

        for r in range(rows_n):
            g_copies[r].wait_recv()
            at = pl.ds(r * part, part)
            dx_give[at, :] = dx_of(r, across).astype(LOW)
            dx_copies[r].start()
        tick()
        for index in range(3):
            left = index * width
            sums = [dot(x_turned[...], chip[side, :, left : left + width]) for side in range(2)]
            late_total[index] = jnp.concatenate(sums, axis=1).astype(LOW)
            late[index].advance()
        tick()
        token_sums = jnp.sum(mine[...].astype(F32), axis=0, keepdims=True)
        group = lax.broadcasted_iota(jnp.int32, (4, 3 * width), 0)
        spread = jnp.where(group == me, token_sums, 0.0)
        spread = jnp.concatenate([spread, jnp.zeros((4, features - 3 * width), F32)], axis=1)
        small_out[8:12, :] = spread
        for r in range(rows_n):
            at = pl.ds(r * part, part)
            dx_out[at, :] += dx_of(r, me)
        tick()

    pl.run_scoped(
        attention,
        pltpu.VMEM(qkv_in.shape, LOW),
        pltpu.VMEM(turned_in.shape, LOW),
        pltpu.VMEM(w_own_in.shape, LOW),
        pltpu.VMEM(w_mate_in.shape, LOW),
        pltpu.VMEM((heads, length, HEAD_DIM), LOW),
        pltpu.VMEM((heads, length, length), LOW),
        pltpu.VMEM((heads, length, length), LOW),
    )
    number = 0
    while number < len(links) or not all(c.done() for c in chunks + late):
        small = None
        if number < len(links):
            small = remote(
                small_out,
                small_land.at[number],
                (small_send, small_recv),
                number,
                place.partner(links[number]),
            )
            small.start()
        tick()
        for chunk in late:
            if not chunk.done():
                chunk.advance()
        if small is not None:
            small.wait()
            small_out[...] += small_land[number]
        number += 1
    for r in range(rows_n):
        dx_copies[r].wait_recv()
        at = pl.ds(r * part, part)
        dx_out[at, :] += dx_land[at, :].astype(F32)
    for copy in dx_copies + g_copies + list(d_copies.values()):
        copy.wait_send()


def attend_rest(mesh_shape, x_rows, mixed, cot, vecs, up_bias, lse, seg_wide, seg_row, qkv, x_turned, w_out, w_up, w_down, w_own, w_mate):
    row_bits = [("r", bit) for bit in axis_bits(mesh_shape["rows"])]
    pos_bits = [("p", bit) for bit in axis_bits(mesh_shape["pos"])]
    one = [pos_bits[0], row_bits[0], *pos_bits[1:], *row_bits[1:]]
    two = [*pos_bits, *row_bits]
    orders = [one if index % 2 == 0 else two for index in range(9)]
    lags = [1 + index // 2 if index < 4 else 1 for index in range(9)]
    rows_n, length = seg_row.shape
    tokens_n, features = x_rows.shape
    inner_n = w_up.shape[1]
    width = mixed.shape[2]
    every = rows_n * length
    steps = len(two)
    early = landing_shape(features, features, plan_splits(features, features, one), 0)
    half = features // 2
    late = landing_shape(half, half, plan_splits(half, half, row_bits), 0)
    vmem = pl.BlockSpec(memory_space=pltpu.VMEM)
    hbm = pl.BlockSpec(memory_space=pl.ANY)
    dma = pltpu.SemaphoreType.DMA
    square = jax.ShapeDtypeStruct((features, features), LOW)
    return pl.pallas_call(
        partial(rest_kernel, rows_n, orders, two, lags),
        out_shape=[
            square,
            square,
            square,
            square,
            jax.ShapeDtypeStruct(w_up.shape, LOW),
            jax.ShapeDtypeStruct(w_down.shape, LOW),
            jax.ShapeDtypeStruct((tokens_n, features), LOW),
            jax.ShapeDtypeStruct((tokens_n, features), F32),
            jax.ShapeDtypeStruct((16, features), F32),
        ],
        in_specs=[vmem] * 8 + [hbm] * 7,
        out_specs=[hbm] * 6 + [vmem] * 3,
        scratch_shapes=[
            pltpu.VMEM((4, tokens_n, width), LOW),
            pltpu.VMEM((every, width), LOW),
            pltpu.VMEM((2, every, 3 * width), LOW),
            pltpu.VMEM((tokens_n, features), LOW),
            pltpu.VMEM((tokens_n, features), LOW),
            pltpu.VMEM((SLOTS, half, features), LOW),
            pltpu.VMEM((9, half, features), LOW),
            pltpu.VMEM((3, half, half), LOW),
            pltpu.VMEM((9, *early), LOW),
            pltpu.VMEM((3, *late), LOW),
            pltpu.VMEM((steps, 16, features), F32),
            dma((12, 2 * steps)),
            dma((12, 2 * steps)),
            dma((12,)),
            dma((steps,)),
            dma((steps,)),
            dma((3, rows_n)),
            dma((3, rows_n)),
            dma((rows_n,)),
            dma((rows_n,)),
            dma((rows_n,)),
            dma((rows_n,)),
            dma((4,)),
        ],
        compiler_params=pltpu.CompilerParams(
            collective_id=0, has_side_effects=True, vmem_limit_bytes=VMEM_LIMIT
        ),
        cost_estimate=pl.CostEstimate(
            flops=4 * 10**10, bytes_accessed=8 * 10**7, transcendentals=8 * 10**6
        ),
        name="attend_rest",
    )(x_rows, mixed, cot, vecs, up_bias, lse, seg_wide, seg_row, qkv, x_turned, w_out, w_up, w_down, w_own, w_mate)


def own_columns(w, index, width):
    return lax.dynamic_slice_in_dim(w, index * width, width, w.ndim - 1)


def on_device(
    mesh_shape,
    tokens,
    segments,
    w_query,
    b_query,
    w_key,
    w_value,
    b_value,
    w_out,
    b_out,
    gain_one,
    shift_one,
    w_up,
    b_up,
    w_down,
    b_down,
    gain_two,
    shift_two,
    cotangent,
):
    rows_n, part_len, features = tokens.shape
    length = segments.shape[1]
    groups = mesh_shape["pos"]
    width = features // groups
    here = lax.axis_index("pos")
    mate = here + 1 - 2 * lax.rem(here, 2)
    x_rows = tokens.reshape(rows_n * part_len, features)
    seg_row = segments.astype(F32)
    seg_wide = jnp.broadcast_to(seg_row[:, :, None], (rows_n, length, LANES))

    def heads_of(index):
        return jnp.concatenate(
            [own_columns(w, index, width) for w in (w_query, w_key, w_value)], axis=1
        )

    w_own, w_mate = heads_of(here), heads_of(mate)
    b_own = jnp.concatenate(
        [
            own_columns(b_query.astype(F32), here, width),
            jnp.zeros((width,), F32),
            own_columns(b_value.astype(F32), here, width),
        ]
    )[None]
    x_turned, qkv, lse, mixed = attend_forward(x_rows, w_own, b_own, seg_wide, seg_row, rows_n)
    vecs = jnp.stack([b_out, gain_one, shift_one, b_down, gain_two, shift_two]).astype(F32)
    *blocks, result, grad_tokens, small = attend_rest(
        mesh_shape,
        x_rows,
        mixed,
        cotangent.reshape(rows_n * part_len, features),
        jnp.pad(vecs, ((0, 2), (0, 0))),
        b_up.astype(F32)[None],
        lse,
        seg_wide,
        seg_row,
        qkv,
        x_turned,
        w_out,
        w_up,
        w_down,
        w_own,
        w_mate,
    )
    grad_w_query, grad_w_key, grad_w_value, grad_w_out, grad_w_up, grad_w_down = (
        b.astype(F32) for b in blocks
    )
    shape = (rows_n, part_len, features)
    return (
        result.reshape(shape),
        grad_tokens.reshape(shape),
        grad_w_query,
        small[8:12, :width].reshape(-1),
        grad_w_key,
        grad_w_value,
        small[8:12, 2 * width : 3 * width].reshape(-1),
        grad_w_out,
        small[0],
        small[1],
        small[2],
        grad_w_up,
        small[12:16].reshape(-1),
        grad_w_down,
        small[3],
        small[4],
        small[5],
    )


def solution(mesh):
    tokens = P("rows", "pos", None)
    return jax.shard_map(
        partial(on_device, dict(mesh.shape)),
        mesh=mesh,
        in_specs=(tokens, P("rows", None), *[P()] * 15, tokens),
        out_specs=(tokens, tokens, *[P()] * 15),
        check_vma=False,
    )
```

```python
from functools import partial

import jax
import jax.numpy as jnp
from jax import lax
from jax.experimental import pallas as pl
from jax.experimental.pallas import tpu as pltpu
from jax.sharding import PartitionSpec as P

HEADS = 12
HEAD_DIM = 64
EPS = 1e-05
MASKED = -1000000000.0
SCALE = HEAD_DIM ** (-0.5)
LANES = 128
VMEM_LIMIT = 60 * 2**20
MESH = pl.DeviceIdType.MESH
LOW = jnp.bfloat16
F32 = jnp.float32


def flip(value, bit):
    return value + bit - 2 * bit * lax.rem(lax.div(value, bit), 2)


def bit_of(value, bit):
    return lax.rem(lax.div(value, bit), 2)


def axis_bits(size):
    assert size & (size - 1) == 0
    return [1 << i for i in range(size.bit_length() - 1)]


def dot(a, b):
    return jnp.dot(a, b, preferred_element_type=F32)


def dot_nt(a, b):
    return lax.dot_general(a, b, (((1,), (1,)), ((), ())), preferred_element_type=F32)


def dot_tn(a, b):
    return lax.dot_general(a, b, (((0,), (0,)), ((), ())), preferred_element_type=F32)


class Place:
    def __init__(self):
        self.row = lax.axis_index("rows")
        self.pos = lax.axis_index("pos")

    def partner(self, link):
        axis, bit = link
        if axis == "r":
            return (flip(self.row, bit), self.pos)
        return (self.row, flip(self.pos, bit))

    def side(self, link):
        axis, bit = link
        return bit_of(self.row if axis == "r" else self.pos, bit)


def remote(src, dst, sems, index, device):
    send_sem, recv_sem = sems
    return pltpu.make_async_remote_copy(
        src_ref=src,
        dst_ref=dst,
        send_sem=send_sem.at[index],
        recv_sem=recv_sem.at[index],
        device_id=device,
        device_id_type=MESH,
    )


def greet(devices):
    barrier = pltpu.get_barrier_semaphore()
    for device in devices:
        pl.semaphore_signal(barrier, inc=1, device_id=device, device_id_type=MESH)
    pl.semaphore_wait(barrier, len(devices))


def rows_at(ref, start, size):
    return ref.at[pl.ds(pl.multiple_of(start, 16), size)]


def forward_kernel(
    rows_n, x_in, w_in, b_in, seg_wide, seg_row, x_turned, qkv, lse, mixed, *scratch
):
    x_all, blend, lse_cols, x_send, x_recv, o_send, o_recv, own_sem = scratch
    place = Place()
    me = place.pos
    mate, across = flip(me, 1), flip(me, 2)
    far = flip(mate, 2)
    peers = [mate, across, far]
    part = x_in.shape[0] // rows_n
    length = 4 * part
    width = w_in.shape[1] // 3
    heads = width // HEAD_DIM
    greet([(place.row, peer) for peer in peers])
    x_sems, o_sems = (x_send, x_recv), (o_send, o_recv)

    def x_spot(r, owner):
        return rows_at(x_all, r * length + owner * part, part)

    to_across, to_mate, passed, own = [], [], [], []
    for r in range(rows_n):
        src = x_in.at[pl.ds(r * part, part)]
        to_across.append(remote(src, x_spot(r, me), x_sems, (0, r), (place.row, across)))
        to_mate.append(remote(src, x_spot(r, me), x_sems, (1, r), (place.row, mate)))
        passed.append(
            remote(x_spot(r, across), x_spot(r, across), x_sems, (2, r), (place.row, mate))
        )
        own.append(pltpu.make_async_copy(src, x_spot(r, me), own_sem.at[r]))
        to_across[r].start()
        to_mate[r].start()
        own[r].start()
    is_query = lax.broadcasted_iota(jnp.int32, (1, 3 * width), 1) < width
    scale = jnp.where(is_query, SCALE, 1.0)
    out_copies = []
    for r in range(rows_n):
        to_across[r].wait_recv()
        passed[r].start()
        to_mate[r].wait_recv()
        own[r].wait()
        passed[r].wait_recv()
        base = r * length
        x_row = x_all[base : base + length, :]
        made = ((dot(x_row, w_in[...]) + b_in[...]) * scale).astype(LOW)
        for index in range(3 * heads):
            qkv[index, base : base + length, :] = made[:, index * HEAD_DIM : (index + 1) * HEAD_DIM]

        @pl.loop(0, length // LANES)
        def _(block):
            here = pl.ds(pl.multiple_of(base + block * LANES, LANES), LANES)
            local = pl.ds(pl.multiple_of(block * LANES, LANES), LANES)
            seg_q = seg_wide[r, local, :]
            same = jnp.concatenate([seg_q] * (length // LANES), axis=1) == seg_row[r : r + 1, :]
            for head in range(heads):
                query = qkv[head, here, :]
                key = qkv[heads + head, base : base + length, :]
                value = qkv[2 * heads + head, base : base + length, :]
                scores = jnp.where(same, dot_nt(query, key), MASKED)
                top = jnp.max(scores, axis=-1, keepdims=True)
                power = jnp.exp(scores - top)
                total = jnp.sum(power, axis=-1, keepdims=True)
                out = dot(power.astype(LOW), value) / total
                blend[here, head * HEAD_DIM : (head + 1) * HEAD_DIM] = out.astype(LOW)
                column = r * heads + head
                lse_cols[local, column : column + 1] = top + jnp.log(total)

        for index, peer in enumerate(peers):
            copy = remote(
                rows_at(blend, base + peer * part, part),
                mixed.at[me, pl.ds(r * part, part)],
                o_sems,
                (index, r),
                (place.row, peer),
            )
            copy.start()
            out_copies.append(copy)
        mixed[me, r * part : (r + 1) * part, :] = blend[
            pl.ds(pl.multiple_of(base + me * part, 16), part), :
        ]
    lse[...] = jnp.transpose(lse_cols[...])[: lse.shape[0], :]
    half = x_turned.shape[0]
    for r in range(rows_n):
        base = r * length
        block = x_all[base : base + length, pl.ds(pl.multiple_of(bit_of(me, 1) * half, LANES), half)]
        x_turned[:, base : base + length] = jnp.transpose(block)
    for copy in to_across + to_mate + passed:
        copy.wait_send()
    for copy in out_copies:
        copy.wait()


def attend_forward(x_rows, w_own, b_own, seg_wide, seg_row, rows_n):
    tokens_n, features = x_rows.shape
    length = seg_row.shape[1]
    every = rows_n * length
    width = w_own.shape[1] // 3
    vmem = pl.BlockSpec(memory_space=pltpu.VMEM)
    dma = pltpu.SemaphoreType.DMA
    return pl.pallas_call(
        partial(forward_kernel, rows_n),
        out_shape=[
            jax.ShapeDtypeStruct((features // 2, every), LOW),
            jax.ShapeDtypeStruct((3 * width // HEAD_DIM, every, HEAD_DIM), LOW),
            jax.ShapeDtypeStruct((16, length), F32),
            jax.ShapeDtypeStruct((4, tokens_n, width), LOW),
        ],
        in_specs=[vmem] * 5,
        out_specs=[vmem] * 4,
        scratch_shapes=[
            pltpu.VMEM((every, features), LOW),
            pltpu.VMEM((every, width), LOW),
            pltpu.VMEM((length, LANES), F32),
            dma((3, rows_n)),
            dma((3, rows_n)),
            dma((3, rows_n)),
            dma((3, rows_n)),
            dma((rows_n,)),
        ],
        compiler_params=pltpu.CompilerParams(
            collective_id=1, has_side_effects=True, vmem_limit_bytes=VMEM_LIMIT
        ),
        cost_estimate=pl.CostEstimate(
            flops=10**10, bytes_accessed=10**7, transcendentals=4 * 10**6
        ),
        name="attend_forward",
    )(x_rows, w_own, b_own, seg_wide, seg_row)


def plan_splits(rows, cols, links):
    kinds = []
    for _ in links:
        if (rows // 2) % 16 == 0:
            rows //= 2
            kinds.append("rows")
        elif (cols // 2) % LANES == 0:
            cols //= 2
            kinds.append("cols")
        else:
            kinds.append("whole")
    return kinds


def shrink(rows, cols, kind):
    return (rows // 2 if kind == "rows" else rows, cols // 2 if kind == "cols" else cols)


def landing_shape(rows, cols, links):
    total, widest = 0, 0
    for kind in plan_splits(rows, cols, links):
        rows, cols = shrink(rows, cols, kind)
        total, widest = total + rows, max(widest, cols)
    return total, widest


def add_into(dst, left, right, rows):
    step = 16 if rows % 48 else 48

    @pl.loop(0, rows // step)
    def _(i):
        at = pl.ds(pl.multiple_of(i * step, step), step)
        dst[at, :] = (left[at, :].astype(F32) + right[at, :].astype(F32)).astype(dst.dtype)


def window(ref, row0, rows, col0, cols):
    if not isinstance(row0, int):
        row0 = pl.multiple_of(row0, 16)
    if not isinstance(col0, int):
        col0 = pl.multiple_of(col0, LANES)
    return ref.at[pl.ds(row0, rows), pl.ds(col0, cols)]


class Chunk:
    def __init__(self, place, fixed, path, gather, give, out, total, landing, sems):
        send_sem, recv_sem, copy_sem = sems
        self.reduces, self.gathers, self.moment, self.gave = [], [], 0, False
        rows, cols = out.shape
        row0, col0, landed, slot = 0, 0, 0, 0
        corner = None
        row_trail, col_trail, kind_of = [], [], {}

        def held(at, rows, cols):
            return window(total, at[0] - corner[0], rows, at[1] - corner[1], cols)

        shape = out.shape
        for _, kind in fixed:
            shape = shrink(*shape, kind)
        kinds = [kind for _, kind in fixed] + plan_splits(*shape, path)
        for number, (link, kind) in enumerate(zip([link for link, _ in fixed] + path, kinds)):
            side = place.side(link)
            kind_of[link] = kind
            keep = other = (row0, col0)
            if kind == "rows":
                row_trail.append((row0, rows))
                rows //= 2
                keep, other = (row0 + side * rows, col0), (row0 + (1 - side) * rows, col0)
            elif kind == "cols":
                col_trail.append((col0, cols))
                cols //= 2
                keep, other = (row0, col0 + side * cols), (row0, col0 + (1 - side) * cols)
            row0, col0 = keep
            if number == max(len(fixed) - 1, 0):
                corner = keep
            if number < len(fixed):
                continue
            land = window(landing, landed, rows, 0, cols)
            landed += rows
            src = give if number == 0 else held(other, rows, cols)
            copy = remote(src, land, (send_sem, recv_sem), slot, place.partner(link))
            slot += 1
            self.reduces.append((copy, held(keep, rows, cols), land, kind == "whole"))
        mine = window(out, row0, rows, col0, cols)
        self.own = pltpu.make_async_copy(held((row0, col0), rows, cols), mine, copy_sem)
        for link in gather:
            kind = kind_of[link]
            if kind == "whole":
                self.gathers.append(None)
                continue
            here = window(out, row0, rows, col0, cols)
            self.gathers.append(remote(here, here, (send_sem, recv_sem), slot, place.partner(link)))
            slot += 1
            if kind == "rows":
                row0, rows = row_trail.pop()
            else:
                col0, cols = col_trail.pop()

    def done(self):
        return self.moment > len(self.reduces) + len(self.gathers)

    def advance(self):
        count, now = len(self.reduces), self.moment
        if 0 < now <= count:
            copy, keep, land, whole = self.reduces[now - 1]
            copy.wait_recv()
            if whole:
                copy.wait_send()
            add_into(keep, keep, land, land.shape[0])
        elif now > count and self.gathers[now - count - 1] is not None:
            self.gathers[now - count - 1].wait_recv()
        if now < count:
            self.reduces[now][0].start()
        elif now < count + len(self.gathers):
            if now == count:
                self.own.start()
                self.own.wait()
            if self.gathers[now - count] is not None:
                self.gathers[now - count].start()
        else:
            for index, (copy, _, _, whole) in enumerate(self.reduces):
                if not whole and not (index == 0 and self.gave):
                    copy.wait_send()
            for copy in self.gathers:
                if copy is not None:
                    copy.wait_send()
        self.moment += 1


PATHS = ("cxyzw", "cyxzw", "czwxy", "cyxzw", "cxyzw", "czwxy", "cxyzw", "czwxy", "cyzwx")
LATE_PATHS = ("wzxyc", "wzyxc", "wzyxc")
TICKS = (
    (),
    (),
    (),
    (),
    (0, 1, 2, 3),
    (),
    (),
    (4,),
    (),
    (0, 1, 2, 5),
    (6,),
    (3,),
    (0, 1, 4, 7),
    (0, 2, 5, 6, 1),
    (3,),
    (8, 0, 2, 4, 7),
    (),
    (6,),
    (5, 3),
    (1,),
    (0, 4, 8, 2),
    (5, 6),
    (),
    (),
    (0, 2, 3, 7, 1, 5),
    (),
    (4, 8),
    (6,),
    (1, 2, 3),
)
DRAIN = (7, 4, 9, 8, 10, 6, 3, 11, 4, 9, 0, 1, 5, 10, 8, 2, 7, 6, 11, 3, 4, 9, 10, 11, 0, 1, 7, 2, 5, 9, 8, 10, 0, 6, 1, 2, 11, 4, 9, 7, 3, 4, 5, 10, 3, 11, 8, 6, 9, 6, 10, 7, 11, 5, 8, 5, 9, 10, 9, 7, 10, 11, 7, 8, 11, 8)
TAIL_STEEP = 0.24
TAIL = (
    0.09575598852910579,
    0.09547705164870551,
    0.093198719112773,
    0.06193635630868121,
    0.1216760657292812,
    -0.06984360139735674,
    0.1555215658230106,
    -0.05372215169653546,
)
TILE = 256
BAND = 48
SLOTS = 4


def gelu_and_slope(u):
    bell = jnp.exp(u * u * -0.5)
    t = 1.0 / (1.0 + TAIL_STEEP * jnp.abs(u))
    f = TAIL[-1]
    for coefficient in TAIL[-2::-1]:
        f = f * t + coefficient
    below = f * t * bell
    phi = jnp.where(u > 0, 1.0 - below, below)
    return u * phi, phi + u * (bell * 0.3989422804014327)


def fold(v):
    return jnp.sum(v.reshape(v.shape[0] // 8, 8, v.shape[1]), axis=0)


def bands(n, init, body):
    def step(i, carry):
        return body(pl.ds(pl.multiple_of(i * BAND, BAND), BAND), carry)

    return lax.fori_loop(0, n // BAND, step, init)


def rest_kernel(rows_n, paths, late_paths, links, *refs):
    (x_in, mixed, cot, vecs, up_bias, lse, seg_wide, seg_row) = refs[:8]
    (qkv_in, turned_in, w_out_in, w_up_in, w_down_in, w_own_in, w_mate_in) = refs[8:15]
    (q_out, k_out, v_out, o_out, up_out, down_out, result, dx_out, small_out) = refs[15:24]
    (d_give, d_all, chip, dx_give, dx_land, gives, total, late_total, landing, late_land) = refs[24:34]
    (small_land, send_sem, recv_sem, copy_sem, small_send, small_recv) = refs[34:40]
    (d_send, d_recv, g_send, g_recv, dx_send, dx_recv, load_sem) = refs[40:47]
    place = Place()
    me = place.pos
    mate, across = flip(me, 1), flip(me, 2)
    peers = [across, flip(mate, 2), mate]
    core = bit_of(me, 1)
    tokens_n, features = x_in.shape
    part = tokens_n // rows_n
    length = 4 * part
    width = d_all.shape[1]
    heads = width // HEAD_DIM
    inner_n = up_bias.shape[1]
    half = features // 2
    quarters = inner_n // features
    outs = [window(down_out, j * features, features, 0, features) for j in range(inner_n // features)]
    outs += [window(up_out, 0, features, j * features, features) for j in range(inner_n // features)]
    outs += [o_out]
    chunks = []
    for index, out in enumerate(outs + [q_out, k_out, v_out]):
        sems = (send_sem.at[index], recv_sem.at[index], copy_sem.at[index])
        if index < len(outs):
            path = paths[index]
            spaces = (gives.at[index % SLOTS], out, total.at[index], landing.at[index])
            chunks.append(Chunk(place, [], path, path[::-1], *spaces, sems))
        else:
            at = index - len(outs)
            fixed = [(links[0], "rows"), (links[1], "cols")]
            spaces = (None, out, late_total.at[at], late_land.at[at])
            chunks.append(Chunk(place, fixed, links[2:], late_paths[at], *spaces, sems))
    mine, other = chip.at[core], chip.at[1 - core]
    d_copies, g_copies, dx_copies = {}, [], []
    for r in range(rows_n):
        at = pl.ds(r * part, part)
        row = pl.ds(r * length, length)
        for index, peer in enumerate(peers):
            d_copies[index, r] = remote(
                d_give.at[peer, at],
                rows_at(d_all, r * length + me * part, part),
                (d_send, d_recv),
                (index, r),
                (place.row, peer),
            )
        g_copies.append(
            remote(mine.at[row], mine.at[row], (g_send, g_recv), r, (place.row, mate))
        )
        dx_copies.append(
            remote(dx_give.at[at], dx_land.at[at], (dx_send, dx_recv), r, (place.row, across))
        )
    ticks = [0]

    def tick():
        for index in TICKS[ticks[0]]:
            if chunks[index].moment > 0 and not chunks[index].done():
                chunks[index].advance()
        ticks[0] += 1

    def new_chunk(index, give, keep):
        chunk = chunks[index]
        if index >= SLOTS:
            chunks[index - SLOTS].reduces[0][0].wait_send()
            chunks[index - SLOTS].gave = True
        gives[index % SLOTS] = give().astype(LOW)
        chunk.advance()
        total[index] = keep().astype(LOW)

    greet([place.partner(link) for link in links] + [(place.row, flip(mate, 2))])
    give_at = pl.ds(pl.multiple_of((1 - core) * half, LANES), half)
    keep_at = pl.ds(pl.multiple_of(core * half, LANES), half)
    small_out[...] = jnp.zeros_like(small_out)

    def dense(w_out, w_up, w_down, joined, hat, spread_one, low, turned, active, slope, d_low, d_up):
        acc = dx_out
        loads = []
        for index, (src, dst) in enumerate(((w_out_in, w_out), (w_up_in, w_up), (w_down_in, w_down))):
            loads.append(pltpu.make_async_copy(src, dst, load_sem.at[index]))
            loads[-1].start()
        for group in range(4):
            joined[:, group * width : (group + 1) * width] = mixed[group]
        gain_one, shift_one = vecs[1:2, :], vecs[2:3, :]
        gain_two, shift_two = vecs[4:5, :], vecs[5:6, :]
        loads[0].wait()
        acc[...] = dot(joined[...], w_out[...])

        def norm_one(at, carry):
            v = x_in[at, :].astype(F32) + (acc[at, :] + vecs[0:1, :])
            centred = v - jnp.mean(v, axis=-1, keepdims=True)
            over = lax.rsqrt(jnp.mean(centred * centred, axis=-1, keepdims=True) + EPS)
            v = centred * over
            hat[at, :] = v
            spread_one[at, :] = jnp.broadcast_to(over, (BAND, LANES))
            low[at, :] = (v * gain_one + shift_one).astype(LOW)
            return carry

        bands(tokens_n, 0, norm_one)
        loads[1].wait()

        @pl.loop(0, inner_n // TILE)
        def _(tile):
            cols = pl.ds(pl.multiple_of(tile * TILE, TILE), TILE)
            u = dot(low[...], w_up[:, cols]) + up_bias[:, cols]
            for band in range(tokens_n // BAND):
                at = slice(band * BAND, (band + 1) * BAND)
                g, s = gelu_and_slope(u[at])
                active[at, cols] = g.astype(LOW)
                slope[at, cols] = s

        loads[2].wait()

        @pl.loop(0, features // TILE)
        def _(tile):
            cols = pl.ds(pl.multiple_of(tile * TILE, TILE), TILE)
            acc[:, cols] = dot(active[...], w_down[:, cols])

        def norm_two(at, carry):
            d_gain, d_shift, d_bias = carry
            v = hat[at, :] * gain_one + shift_one + (acc[at, :] + vecs[3:4, :])
            centred = v - jnp.mean(v, axis=-1, keepdims=True)
            over = lax.rsqrt(jnp.mean(centred * centred, axis=-1, keepdims=True) + EPS)
            v = centred * over
            result[at, :] = (v * gain_two + shift_two).astype(LOW)
            d = cot[at, :].astype(F32)
            d_gain += fold(d * v)
            d_shift += fold(d)
            d = d * gain_two
            d = d - jnp.mean(d, axis=-1, keepdims=True) - v * jnp.mean(d * v, axis=-1, keepdims=True)
            d = d * over
            acc[at, :] = d
            d = d.astype(LOW)
            d_low[at, :] = d
            return d_gain, d_shift, d_bias + fold(d.astype(F32))

        blank = jnp.zeros((8, features), F32)
        d_gain, d_shift, d_bias = bands(tokens_n, (blank, blank, blank), norm_two)
        for index, value in ((3, d_bias), (4, d_gain), (5, d_shift)):
            small_out[index : index + 1, :] = jnp.sum(value, axis=0, keepdims=True)

        for quarter in range(quarters):
            first = quarter * features

            def some_down(side):
                at = pl.ds(pl.multiple_of(first + side * half, LANES), half)
                return dot_tn(active[:, at], d_low[...])

            new_chunk(quarter, lambda: some_down(1 - core), lambda: some_down(core))
            tick()
        turned[...] = jnp.transpose(low[...])
        for quarter in range(quarters):
            first = quarter * features

            @pl.loop(0, features // TILE)
            def _(tile):
                rows = pl.ds(pl.multiple_of(first + tile * TILE, TILE), TILE)
                cols = pl.ds(pl.multiple_of(tile * TILE, TILE), TILE)
                d = (dot_nt(d_low[...], w_down[rows, :]) * slope[:, rows]).astype(LOW)
                d_up[:, cols] = d
                small_out[12 + quarter : 13 + quarter, cols] = jnp.sum(
                    d.astype(F32), axis=0, keepdims=True
                )

            tick()
            new_chunk(
                quarters + quarter,
                lambda: dot(turned[give_at, :], d_up[...]),
                lambda: dot(turned[keep_at, :], d_up[...]),
            )
            acc[...] += dot_nt(d_up[...], w_up[:, first : first + features])
            tick()

        def norm_back(at, carry):
            d_gain, d_shift, d_bias = carry
            v, d = hat[at, :], acc[at, :]
            d_gain += fold(d * v)
            d_shift += fold(d)
            d = d * gain_one
            d = d - jnp.mean(d, axis=-1, keepdims=True) - v * jnp.mean(d * v, axis=-1, keepdims=True)
            d = d * spread_one[at, 0:1]
            acc[at, :] = d
            d = d.astype(LOW)
            d_low[at, :] = d
            return d_gain, d_shift, d_bias + fold(d.astype(F32))

        d_gain, d_shift, d_bias = bands(tokens_n, (blank, blank, blank), norm_back)
        for index, value in ((0, d_bias), (1, d_gain), (2, d_shift)):
            small_out[index : index + 1, :] = jnp.sum(value, axis=0, keepdims=True)
        for group in range(4):
            at = slice(group * width, (group + 1) * width)
            d_give[group] = dot_nt(d_low[...], w_out[at, :]).astype(LOW)
        for r in range(rows_n):
            for index in range(3):
                d_copies[index, r].start()
        new_chunk(
            2 * quarters,
            lambda: dot_tn(joined[:, give_at], d_low[...]),
            lambda: dot_tn(joined[:, keep_at], d_low[...]),
        )
        tick()

    square = (tokens_n, features)
    pl.run_scoped(
        dense,
        pltpu.VMEM((features, features), LOW),
        pltpu.VMEM((features, inner_n), LOW),
        pltpu.VMEM((inner_n, features), LOW),
        pltpu.VMEM(square, LOW),
        pltpu.VMEM(square, F32),
        pltpu.VMEM((tokens_n, LANES), F32),
        pltpu.VMEM(square, LOW),
        pltpu.VMEM((features, tokens_n), LOW),
        pltpu.VMEM((tokens_n, inner_n), LOW),
        pltpu.VMEM((tokens_n, inner_n), F32),
        pltpu.VMEM(square, LOW),
        pltpu.VMEM(square, LOW),
    )

    def attention(qkv, x_turned, w_own, w_mate, d_heads, prob, d_score):
        loads = []
        for index, (src, dst) in enumerate(
            ((qkv_in, qkv), (turned_in, x_turned), (w_own_in, w_own), (w_mate_in, w_mate))
        ):
            loads.append(pltpu.make_async_copy(src, dst, load_sem.at[index]))
            loads[-1].start()
        for load in loads:
            load.wait()
        for r in range(rows_n):
            base = r * length
            own_rows = pl.ds(pl.multiple_of(base + me * part, 16), part)
            d_all[own_rows, :] = d_give[me, r * part : (r + 1) * part, :]
            for index in range(3):
                d_copies[index, r].wait_recv()
            d_row = d_all[base : base + length, :]
            for head in range(heads):
                d_heads[head] = d_row[:, head * HEAD_DIM : (head + 1) * HEAD_DIM]

            def scores(block):
                here = pl.ds(pl.multiple_of(base + block * LANES, LANES), LANES)
                local = pl.ds(pl.multiple_of(block * LANES, LANES), LANES)
                same = seg_wide[r] == seg_row[r : r + 1, local]
                for head in range(heads):
                    query = qkv[head, here, :]
                    key = qkv[heads + head, base : base + length, :]
                    value = qkv[2 * heads + head, base : base + length, :]
                    log_total = lse[r * heads + head : r * heads + head + 1, local]
                    p = jnp.exp(jnp.where(same, dot_nt(key, query) - log_total, MASKED))
                    dp = dot_nt(value, d_heads[head, local, :])
                    inner = jnp.sum(dp * p, axis=0, keepdims=True)
                    prob[head, :, local] = p.astype(LOW)
                    d_score[head, :, local] = (p * (dp - inner)).astype(LOW)

            blocks = length // LANES
            pl.loop(0, blocks // 2)(scores)
            tick()
            pl.loop(blocks // 2, blocks)(scores)
            tick()
            for head in range(heads):
                query = qkv[head, base : base + length, :]
                key = qkv[heads + head, base : base + length, :]
                ds = d_score[head]
                at = slice(base, base + length)
                left = head * HEAD_DIM
                dq = dot_tn(ds, key) * SCALE
                mine[at, left : left + HEAD_DIM] = dq.astype(LOW)
                left += width
                mine[at, left : left + HEAD_DIM] = dot(ds, query).astype(LOW)
                left += width
                mine[at, left : left + HEAD_DIM] = dot(prob[head], d_heads[head]).astype(LOW)
            g_copies[r].start()
            tick()

        def dx_of(r, owner):
            at = pl.ds(pl.multiple_of(r * length + owner * part, 16), part)
            return dot_nt(mine[at, :], w_own[...]) + dot_nt(other[at, :], w_mate[...])

        for r in range(rows_n):
            g_copies[r].wait_recv()
            at = pl.ds(r * part, part)
            dx_give[at, :] = dx_of(r, across).astype(LOW)
            dx_copies[r].start()
            tick()
        for index in range(3):
            left = index * width
            sums = [dot(x_turned[...], chip[side, :, left : left + width]) for side in range(2)]
            late_total[index] = jnp.concatenate(sums, axis=1).astype(LOW)
            chunks[2 * quarters + 1 + index].advance()
            tick()
        token_sums = jnp.sum(mine[...].astype(F32), axis=0, keepdims=True)
        group = lax.broadcasted_iota(jnp.int32, (4, 3 * width), 0)
        spread = jnp.where(group == me, token_sums, 0.0)
        spread = jnp.concatenate([spread, jnp.zeros((4, features - 3 * width), F32)], axis=1)
        small_out[8:12, :] = spread
        for r in range(rows_n):
            at = pl.ds(r * part, part)
            dx_out[at, :] += dx_of(r, me)
        tick()

    pl.run_scoped(
        attention,
        pltpu.VMEM(qkv_in.shape, LOW),
        pltpu.VMEM(turned_in.shape, LOW),
        pltpu.VMEM(w_own_in.shape, LOW),
        pltpu.VMEM(w_mate_in.shape, LOW),
        pltpu.VMEM((heads, length, HEAD_DIM), LOW),
        pltpu.VMEM((heads, length, length), LOW),
        pltpu.VMEM((heads, length, length), LOW),
    )
    smalls = [
        remote(
            small_out, small_land.at[number], (small_send, small_recv), number, place.partner(link)
        )
        for number, link in enumerate(links)
    ]
    gap = len(DRAIN) // (len(links) + 1)

    def small_step(number):
        if 0 < number <= len(links):
            smalls[number - 1].wait()
            small_out[...] += small_land[number - 1]
        if number < len(links):
            smalls[number].start()

    for at, index in enumerate(DRAIN):
        if at % gap == 0:
            small_step(at // gap)
        if not chunks[index].done():
            chunks[index].advance()
    for number in range((len(DRAIN) - 1) // gap + 1, len(links) + 1):
        small_step(number)
    while not all(chunk.done() for chunk in chunks):
        for chunk in chunks:
            if not chunk.done():
                chunk.advance()
    for r in range(rows_n):
        dx_copies[r].wait_recv()
        at = pl.ds(r * part, part)
        dx_out[at, :] += dx_land[at, :].astype(F32)
    for copy in dx_copies + g_copies + list(d_copies.values()):
        copy.wait_send()


def attend_rest(mesh_shape, x_rows, mixed, cot, vecs, up_bias, lse, seg_wide, seg_row, qkv, x_turned, w_out, w_up, w_down, w_own, w_mate):
    row_bits = [("r", bit) for bit in axis_bits(mesh_shape["rows"])]
    pos_bits = [("p", bit) for bit in axis_bits(mesh_shape["pos"])]
    name = dict(zip("cyxzw", pos_bits + row_bits))
    paths = [[name[letter] for letter in path] + row_bits[3:] for path in PATHS]
    late_paths = [row_bits[3:][::-1] + [name[letter] for letter in path] for path in LATE_PATHS]
    links = pos_bits + row_bits
    rows_n, length = seg_row.shape
    tokens_n, features = x_rows.shape
    inner_n = w_up.shape[1]
    width = mixed.shape[2]
    every = rows_n * length
    steps = len(links)
    half = features // 2
    early = landing_shape(features, features, links)
    late = landing_shape(half, half, row_bits)
    vmem = pl.BlockSpec(memory_space=pltpu.VMEM)
    hbm = pl.BlockSpec(memory_space=pl.ANY)
    dma = pltpu.SemaphoreType.DMA
    square = jax.ShapeDtypeStruct((features, features), LOW)
    return pl.pallas_call(
        partial(rest_kernel, rows_n, paths, late_paths, links),
        out_shape=[
            square,
            square,
            square,
            square,
            jax.ShapeDtypeStruct(w_up.shape, LOW),
            jax.ShapeDtypeStruct(w_down.shape, LOW),
            jax.ShapeDtypeStruct((tokens_n, features), LOW),
            jax.ShapeDtypeStruct((tokens_n, features), F32),
            jax.ShapeDtypeStruct((16, features), F32),
        ],
        in_specs=[vmem] * 8 + [hbm] * 7,
        out_specs=[hbm] * 6 + [vmem] * 3,
        scratch_shapes=[
            pltpu.VMEM((4, tokens_n, width), LOW),
            pltpu.VMEM((every, width), LOW),
            pltpu.VMEM((2, every, 3 * width), LOW),
            pltpu.VMEM((tokens_n, features), LOW),
            pltpu.VMEM((tokens_n, features), LOW),
            pltpu.VMEM((SLOTS, half, features), LOW),
            pltpu.VMEM((9, half, features), LOW),
            pltpu.VMEM((3, half, half), LOW),
            pltpu.VMEM((9, *early), LOW),
            pltpu.VMEM((3, *late), LOW),
            pltpu.VMEM((steps, 16, features), F32),
            dma((12, 2 * steps)),
            dma((12, 2 * steps)),
            dma((12,)),
            dma((steps,)),
            dma((steps,)),
            dma((3, rows_n)),
            dma((3, rows_n)),
            dma((rows_n,)),
            dma((rows_n,)),
            dma((rows_n,)),
            dma((rows_n,)),
            dma((4,)),
        ],
        compiler_params=pltpu.CompilerParams(
            collective_id=0, has_side_effects=True, vmem_limit_bytes=VMEM_LIMIT
        ),
        cost_estimate=pl.CostEstimate(
            flops=4 * 10**10, bytes_accessed=8 * 10**7, transcendentals=8 * 10**6
        ),
        name="attend_rest",
    )(x_rows, mixed, cot, vecs, up_bias, lse, seg_wide, seg_row, qkv, x_turned, w_out, w_up, w_down, w_own, w_mate)


def widen_kernel(*refs):
    half = len(refs) // 2
    for src, dst in zip(refs[:half], refs[half:]):
        dst[...] = src[...].astype(F32)


def widen(arrays, steps):
    specs = [pl.BlockSpec((a.shape[0] // steps, a.shape[1]), lambda i: (i, 0)) for a in arrays]
    moved = sum(6 * a.size for a in arrays)
    return pl.pallas_call(
        widen_kernel,
        grid=(steps,),
        out_shape=[jax.ShapeDtypeStruct(a.shape, F32) for a in arrays],
        in_specs=specs,
        out_specs=specs,
        compiler_params=pltpu.CompilerParams(vmem_limit_bytes=VMEM_LIMIT),
        cost_estimate=pl.CostEstimate(flops=0, bytes_accessed=moved, transcendentals=0),
        name="widen",
    )(*arrays)


def own_columns(w, index, width):
    return lax.dynamic_slice_in_dim(w, index * width, width, w.ndim - 1)


def on_device(
    mesh_shape,
    tokens,
    segments,
    w_query,
    b_query,
    w_key,
    w_value,
    b_value,
    w_out,
    b_out,
    gain_one,
    shift_one,
    w_up,
    b_up,
    w_down,
    b_down,
    gain_two,
    shift_two,
    cotangent,
):
    rows_n, part_len, features = tokens.shape
    length = segments.shape[1]
    groups = mesh_shape["pos"]
    width = features // groups
    here = lax.axis_index("pos")
    mate = here + 1 - 2 * lax.rem(here, 2)
    x_rows = tokens.reshape(rows_n * part_len, features)
    seg_row = segments.astype(F32)
    seg_wide = jnp.broadcast_to(seg_row[:, :, None], (rows_n, length, LANES))

    def heads_of(index):
        return jnp.concatenate(
            [own_columns(w, index, width) for w in (w_query, w_key, w_value)], axis=1
        )

    w_own, w_mate = heads_of(here), heads_of(mate)
    b_own = jnp.concatenate(
        [
            own_columns(b_query.astype(F32), here, width),
            jnp.zeros((width,), F32),
            own_columns(b_value.astype(F32), here, width),
        ]
    )[None]
    x_turned, qkv, lse, mixed = attend_forward(x_rows, w_own, b_own, seg_wide, seg_row, rows_n)
    vecs = jnp.stack([b_out, gain_one, shift_one, b_down, gain_two, shift_two]).astype(F32)
    *blocks, result, grad_tokens, small = attend_rest(
        mesh_shape,
        x_rows,
        mixed,
        cotangent.reshape(rows_n * part_len, features),
        jnp.pad(vecs, ((0, 2), (0, 0))),
        b_up.astype(F32)[None],
        lse,
        seg_wide,
        seg_row,
        qkv,
        x_turned,
        w_out,
        w_up,
        w_down,
        w_own,
        w_mate,
    )
    grad_w_query, grad_w_key, grad_w_value, grad_w_out, grad_w_up, grad_w_down = widen(blocks, 12)
    shape = (rows_n, part_len, features)
    return (
        result.reshape(shape),
        grad_tokens.reshape(shape),
        grad_w_query,
        small[8:12, :width].reshape(-1),
        grad_w_key,
        grad_w_value,
        small[8:12, 2 * width : 3 * width].reshape(-1),
        grad_w_out,
        small[0],
        small[1],
        small[2],
        grad_w_up,
        small[12:16].reshape(-1),
        grad_w_down,
        small[3],
        small[4],
        small[5],
    )


def solution(mesh):
    tokens = P("rows", "pos", None)
    return jax.shard_map(
        partial(on_device, dict(mesh.shape)),
        mesh=mesh,
        in_specs=(tokens, P("rows", None), *[P()] * 15, tokens),
        out_specs=(tokens, tokens, *[P()] * 15),
        check_vma=False,
    )
```

```python
from functools import partial

import jax
import jax.numpy as jnp
from jax import lax
from jax.experimental import pallas as pl
from jax.experimental.pallas import tpu as pltpu
from jax.sharding import PartitionSpec as P

HEADS = 12
HEAD_DIM = 64
EPS = 1e-05
MASKED = -1000000000.0
SCALE = HEAD_DIM ** (-0.5)
LANES = 128
VMEM_LIMIT = 60 * 2**20
MESH = pl.DeviceIdType.MESH
LOW = jnp.bfloat16
F32 = jnp.float32


def flip(value, bit):
    return value + bit - 2 * bit * lax.rem(lax.div(value, bit), 2)


def bit_of(value, bit):
    return lax.rem(lax.div(value, bit), 2)


def axis_bits(size):
    assert size & (size - 1) == 0
    return [1 << i for i in range(size.bit_length() - 1)]


def dot(a, b):
    return jnp.dot(a, b, preferred_element_type=F32)


def dot_nt(a, b):
    return lax.dot_general(a, b, (((1,), (1,)), ((), ())), preferred_element_type=F32)


def dot_tn(a, b):
    return lax.dot_general(a, b, (((0,), (0,)), ((), ())), preferred_element_type=F32)


class Place:
    def __init__(self):
        self.row = lax.axis_index("rows")
        self.pos = lax.axis_index("pos")

    def partner(self, link):
        axis, bit = link
        if axis == "r":
            return (flip(self.row, bit), self.pos)
        return (self.row, flip(self.pos, bit))

    def side(self, link):
        axis, bit = link
        return bit_of(self.row if axis == "r" else self.pos, bit)


def remote(src, dst, sems, index, device):
    send_sem, recv_sem = sems
    return pltpu.make_async_remote_copy(
        src_ref=src,
        dst_ref=dst,
        send_sem=send_sem.at[index],
        recv_sem=recv_sem.at[index],
        device_id=device,
        device_id_type=MESH,
    )


def greet(devices):
    barrier = pltpu.get_barrier_semaphore()
    for device in devices:
        pl.semaphore_signal(barrier, inc=1, device_id=device, device_id_type=MESH)
    pl.semaphore_wait(barrier, len(devices))


def rows_at(ref, start, size):
    return ref.at[pl.ds(pl.multiple_of(start, 16), size)]


def plan_splits(rows, cols, links):
    kinds = []
    for _ in links:
        if (rows // 2) % 16 == 0:
            rows //= 2
            kinds.append("rows")
        elif (cols // 2) % LANES == 0:
            cols //= 2
            kinds.append("cols")
        else:
            kinds.append("whole")
    return kinds


def shrink(rows, cols, kind):
    return (rows // 2 if kind == "rows" else rows, cols // 2 if kind == "cols" else cols)


def landing_shape(rows, cols, links):
    total, widest = 0, 0
    for kind in plan_splits(rows, cols, links):
        rows, cols = shrink(rows, cols, kind)
        total, widest = total + rows, max(widest, cols)
    return total, widest


def add_into(dst, left, right, rows):
    step = 16 if rows % 48 else 48

    @pl.loop(0, rows // step)
    def _(i):
        at = pl.ds(pl.multiple_of(i * step, step), step)
        dst[at, :] = (left[at, :].astype(F32) + right[at, :].astype(F32)).astype(dst.dtype)


def window(ref, row0, rows, col0, cols):
    if not isinstance(row0, int):
        row0 = pl.multiple_of(row0, 16)
    if not isinstance(col0, int):
        col0 = pl.multiple_of(col0, LANES)
    return ref.at[pl.ds(row0, rows), pl.ds(col0, cols)]


class Chunk:
    def __init__(self, place, fixed, path, gather, give, out, total, landing, sems):
        send_sem, recv_sem, copy_sem = sems
        self.reduces, self.gathers, self.moment, self.gave = [], [], 0, False
        rows, cols = out.shape
        row0, col0, landed, slot = 0, 0, 0, 0
        corner = None
        row_trail, col_trail, kind_of = [], [], {}

        def held(at, rows, cols):
            return window(total, at[0] - corner[0], rows, at[1] - corner[1], cols)

        shape = out.shape
        for _, kind in fixed:
            shape = shrink(*shape, kind)
        kinds = [kind for _, kind in fixed] + plan_splits(*shape, path)
        for number, (link, kind) in enumerate(zip([link for link, _ in fixed] + path, kinds)):
            side = place.side(link)
            kind_of[link] = kind
            keep = other = (row0, col0)
            if kind == "rows":
                row_trail.append((row0, rows))
                rows //= 2
                keep, other = (row0 + side * rows, col0), (row0 + (1 - side) * rows, col0)
            elif kind == "cols":
                col_trail.append((col0, cols))
                cols //= 2
                keep, other = (row0, col0 + side * cols), (row0, col0 + (1 - side) * cols)
            row0, col0 = keep
            if number == max(len(fixed) - 1, 0):
                corner = keep
            if number < len(fixed):
                continue
            land = window(landing, landed, rows, 0, cols)
            landed += rows
            src = give if number == 0 else held(other, rows, cols)
            copy = remote(src, land, (send_sem, recv_sem), slot, place.partner(link))
            slot += 1
            self.reduces.append((copy, held(keep, rows, cols), land, kind == "whole"))
        mine = window(out, row0, rows, col0, cols)
        self.own = pltpu.make_async_copy(held((row0, col0), rows, cols), mine, copy_sem)
        for link in gather:
            kind = kind_of[link]
            if kind == "whole":
                self.gathers.append(None)
                continue
            here = window(out, row0, rows, col0, cols)
            self.gathers.append(remote(here, here, (send_sem, recv_sem), slot, place.partner(link)))
            slot += 1
            if kind == "rows":
                row0, rows = row_trail.pop()
            else:
                col0, cols = col_trail.pop()

    def done(self):
        return self.moment > len(self.reduces) + len(self.gathers)

    def advance(self):
        count, now = len(self.reduces), self.moment
        if 0 < now <= count:
            copy, keep, land, whole = self.reduces[now - 1]
            copy.wait_recv()
            if whole:
                copy.wait_send()
            add_into(keep, keep, land, land.shape[0])
        elif now > count and self.gathers[now - count - 1] is not None:
            self.gathers[now - count - 1].wait_recv()
        if now < count:
            self.reduces[now][0].start()
        elif now < count + len(self.gathers):
            if now == count:
                self.own.start()
                self.own.wait()
            if self.gathers[now - count] is not None:
                self.gathers[now - count].start()
        else:
            for index, (copy, _, _, whole) in enumerate(self.reduces):
                if not whole and not (index == 0 and self.gave):
                    copy.wait_send()
            for copy in self.gathers:
                if copy is not None:
                    copy.wait_send()
        self.moment += 1


PATHS = ("cxyzw", "cyxzw", "czwxy", "cyxzw", "cxyzw", "czwxy", "cxyzw", "czwxy", "cyzwx")
LATE_PATHS = ("wzxyc", "wzyxc", "wzyxc")
TICKS = (
    (),
    (),
    (),
    (),
    (0, 1, 2, 3),
    (),
    (),
    (4,),
    (),
    (0, 1, 2, 5),
    (6,),
    (3,),
    (0, 1, 4, 7),
    (0, 2, 5, 6, 1),
    (3,),
    (8, 0, 2, 4, 7),
    (),
    (6,),
    (5, 3),
    (1,),
    (0, 4, 8, 2),
    (5, 6),
    (),
    (),
    (0, 2, 3, 7, 1, 5),
    (),
    (4, 8),
    (6,),
    (1, 2, 3),
)
DRAIN = (7, 4, 9, 8, 10, 6, 3, 11, 4, 9, 0, 1, 5, 10, 8, 2, 7, 6, 11, 3, 4, 9, 10, 11, 0, 1, 7, 2, 5, 9, 8, 10, 0, 6, 1, 2, 11, 4, 9, 7, 3, 4, 5, 10, 3, 11, 8, 6, 9, 6, 10, 7, 11, 5, 8, 5, 9, 10, 9, 7, 10, 11, 7, 8, 11, 8)
TAIL_STEEP = 0.24
TAIL = (
    0.09575598852910579,
    0.09547705164870551,
    0.093198719112773,
    0.06193635630868121,
    0.1216760657292812,
    -0.06984360139735674,
    0.1555215658230106,
    -0.05372215169653546,
)
TILE = 256
BAND = 48
SLOTS = 4


def gelu_and_slope(u):
    bell = jnp.exp(u * u * -0.5)
    t = 1.0 / (1.0 + TAIL_STEEP * jnp.abs(u))
    f = TAIL[-1]
    for coefficient in TAIL[-2::-1]:
        f = f * t + coefficient
    below = f * t * bell
    phi = jnp.where(u > 0, 1.0 - below, below)
    return u * phi, phi + u * (bell * 0.3989422804014327)


def fold(v):
    return jnp.sum(v.reshape(v.shape[0] // 8, 8, v.shape[1]), axis=0)


def bands(n, init, body):
    def step(i, carry):
        return body(pl.ds(pl.multiple_of(i * BAND, BAND), BAND), carry)

    return lax.fori_loop(0, n // BAND, step, init)


def layer_kernel(rows_n, paths, late_paths, links, *refs):
    vector_refs, refs = refs[:9], refs[9:]
    (x_in, cot, segments, q_in, k_in, v_in, w_out_in, w_up_in, w_down_in) = refs[:9]
    refs = refs[:2] + refs[1:]
    (q_out, k_out, v_out, o_out, up_out, down_out, qkv_kept, turned_kept) = refs[10:18]
    (result, dx_out, small_out) = refs[18:21]
    (x_all, mixed, w_out, w_up, w_down, w_own, w_mate, lse, seg_row, seg_wide) = refs[21:31]
    (d_all, chip, dx_give, dx_land, gives, total, late_total, landing, late_land) = refs[31:40]
    (small_land, send_sem, recv_sem, copy_sem, small_send, small_recv) = refs[40:46]
    (x_send, x_recv, m_send, m_recv, d_send, d_recv) = refs[46:52]
    (g_send, g_recv, dx_send, dx_recv, load_sem, own_sem, vecs) = refs[52:59]
    d_give = mixed
    place = Place()
    me = place.pos
    mate, across = flip(me, 1), flip(me, 2)
    far = flip(mate, 2)
    peers = [across, far, mate]
    core = bit_of(me, 1)
    tokens_n, features = x_in.shape
    part = tokens_n // rows_n
    length = 4 * part
    width = d_all.shape[1]
    heads = width // HEAD_DIM
    inner_n = w_up.shape[1]
    half = features // 2
    quarters = inner_n // features
    outs = [window(down_out, j * features, features, 0, features) for j in range(inner_n // features)]
    outs += [window(up_out, 0, features, j * features, features) for j in range(inner_n // features)]
    outs += [o_out]
    chunks = []
    for index, out in enumerate(outs + [q_out, k_out, v_out]):
        sems = (send_sem.at[index], recv_sem.at[index], copy_sem.at[index])
        if index < len(outs):
            path = paths[index]
            spaces = (gives.at[index % SLOTS], out, total.at[index], landing.at[index])
            chunks.append(Chunk(place, [], path, path[::-1], *spaces, sems))
        else:
            at = index - len(outs)
            fixed = [(links[0], "rows"), (links[1], "cols")]
            spaces = (None, out, late_total.at[at], late_land.at[at])
            chunks.append(Chunk(place, fixed, links[2:], late_paths[at], *spaces, sems))
    mine, other = chip.at[core], chip.at[1 - core]
    d_copies, g_copies, dx_copies = {}, [], []
    for r in range(rows_n):
        at = pl.ds(r * part, part)
        row = pl.ds(r * length, length)
        for index, peer in enumerate(peers):
            d_copies[index, r] = remote(
                d_give.at[peer, at],
                rows_at(d_all, r * length + me * part, part),
                (d_send, d_recv),
                (index, r),
                (place.row, peer),
            )
        g_copies.append(
            remote(mine.at[row], mine.at[row], (g_send, g_recv), r, (place.row, mate))
        )
        dx_copies.append(
            remote(dx_give.at[at], dx_land.at[at], (dx_send, dx_recv), r, (place.row, across))
        )
    ticks = [0]

    def tick():
        for index in TICKS[ticks[0]]:
            if chunks[index].moment > 0 and not chunks[index].done():
                chunks[index].advance()
        ticks[0] += 1

    def new_chunk(index, give, keep):
        chunk = chunks[index]
        if index >= SLOTS:
            chunks[index - SLOTS].reduces[0][0].wait_send()
            chunks[index - SLOTS].gave = True
        gives[index % SLOTS] = give().astype(LOW)
        chunk.advance()
        total[index] = keep().astype(LOW)

    to_across, to_mate, passed, own, m_copies = [], [], [], [], []

    def x_spot(r, owner):
        return rows_at(x_all, r * length + owner * part, part)

    for r in range(rows_n):
        src = x_in.at[pl.ds(r * part, part)]
        x_sems = (x_send, x_recv)
        to_across.append(remote(src, x_spot(r, me), x_sems, (0, r), (place.row, across)))
        to_mate.append(remote(src, x_spot(r, me), x_sems, (1, r), (place.row, mate)))
        spot = x_spot(r, across)
        passed.append(remote(spot, spot, x_sems, (2, r), (place.row, mate)))
        own.append(pltpu.make_async_copy(src, x_spot(r, me), own_sem.at[r]))
        own[r].start()
    weights = [
        pltpu.make_async_copy(src, dst, load_sem.at[index])
        for index, (src, dst) in enumerate(((w_out_in, w_out), (w_up_in, w_up), (w_down_in, w_down)))
    ]
    greet([place.partner(link) for link in links] + [(place.row, far)])
    for r in range(rows_n):
        to_across[r].start()
        to_mate[r].start()
    give_at = pl.ds(pl.multiple_of((1 - core) * half, LANES), half)
    keep_at = pl.ds(pl.multiple_of(core * half, LANES), half)
    small_out[...] = jnp.zeros_like(small_out)

    def attend(windows, qkv, x_turned, blend, lse_cols):
        loads = []
        for owner in range(2):
            first = lax.div(3 * (me if owner == 0 else mate), 2) * LANES
            for index, src in enumerate((q_in, k_in, v_in)):
                at = 3 * owner + index
                window_of = src.at[:, pl.ds(pl.multiple_of(first, LANES), TILE)]
                loads.append(pltpu.make_async_copy(window_of, windows.at[at], load_sem.at[3 + at]))
                loads[-1].start()
        for copy in weights:
            copy.start()
        for index, ref in enumerate(vector_refs[:8]):
            vecs[index : index + 1, :] = ref[...].astype(F32)[None]
        up_bias = vector_refs[8][...].astype(F32)[None]
        for quarter in range(quarters):
            at = slice(quarter * features, (quarter + 1) * features)
            vecs[8 + quarter : 9 + quarter, :] = up_bias[:, at]
        seg_row[...] = segments[...].astype(F32)
        for r in range(rows_n):
            row = seg_row[r : r + 1, :]
            seg_wide[r] = jnp.transpose(jnp.broadcast_to(row, (LANES, length)))
        for load in loads:
            load.wait()
        for owner, dst in enumerate((w_own, w_mate)):
            for index in range(3):
                at = slice(index * width, (index + 1) * width)
                for odd in range(2):

                    @pl.when(lax.rem(me + owner, 2) == odd)
                    def _():
                        left = odd * HEAD_DIM
                        dst[:, at] = windows[3 * owner + index, :, left : left + width]

        first = pl.ds(pl.multiple_of(lax.div(3 * me, 2) * LANES, LANES), TILE)
        odd = lax.rem(me, 2) == 1
        biases = []
        for index in range(2):
            bias = vecs[index : index + 1, first]
            biases.append(jnp.where(odd, bias[:, HEAD_DIM : HEAD_DIM + width], bias[:, :width]))
        b_own = jnp.concatenate([biases[0], jnp.zeros((1, width), F32), biases[1]], axis=1)
        is_query = lax.broadcasted_iota(jnp.int32, (1, 3 * width), 1) < width
        scale = jnp.where(is_query, SCALE, 1.0)
        kept = []
        for r in range(rows_n):
            to_across[r].wait_recv()
            passed[r].start()
            to_mate[r].wait_recv()
            own[r].wait()
            passed[r].wait_recv()
            base = r * length
            x_row = x_all[base : base + length, :]
            made = ((dot(x_row, w_own[...]) + b_own) * scale).astype(LOW)
            for index in range(3 * heads):
                left = index * HEAD_DIM
                qkv[index, base : base + length, :] = made[:, left : left + HEAD_DIM]
            row = pl.ds(base, length)
            kept.append(
                pltpu.make_async_copy(qkv.at[:, row, :], qkv_kept.at[:, row, :], own_sem.at[r])
            )
            kept[-1].start()

            @pl.loop(0, length // LANES)
            def _(block):
                here = pl.ds(pl.multiple_of(base + block * LANES, LANES), LANES)
                local = pl.ds(pl.multiple_of(block * LANES, LANES), LANES)
                seg_q = seg_wide[r, local, :]
                same = jnp.concatenate([seg_q] * (length // LANES), axis=1) == seg_row[r : r + 1, :]
                for head in range(heads):
                    query = qkv[head, here, :]
                    key = qkv[heads + head, base : base + length, :]
                    value = qkv[2 * heads + head, base : base + length, :]
                    scores = jnp.where(same, dot_nt(query, key), MASKED)
                    top = jnp.max(scores, axis=-1, keepdims=True)
                    power = jnp.exp(scores - top)
                    sums = jnp.sum(power, axis=-1, keepdims=True)
                    out = dot(power.astype(LOW), value) / sums
                    blend[here, head * HEAD_DIM : (head + 1) * HEAD_DIM] = out.astype(LOW)
                    column = r * heads + head
                    lse_cols[local, column : column + 1] = top + jnp.log(sums)

            for index, peer in enumerate(peers):
                copy = remote(
                    rows_at(blend, base + peer * part, part),
                    mixed.at[me, pl.ds(r * part, part)],
                    (m_send, m_recv),
                    (index, r),
                    (place.row, peer),
                )
                copy.start()
                m_copies.append(copy)
            mixed[me, r * part : (r + 1) * part, :] = blend[
                pl.ds(pl.multiple_of(base + me * part, 16), part), :
            ]
        lse[...] = jnp.transpose(lse_cols[...])[: lse.shape[0], :]
        mine_half = pl.ds(pl.multiple_of(core * half, LANES), half)
        for r in range(rows_n):
            base = r * length
            x_turned[:, base : base + length] = jnp.transpose(x_all[base : base + length, mine_half])
        kept.append(pltpu.make_async_copy(x_turned, turned_kept, own_sem.at[rows_n]))
        kept[-1].start()
        for copy in to_across + to_mate + passed:
            copy.wait_send()
        for copy in m_copies:
            copy.wait()
        for copy in kept:
            copy.wait()

    every = rows_n * length
    pl.run_scoped(
        attend,
        pltpu.VMEM((6, features, TILE), LOW),
        pltpu.VMEM(qkv_kept.shape, LOW),
        pltpu.VMEM(turned_kept.shape, LOW),
        pltpu.VMEM((every, width), LOW),
        pltpu.VMEM((length, LANES), F32),
    )

    active = x_all

    def dense(joined, hat, spread_one, low, turned, slope, d_low, d_up):
        acc = dx_out
        for group in range(4):
            joined[:, group * width : (group + 1) * width] = mixed[group]
        gain_one, shift_one = vecs[3:4, :], vecs[4:5, :]
        gain_two, shift_two = vecs[6:7, :], vecs[7:8, :]
        weights[0].wait()
        acc[...] = dot(joined[...], w_out[...])

        def norm_one(at, carry):
            v = x_in[at, :].astype(F32) + (acc[at, :] + vecs[2:3, :])
            centred = v - jnp.mean(v, axis=-1, keepdims=True)
            over = lax.rsqrt(jnp.mean(centred * centred, axis=-1, keepdims=True) + EPS)
            v = centred * over
            hat[at, :] = v
            spread_one[at, :] = jnp.broadcast_to(over, (BAND, LANES))
            low[at, :] = (v * gain_one + shift_one).astype(LOW)
            return carry

        bands(tokens_n, 0, norm_one)
        weights[1].wait()
        for quarter in range(quarters):

            @pl.loop(0, features // TILE)
            def _(tile):
                cols = pl.ds(pl.multiple_of(tile * TILE, TILE), TILE)
                wide = pl.ds(pl.multiple_of(quarter * features + tile * TILE, TILE), TILE)
                u = dot(low[...], w_up[:, wide]) + vecs[8 + quarter : 9 + quarter, cols]
                for band in range(tokens_n // BAND):
                    at = slice(band * BAND, (band + 1) * BAND)
                    g, s = gelu_and_slope(u[at])
                    active[quarter * tokens_n + band * BAND : quarter * tokens_n + (band + 1) * BAND, cols] = g.astype(LOW)
                    slope[at, wide] = s

        weights[2].wait()

        @pl.loop(0, features // TILE)
        def _(tile):
            cols = pl.ds(pl.multiple_of(tile * TILE, TILE), TILE)
            acc[:, cols] = sum(
                dot(
                    active[quarter * tokens_n : (quarter + 1) * tokens_n, :],
                    w_down[quarter * features : (quarter + 1) * features, cols],
                )
                for quarter in range(quarters)
            )

        def norm_two(at, carry):
            d_gain, d_shift, d_bias = carry
            v = hat[at, :] * gain_one + shift_one + (acc[at, :] + vecs[5:6, :])
            centred = v - jnp.mean(v, axis=-1, keepdims=True)
            over = lax.rsqrt(jnp.mean(centred * centred, axis=-1, keepdims=True) + EPS)
            v = centred * over
            result[at, :] = (v * gain_two + shift_two).astype(LOW)
            d = cot[at, :].astype(F32)
            d_gain += fold(d * v)
            d_shift += fold(d)
            d = d * gain_two
            d = d - jnp.mean(d, axis=-1, keepdims=True) - v * jnp.mean(d * v, axis=-1, keepdims=True)
            d = d * over
            acc[at, :] = d
            d = d.astype(LOW)
            d_low[at, :] = d
            return d_gain, d_shift, d_bias + fold(d.astype(F32))

        blank = jnp.zeros((8, features), F32)
        d_gain, d_shift, d_bias = bands(tokens_n, (blank, blank, blank), norm_two)
        for index, value in ((3, d_bias), (4, d_gain), (5, d_shift)):
            small_out[index : index + 1, :] = jnp.sum(value, axis=0, keepdims=True)

        for quarter in range(quarters):

            def some_down(side):
                at = pl.ds(pl.multiple_of(side * half, LANES), half)
                return dot_tn(active[quarter * tokens_n : (quarter + 1) * tokens_n, at], d_low[...])

            new_chunk(quarter, lambda: some_down(1 - core), lambda: some_down(core))
            tick()
        turned[...] = jnp.transpose(low[...])
        for quarter in range(quarters):
            first = quarter * features

            @pl.loop(0, features // TILE)
            def _(tile):
                rows = pl.ds(pl.multiple_of(first + tile * TILE, TILE), TILE)
                cols = pl.ds(pl.multiple_of(tile * TILE, TILE), TILE)
                d = (dot_nt(d_low[...], w_down[rows, :]) * slope[:, rows]).astype(LOW)
                d_up[:, cols] = d
                small_out[12 + quarter : 13 + quarter, cols] = jnp.sum(
                    d.astype(F32), axis=0, keepdims=True
                )

            tick()
            new_chunk(
                quarters + quarter,
                lambda: dot(turned[give_at, :], d_up[...]),
                lambda: dot(turned[keep_at, :], d_up[...]),
            )
            acc[...] += dot_nt(d_up[...], w_up[:, first : first + features])
            tick()

        def norm_back(at, carry):
            d_gain, d_shift, d_bias = carry
            v, d = hat[at, :], acc[at, :]
            d_gain += fold(d * v)
            d_shift += fold(d)
            d = d * gain_one
            d = d - jnp.mean(d, axis=-1, keepdims=True) - v * jnp.mean(d * v, axis=-1, keepdims=True)
            d = d * spread_one[at, 0:1]
            acc[at, :] = d
            d = d.astype(LOW)
            d_low[at, :] = d
            return d_gain, d_shift, d_bias + fold(d.astype(F32))

        d_gain, d_shift, d_bias = bands(tokens_n, (blank, blank, blank), norm_back)
        for index, value in ((0, d_bias), (1, d_gain), (2, d_shift)):
            small_out[index : index + 1, :] = jnp.sum(value, axis=0, keepdims=True)
        for group in range(4):
            at = slice(group * width, (group + 1) * width)
            d_give[group] = dot_nt(d_low[...], w_out[at, :]).astype(LOW)
        for r in range(rows_n):
            for index in range(3):
                d_copies[index, r].start()
        new_chunk(
            2 * quarters,
            lambda: dot_tn(joined[:, give_at], d_low[...]),
            lambda: dot_tn(joined[:, keep_at], d_low[...]),
        )
        tick()

    square = (tokens_n, features)
    pl.run_scoped(
        dense,
        pltpu.VMEM(square, LOW),
        pltpu.VMEM(square, F32),
        pltpu.VMEM((tokens_n, LANES), F32),
        pltpu.VMEM(square, LOW),
        pltpu.VMEM((features, tokens_n), LOW),
        pltpu.VMEM((tokens_n, inner_n), F32),
        pltpu.VMEM(square, LOW),
        pltpu.VMEM(square, LOW),
    )
    prob = [w_up.at[pl.ds(0, length), pl.ds(head * length, length)] for head in range(heads)]
    d_score = [w_down.at[pl.ds(head * features, length), pl.ds(0, length)] for head in range(heads)]

    def attention(qkv, x_turned, d_heads):
        loads = []
        for index, (src, dst) in enumerate(((qkv_kept, qkv), (turned_kept, x_turned))):
            loads.append(pltpu.make_async_copy(src, dst, load_sem.at[index]))
            loads[-1].start()
        for load in loads:
            load.wait()
        for r in range(rows_n):
            base = r * length
            own_rows = pl.ds(pl.multiple_of(base + me * part, 16), part)
            d_all[own_rows, :] = d_give[me, r * part : (r + 1) * part, :]
            for index in range(3):
                d_copies[index, r].wait_recv()
            d_row = d_all[base : base + length, :]
            for head in range(heads):
                d_heads[head] = d_row[:, head * HEAD_DIM : (head + 1) * HEAD_DIM]

            def scores(block):
                here = pl.ds(pl.multiple_of(base + block * LANES, LANES), LANES)
                local = pl.ds(pl.multiple_of(block * LANES, LANES), LANES)
                same = seg_wide[r] == seg_row[r : r + 1, local]
                for head in range(heads):
                    query = qkv[head, here, :]
                    key = qkv[heads + head, base : base + length, :]
                    value = qkv[2 * heads + head, base : base + length, :]
                    log_total = lse[r * heads + head : r * heads + head + 1, local]
                    p = jnp.exp(jnp.where(same, dot_nt(key, query) - log_total, MASKED))
                    dp = dot_nt(value, d_heads[head, local, :])
                    inner = jnp.sum(dp * p, axis=0, keepdims=True)
                    prob[head][:, local] = p.astype(LOW)
                    d_score[head][:, local] = (p * (dp - inner)).astype(LOW)

            blocks = length // LANES
            pl.loop(0, blocks // 2)(scores)
            tick()
            pl.loop(blocks // 2, blocks)(scores)
            tick()
            for head in range(heads):
                query = qkv[head, base : base + length, :]
                key = qkv[heads + head, base : base + length, :]
                ds = d_score[head][...]
                at = slice(base, base + length)
                left = head * HEAD_DIM
                dq = dot_tn(ds, key) * SCALE
                mine[at, left : left + HEAD_DIM] = dq.astype(LOW)
                left += width
                mine[at, left : left + HEAD_DIM] = dot(ds, query).astype(LOW)
                left += width
                mine[at, left : left + HEAD_DIM] = dot(prob[head][...], d_heads[head]).astype(LOW)
            g_copies[r].start()
            tick()

        def dx_of(r, owner):
            at = pl.ds(pl.multiple_of(r * length + owner * part, 16), part)
            return dot_nt(mine[at, :], w_own[...]) + dot_nt(other[at, :], w_mate[...])

        for r in range(rows_n):
            g_copies[r].wait_recv()
            at = pl.ds(r * part, part)
            dx_give[at, :] = dx_of(r, across).astype(LOW)
            dx_copies[r].start()
            tick()
        for index in range(3):
            left = index * width
            sums = [dot(x_turned[...], chip[side, :, left : left + width]) for side in range(2)]
            late_total[index] = jnp.concatenate(sums, axis=1).astype(LOW)
            chunks[2 * quarters + 1 + index].advance()
            tick()
        token_sums = jnp.sum(mine[...].astype(F32), axis=0, keepdims=True)
        owner = lax.div(lax.broadcasted_iota(jnp.int32, (1, features), 1), width)
        for row, left in ((8, 0), (9, 2 * width)):
            spread = jnp.concatenate([token_sums[:, left : left + width]] * 4, axis=1)
            small_out[row : row + 1, :] = jnp.where(owner == me, spread, 0.0)
        for r in range(rows_n):
            at = pl.ds(r * part, part)
            dx_out[at, :] += dx_of(r, me)
        tick()

    pl.run_scoped(
        attention,
        pltpu.VMEM(qkv_kept.shape, LOW),
        pltpu.VMEM(turned_kept.shape, LOW),
        pltpu.VMEM((heads, length, HEAD_DIM), LOW),
    )
    smalls = [
        remote(
            small_out, small_land.at[number], (small_send, small_recv), number, place.partner(link)
        )
        for number, link in enumerate(links)
    ]
    gap = len(DRAIN) // (len(links) + 1)

    def small_step(number):
        if 0 < number <= len(links):
            smalls[number - 1].wait()
            small_out[...] += small_land[number - 1]
        if number < len(links):
            smalls[number].start()

    for at, index in enumerate(DRAIN):
        if at % gap == 0:
            small_step(at // gap)
        if not chunks[index].done():
            chunks[index].advance()
    for number in range((len(DRAIN) - 1) // gap + 1, len(links) + 1):
        small_step(number)
    while not all(chunk.done() for chunk in chunks):
        for chunk in chunks:
            if not chunk.done():
                chunk.advance()
    for r in range(rows_n):
        dx_copies[r].wait_recv()
        at = pl.ds(r * part, part)
        dx_out[at, :] += dx_land[at, :].astype(F32)
    for copy in dx_copies + g_copies + list(d_copies.values()):
        copy.wait_send()


def layer(mesh_shape, vectors, x_rows, cot, segments, weights):
    row_bits = [("r", bit) for bit in axis_bits(mesh_shape["rows"])]
    pos_bits = [("p", bit) for bit in axis_bits(mesh_shape["pos"])]
    name = dict(zip("cyxzw", pos_bits + row_bits))
    paths = [[name[letter] for letter in path] + row_bits[3:] for path in PATHS]
    late_paths = [row_bits[3:][::-1] + [name[letter] for letter in path] for path in LATE_PATHS]
    links = pos_bits + row_bits
    rows_n, length = segments.shape
    tokens_n, features = x_rows.shape
    inner_n = weights[4].shape[1]
    width = features // 4
    every = rows_n * length
    steps = len(links)
    half = features // 2
    early = landing_shape(features, features, links)
    late = landing_shape(half, half, row_bits)
    vmem = pl.BlockSpec(memory_space=pltpu.VMEM)
    hbm = pl.BlockSpec(memory_space=pl.ANY)
    dma = pltpu.SemaphoreType.DMA
    shape = jax.ShapeDtypeStruct
    square = shape((features, features), LOW)
    return pl.pallas_call(
        partial(layer_kernel, rows_n, paths, late_paths, links),
        out_shape=[
            square,
            square,
            square,
            square,
            shape((features, inner_n), LOW),
            shape((inner_n, features), LOW),
            shape((3 * width // HEAD_DIM, every, HEAD_DIM), LOW),
            shape((half, every), LOW),
            shape((tokens_n, features), LOW),
            shape((tokens_n, features), F32),
            shape((16, features), F32),
        ],
        in_specs=[vmem] * 12 + [hbm] * 6,
        out_specs=[hbm] * 8 + [vmem] * 3,
        scratch_shapes=[
            pltpu.VMEM((every, features), LOW),
            pltpu.VMEM((4, tokens_n, width), LOW),
            pltpu.VMEM((features, features), LOW),
            pltpu.VMEM((features, inner_n), LOW),
            pltpu.VMEM((inner_n, features), LOW),
            pltpu.VMEM((features, 3 * width), LOW),
            pltpu.VMEM((features, 3 * width), LOW),
            pltpu.VMEM((16, length), F32),
            pltpu.VMEM((rows_n, length), F32),
            pltpu.VMEM((rows_n, length, LANES), F32),
            pltpu.VMEM((every, width), LOW),
            pltpu.VMEM((2, every, 3 * width), LOW),
            pltpu.VMEM((tokens_n, features), LOW),
            pltpu.VMEM((tokens_n, features), LOW),
            pltpu.VMEM((SLOTS, half, features), LOW),
            pltpu.VMEM((9, half, features), LOW),
            pltpu.VMEM((3, half, half), LOW),
            pltpu.VMEM((9, *early), LOW),
            pltpu.VMEM((3, *late), LOW),
            pltpu.VMEM((steps, 16, features), F32),
            dma((12, 2 * steps)),
            dma((12, 2 * steps)),
            dma((12,)),
            dma((steps,)),
            dma((steps,)),
            *[dma((3, rows_n))] * 6,
            *[dma((rows_n,))] * 4,
            dma((9,)),
            dma((rows_n + 1,)),
            pltpu.VMEM((16, features), F32),
        ],
        compiler_params=pltpu.CompilerParams(
            collective_id=0, has_side_effects=True, vmem_limit_bytes=VMEM_LIMIT
        ),
        cost_estimate=pl.CostEstimate(
            flops=4 * 10**10, bytes_accessed=8 * 10**7, transcendentals=8 * 10**6
        ),
        name="layer",
    )(*vectors, x_rows, cot, segments, *weights)


def finish_kernel(moved, *refs):
    sources = refs[: moved + 1]
    outs = refs[moved + 1 :]
    for src, dst in zip(sources[:moved], outs[:moved]):
        dst[...] = src[...].astype(dst.dtype)
    small = sources[moved]
    for index, dst in enumerate(outs[moved:-1]):
        dst[...] = small[index, :]
    outs[-1][...] = jnp.concatenate([small[index, :] for index in range(12, 16)])


def finish(blocks, result, grad_tokens, small, steps):
    arrays = [*blocks, result, grad_tokens]
    kinds = [F32] * len(blocks) + [result.dtype, grad_tokens.dtype]
    specs = [pl.BlockSpec((a.shape[0] // steps, a.shape[1]), lambda i: (i, 0)) for a in arrays]
    features = small.shape[1]
    vectors = [features] * 10 + [4 * features]
    shape = jax.ShapeDtypeStruct
    return pl.pallas_call(
        partial(finish_kernel, len(arrays)),
        grid=(steps,),
        out_shape=[shape(a.shape, kind) for a, kind in zip(arrays, kinds)]
        + [shape((size,), F32) for size in vectors],
        in_specs=[*specs, pl.BlockSpec(small.shape, lambda i: (0, 0))],
        out_specs=[*specs, *[pl.BlockSpec((size,), lambda i: (0,)) for size in vectors]],
        compiler_params=pltpu.CompilerParams(vmem_limit_bytes=VMEM_LIMIT),
        cost_estimate=pl.CostEstimate(
            flops=0, bytes_accessed=6 * sum(a.size for a in arrays), transcendentals=0
        ),
        name="finish",
    )(*arrays, small)


def on_device(
    mesh_shape,
    tokens,
    segments,
    w_query,
    b_query,
    w_key,
    w_value,
    b_value,
    w_out,
    b_out,
    gain_one,
    shift_one,
    w_up,
    b_up,
    w_down,
    b_down,
    gain_two,
    shift_two,
    cotangent,
):
    rows_n, part_len, features = tokens.shape
    flat = (rows_n * part_len, features)
    vectors = (b_query, b_value, b_out, gain_one, shift_one, b_down, gain_two, shift_two, b_up)
    outs = layer(
        mesh_shape,
        vectors,
        tokens.reshape(flat),
        cotangent.reshape(flat),
        segments,
        (w_query, w_key, w_value, w_out, w_up, w_down),
    )
    (g_query, g_key, g_value, g_out, g_up, g_down, result, grad_tokens, *vectors) = finish(
        outs[:6], *outs[8:], 6
    )
    shape = (rows_n, part_len, features)
    return (
        result.reshape(shape),
        grad_tokens.reshape(shape),
        g_query,
        vectors[8],
        g_key,
        g_value,
        vectors[9],
        g_out,
        vectors[0],
        vectors[1],
        vectors[2],
        g_up,
        vectors[10],
        g_down,
        vectors[3],
        vectors[4],
        vectors[5],
    )


def solution(mesh):
    tokens = P("rows", "pos", None)
    return jax.shard_map(
        partial(on_device, dict(mesh.shape)),
        mesh=mesh,
        in_specs=(tokens, P("rows", None), *[P()] * 15, tokens),
        out_specs=(tokens, tokens, *[P()] * 15),
        check_vma=False,
    )
```

```python
from functools import partial

import jax
import jax.numpy as jnp
from jax import lax
from jax.experimental import pallas as pl
from jax.experimental.pallas import tpu as pltpu
from jax.sharding import PartitionSpec as P

HEADS = 12
HEAD_DIM = 64
EPS = 1e-05
MASKED = -1000000000.0
SCALE = HEAD_DIM ** (-0.5)
LANES = 128
VMEM_LIMIT = 60 * 2**20
MESH = pl.DeviceIdType.MESH
LOW = jnp.bfloat16
F32 = jnp.float32


def flip(value, bit):
    return value + bit - 2 * bit * lax.rem(lax.div(value, bit), 2)


def bit_of(value, bit):
    return lax.rem(lax.div(value, bit), 2)


def axis_bits(size):
    assert size & (size - 1) == 0
    return [1 << i for i in range(size.bit_length() - 1)]


def dot(a, b):
    return jnp.dot(a, b, preferred_element_type=F32)


def dot_nt(a, b):
    return lax.dot_general(a, b, (((1,), (1,)), ((), ())), preferred_element_type=F32)


def dot_tn(a, b):
    return lax.dot_general(a, b, (((0,), (0,)), ((), ())), preferred_element_type=F32)


class Place:
    def __init__(self):
        self.row = lax.axis_index("rows")
        self.pos = lax.axis_index("pos")

    def partner(self, link):
        axis, bit = link
        if axis == "r":
            return (flip(self.row, bit), self.pos)
        return (self.row, flip(self.pos, bit))

    def side(self, link):
        axis, bit = link
        return bit_of(self.row if axis == "r" else self.pos, bit)


def remote(src, dst, sems, index, device):
    send_sem, recv_sem = sems
    return pltpu.make_async_remote_copy(
        src_ref=src,
        dst_ref=dst,
        send_sem=send_sem.at[index],
        recv_sem=recv_sem.at[index],
        device_id=device,
        device_id_type=MESH,
    )


def greet(devices):
    barrier = pltpu.get_barrier_semaphore()
    for device in devices:
        pl.semaphore_signal(barrier, inc=1, device_id=device, device_id_type=MESH)
    pl.semaphore_wait(barrier, len(devices))


def rows_at(ref, start, size):
    return ref.at[pl.ds(pl.multiple_of(start, 16), size)]


def plan_splits(rows, cols, links):
    kinds = []
    for _ in links:
        if (rows // 2) % 16 == 0:
            rows //= 2
            kinds.append("rows")
        elif (cols // 2) % LANES == 0:
            cols //= 2
            kinds.append("cols")
        else:
            kinds.append("whole")
    return kinds


def shrink(rows, cols, kind):
    return (rows // 2 if kind == "rows" else rows, cols // 2 if kind == "cols" else cols)


def landing_shape(rows, cols, links):
    total, widest = 0, 0
    for kind in plan_splits(rows, cols, links):
        rows, cols = shrink(rows, cols, kind)
        total, widest = total + rows, max(widest, cols)
    return total, widest


def add_into(dst, left, right, rows):
    step = 16 if rows % 48 else 48

    @pl.loop(0, rows // step)
    def _(i):
        at = pl.ds(pl.multiple_of(i * step, step), step)
        dst[at, :] = (left[at, :].astype(F32) + right[at, :].astype(F32)).astype(dst.dtype)


def window(ref, row0, rows, col0, cols):
    if not isinstance(row0, int):
        row0 = pl.multiple_of(row0, 16)
    if not isinstance(col0, int):
        col0 = pl.multiple_of(col0, LANES)
    return ref.at[pl.ds(row0, rows), pl.ds(col0, cols)]


class Chunk:
    def __init__(self, place, fixed, path, gather, give, out, total, landing, sems):
        send_sem, recv_sem, copy_sem = sems
        self.reduces, self.gathers, self.moment, self.gave = [], [], 0, False
        rows, cols = out.shape
        row0, col0, landed, slot = 0, 0, 0, 0
        corner = None
        row_trail, col_trail, kind_of = [], [], {}

        def held(at, rows, cols):
            return window(total, at[0] - corner[0], rows, at[1] - corner[1], cols)

        shape = out.shape
        for _, kind in fixed:
            shape = shrink(*shape, kind)
        kinds = [kind for _, kind in fixed] + plan_splits(*shape, path)
        for number, (link, kind) in enumerate(zip([link for link, _ in fixed] + path, kinds)):
            side = place.side(link)
            kind_of[link] = kind
            keep = other = (row0, col0)
            if kind == "rows":
                row_trail.append((row0, rows))
                rows //= 2
                keep, other = (row0 + side * rows, col0), (row0 + (1 - side) * rows, col0)
            elif kind == "cols":
                col_trail.append((col0, cols))
                cols //= 2
                keep, other = (row0, col0 + side * cols), (row0, col0 + (1 - side) * cols)
            row0, col0 = keep
            if number == max(len(fixed) - 1, 0):
                corner = keep
            if number < len(fixed):
                continue
            land = window(landing, landed, rows, 0, cols)
            landed += rows
            src = give if number == 0 else held(other, rows, cols)
            copy = remote(src, land, (send_sem, recv_sem), slot, place.partner(link))
            slot += 1
            self.reduces.append((copy, held(keep, rows, cols), land, kind == "whole"))
        mine = window(out, row0, rows, col0, cols)
        self.own = pltpu.make_async_copy(held((row0, col0), rows, cols), mine, copy_sem)
        for link in gather:
            kind = kind_of[link]
            if kind == "whole":
                self.gathers.append(None)
                continue
            here = window(out, row0, rows, col0, cols)
            self.gathers.append(remote(here, here, (send_sem, recv_sem), slot, place.partner(link)))
            slot += 1
            if kind == "rows":
                row0, rows = row_trail.pop()
            else:
                col0, cols = col_trail.pop()

    def done(self):
        return self.moment > len(self.reduces) + len(self.gathers)

    def advance(self):
        count, now = len(self.reduces), self.moment
        if 0 < now <= count:
            copy, keep, land, whole = self.reduces[now - 1]
            copy.wait_recv()
            if whole:
                copy.wait_send()
            add_into(keep, keep, land, land.shape[0])
        elif now > count and self.gathers[now - count - 1] is not None:
            self.gathers[now - count - 1].wait_recv()
        if now < count:
            self.reduces[now][0].start()
        elif now < count + len(self.gathers):
            if now == count:
                self.own.start()
                self.own.wait()
            if self.gathers[now - count] is not None:
                self.gathers[now - count].start()
        else:
            for index, (copy, _, _, whole) in enumerate(self.reduces):
                if not whole and not (index == 0 and self.gave):
                    copy.wait_send()
            for copy in self.gathers:
                if copy is not None:
                    copy.wait_send()
        self.moment += 1


PATHS = ("cyxzw", "cxyzw", "czwxy", "cyxzw", "czwxy", "cxyzw", "cxyzw", "cyzwx", "cxyzw")
LATE_PATHS = ("wzxyc", "wzxyc", "wyzxc")
TICKS = (
    (),
    (),
    (),
    (),
    (0, 1, 2),
    (),
    (),
    (3, 4),
    (5,),
    (0, 1, 2),
    (6,),
    (),
    (3, 4, 5, 7, 1),
    (0, 2, 8),
    (1,),
    (4, 6, 0),
    (3,),
    (1, 2),
    (5,),
    (0, 3),
    (8, 1),
    (4, 5, 7),
    (),
    (0, 6),
    (1, 2, 3),
    (),
    (4, 5, 8),
    (),
    (0, 7),
)
DRAIN = (3, 6, 9, 5, 8, 10, 3, 7, 11, 6, 9, 8, 5, 0, 10, 3, 6, 1, 11, 7, 2, 9, 4, 8, 10, 5, 6, 11, 9, 8, 1, 7, 10, 0, 2, 11, 1, 9, 4, 0, 10, 3, 7, 5, 3, 6, 5, 9, 8, 2, 11, 10, 7, 4, 6, 9, 2, 6, 9, 11, 2, 8, 10, 8, 10, 4, 7, 4, 11, 7, 11)
TAIL_STEEP = 0.24
TAIL = (
    0.09575598852910579,
    0.09547705164870551,
    0.093198719112773,
    0.06193635630868121,
    0.1216760657292812,
    -0.06984360139735674,
    0.1555215658230106,
    -0.05372215169653546,
)
TILE = 256
BAND = 48
SLOTS = 4


def gelu_and_slope(u):
    bell = jnp.exp(u * u * -0.5)
    t = 1.0 / (1.0 + TAIL_STEEP * jnp.abs(u))
    f = TAIL[-1]
    for coefficient in TAIL[-2::-1]:
        f = f * t + coefficient
    below = f * t * bell
    phi = jnp.where(u > 0, 1.0 - below, below)
    return u * phi, phi + u * (bell * 0.3989422804014327)


def fold(v):
    return jnp.sum(v.reshape(v.shape[0] // 8, 8, v.shape[1]), axis=0)


def bands(n, init, body):
    def step(i, carry):
        return body(pl.ds(pl.multiple_of(i * BAND, BAND), BAND), carry)

    return lax.fori_loop(0, n // BAND, step, init)


def layer_kernel(rows_n, paths, late_paths, links, *refs):
    vector_refs, refs = refs[:9], refs[9:]
    (x_in, cot, segments, q_in, k_in, v_in, w_out_in, w_up_in, w_down_in) = refs[:9]
    refs = refs[:2] + refs[1:]
    (q_out, k_out, v_out, o_out, up_out, down_out, qkv_kept, turned_kept) = refs[10:18]
    (result, dx_out, small_out) = refs[18:21]
    (x_all, mixed, w_out, w_up, w_down, w_own, w_mate, lse, seg_row, seg_wide) = refs[21:31]
    (d_all, chip, dx_give, dx_land, gives, total, late_total, landing, late_land) = refs[31:40]
    (small_land, send_sem, recv_sem, copy_sem, small_send, small_recv) = refs[40:46]
    (x_send, x_recv, m_send, m_recv, d_send, d_recv) = refs[46:52]
    (g_send, g_recv, dx_send, dx_recv, load_sem, own_sem, vecs) = refs[52:59]
    d_give = mixed
    place = Place()
    me = place.pos
    mate, across = flip(me, 1), flip(me, 2)
    far = flip(mate, 2)
    peers = [across, far, mate]
    core = bit_of(me, 1)
    tokens_n, features = x_in.shape
    part = tokens_n // rows_n
    length = 4 * part
    width = d_all.shape[1]
    heads = width // HEAD_DIM
    inner_n = w_up.shape[1]
    half = features // 2
    quarters = inner_n // features
    outs = [window(down_out, j * features, features, 0, features) for j in range(inner_n // features)]
    outs += [window(up_out, 0, features, j * features, features) for j in range(inner_n // features)]
    outs += [o_out]
    chunks = []
    for index, out in enumerate(outs + [q_out, k_out, v_out]):
        sems = (send_sem.at[index], recv_sem.at[index], copy_sem.at[index])
        if index < len(outs):
            path = paths[index]
            spaces = (gives.at[index % SLOTS], out, total.at[index], landing.at[index])
            chunks.append(Chunk(place, [], path, path[::-1], *spaces, sems))
        else:
            at = index - len(outs)
            fixed = [(links[0], "rows"), (links[1], "cols")]
            spaces = (None, out, late_total.at[at], late_land.at[at])
            chunks.append(Chunk(place, fixed, links[2:], late_paths[at], *spaces, sems))
    mine, other = chip.at[core], chip.at[1 - core]
    d_copies, g_copies, dx_copies = {}, [], []
    for r in range(rows_n):
        at = pl.ds(r * part, part)
        row = pl.ds(r * length, length)
        for index, peer in enumerate(peers):
            d_copies[index, r] = remote(
                d_give.at[peer, at],
                rows_at(d_all, r * length + me * part, part),
                (d_send, d_recv),
                (index, r),
                (place.row, peer),
            )
        g_copies.append(
            remote(mine.at[row], mine.at[row], (g_send, g_recv), r, (place.row, mate))
        )
        dx_copies.append(
            remote(dx_give.at[at], dx_land.at[at], (dx_send, dx_recv), r, (place.row, across))
        )
    ticks = [0]

    def tick():
        for index in TICKS[ticks[0]]:
            if chunks[index].moment > 0 and not chunks[index].done():
                chunks[index].advance()
        ticks[0] += 1

    def new_chunk(index, give, keep):
        chunk = chunks[index]
        if index >= SLOTS:
            chunks[index - SLOTS].reduces[0][0].wait_send()
            chunks[index - SLOTS].gave = True
        gives[index % SLOTS] = give().astype(LOW)
        chunk.advance()
        total[index] = keep().astype(LOW)

    to_across, to_mate, passed, own, m_copies = [], [], [], [], []

    def x_spot(r, owner):
        return rows_at(x_all, r * length + owner * part, part)

    for r in range(rows_n):
        src = x_in.at[pl.ds(r * part, part)]
        x_sems = (x_send, x_recv)
        to_across.append(remote(src, x_spot(r, me), x_sems, (0, r), (place.row, across)))
        to_mate.append(remote(src, x_spot(r, me), x_sems, (1, r), (place.row, mate)))
        spot = x_spot(r, across)
        passed.append(remote(spot, spot, x_sems, (2, r), (place.row, mate)))
        own.append(pltpu.make_async_copy(src, x_spot(r, me), own_sem.at[r]))
        own[r].start()
    weights = [
        pltpu.make_async_copy(src, dst, load_sem.at[index])
        for index, (src, dst) in enumerate(((w_out_in, w_out), (w_up_in, w_up), (w_down_in, w_down)))
    ]
    greet([place.partner(link) for link in links] + [(place.row, far)])
    for r in range(rows_n):
        to_across[r].start()
        to_mate[r].start()
    give_at = pl.ds(pl.multiple_of((1 - core) * half, LANES), half)
    keep_at = pl.ds(pl.multiple_of(core * half, LANES), half)
    small_out[...] = jnp.zeros_like(small_out)

    def attend(windows, qkv, x_turned, blend, lse_cols):
        loads = []
        for owner in range(2):
            first = lax.div(3 * (me if owner == 0 else mate), 2) * LANES
            for index, src in enumerate((q_in, k_in, v_in)):
                at = 3 * owner + index
                window_of = src.at[:, pl.ds(pl.multiple_of(first, LANES), TILE)]
                loads.append(pltpu.make_async_copy(window_of, windows.at[at], load_sem.at[3 + at]))
                loads[-1].start()
        for copy in weights:
            copy.start()
        for index, ref in enumerate(vector_refs[:8]):
            vecs[index : index + 1, :] = ref[...].astype(F32)[None]
        up_bias = vector_refs[8][...].astype(F32)[None]
        for quarter in range(quarters):
            at = slice(quarter * features, (quarter + 1) * features)
            vecs[8 + quarter : 9 + quarter, :] = up_bias[:, at]
        seg_row[...] = segments[...].astype(F32)
        for r in range(rows_n):
            row = seg_row[r : r + 1, :]
            seg_wide[r] = jnp.transpose(jnp.broadcast_to(row, (LANES, length)))
        for load in loads:
            load.wait()
        for owner, dst in enumerate((w_own, w_mate)):
            for index in range(3):
                at = slice(index * width, (index + 1) * width)
                for odd in range(2):

                    @pl.when(lax.rem(me + owner, 2) == odd)
                    def _():
                        left = odd * HEAD_DIM
                        dst[:, at] = windows[3 * owner + index, :, left : left + width]

        first = pl.ds(pl.multiple_of(lax.div(3 * me, 2) * LANES, LANES), TILE)
        odd = lax.rem(me, 2) == 1
        biases = []
        for index in range(2):
            bias = vecs[index : index + 1, first]
            biases.append(jnp.where(odd, bias[:, HEAD_DIM : HEAD_DIM + width], bias[:, :width]))
        b_own = jnp.concatenate([biases[0], jnp.zeros((1, width), F32), biases[1]], axis=1)
        is_query = lax.broadcasted_iota(jnp.int32, (1, 3 * width), 1) < width
        scale = jnp.where(is_query, SCALE, 1.0)
        kept = []
        for r in range(rows_n):
            if r == 0:
                to_across[r].wait_recv()
                passed[r].start()
            to_mate[r].wait_recv()
            own[r].wait()
            passed[r].wait_recv()
            base = r * length
            x_row = x_all[base : base + length, :]
            made = ((dot(x_row, w_own[...]) + b_own) * scale).astype(LOW)
            for index in range(3 * heads):
                left = index * HEAD_DIM
                qkv[index, base : base + length, :] = made[:, left : left + HEAD_DIM]
            row = pl.ds(base, length)
            kept.append(
                pltpu.make_async_copy(qkv.at[:, row, :], qkv_kept.at[:, row, :], own_sem.at[r])
            )
            kept[-1].start()

            for index, owner in enumerate((*peers, me)):
                here = pl.ds(pl.multiple_of(base + owner * part, 16), part)
                local = pl.ds(pl.multiple_of(owner * part, 16), part)
                seg_q = seg_wide[r, local, :]
                same = jnp.concatenate([seg_q] * (length // LANES), axis=1) == seg_row[r : r + 1, :]
                for head in range(heads):
                    query = qkv[head, here, :]
                    key = qkv[heads + head, base : base + length, :]
                    value = qkv[2 * heads + head, base : base + length, :]
                    scores = jnp.where(same, dot_nt(query, key), MASKED)
                    top = jnp.max(scores, axis=-1, keepdims=True)
                    power = jnp.exp(scores - top)
                    sums = jnp.sum(power, axis=-1, keepdims=True)
                    out = dot(power.astype(LOW), value) / sums
                    blend[here, head * HEAD_DIM : (head + 1) * HEAD_DIM] = out.astype(LOW)
                    column = r * heads + head
                    lse_cols[local, column : column + 1] = top + jnp.log(sums)
                if index < len(peers):
                    copy = remote(
                        blend.at[here],
                        mixed.at[me, pl.ds(r * part, part)],
                        (m_send, m_recv),
                        (index, r),
                        (place.row, owner),
                    )
                    copy.start()
                    m_copies.append(copy)
                else:
                    mixed[me, r * part : (r + 1) * part, :] = blend[here, :]
                if index == 1 and r + 1 < rows_n:
                    to_across[r + 1].wait_recv()
                    passed[r + 1].start()
        lse[...] = jnp.transpose(lse_cols[...])[: lse.shape[0], :]
        mine_half = pl.ds(pl.multiple_of(core * half, LANES), half)
        for r in range(rows_n):
            base = r * length
            x_turned[:, base : base + length] = jnp.transpose(x_all[base : base + length, mine_half])
        kept.append(pltpu.make_async_copy(x_turned, turned_kept, own_sem.at[rows_n]))
        kept[-1].start()
        for copy in to_across + to_mate + passed:
            copy.wait_send()
        for copy in m_copies:
            copy.wait()
        for copy in kept:
            copy.wait()

    every = rows_n * length
    pl.run_scoped(
        attend,
        pltpu.VMEM((6, features, TILE), LOW),
        pltpu.VMEM(qkv_kept.shape, LOW),
        pltpu.VMEM(turned_kept.shape, LOW),
        pltpu.VMEM((every, width), LOW),
        pltpu.VMEM((length, LANES), F32),
    )

    active = x_all

    def dense(joined, hat, spread_one, low, turned, slope, d_low, d_up):
        acc = dx_out
        for group in range(4):
            joined[:, group * width : (group + 1) * width] = mixed[group]
        gain_one, shift_one = vecs[3:4, :], vecs[4:5, :]
        gain_two, shift_two = vecs[6:7, :], vecs[7:8, :]
        weights[0].wait()
        acc[...] = dot(joined[...], w_out[...])

        def norm_one(at, carry):
            v = x_in[at, :].astype(F32) + (acc[at, :] + vecs[2:3, :])
            centred = v - jnp.mean(v, axis=-1, keepdims=True)
            over = lax.rsqrt(jnp.mean(centred * centred, axis=-1, keepdims=True) + EPS)
            v = centred * over
            hat[at, :] = v
            spread_one[at, :] = jnp.broadcast_to(over, (BAND, LANES))
            low[at, :] = (v * gain_one + shift_one).astype(LOW)
            return carry

        bands(tokens_n, 0, norm_one)
        weights[1].wait()
        for quarter in range(quarters):

            @pl.loop(0, features // TILE)
            def _(tile):
                cols = pl.ds(pl.multiple_of(tile * TILE, TILE), TILE)
                wide = pl.ds(pl.multiple_of(quarter * features + tile * TILE, TILE), TILE)
                u = dot(low[...], w_up[:, wide]) + vecs[8 + quarter : 9 + quarter, cols]
                for band in range(tokens_n // BAND):
                    at = slice(band * BAND, (band + 1) * BAND)
                    g, s = gelu_and_slope(u[at])
                    active[quarter * tokens_n + band * BAND : quarter * tokens_n + (band + 1) * BAND, cols] = g.astype(LOW)
                    slope[at, wide] = s

        weights[2].wait()

        @pl.loop(0, features // TILE)
        def _(tile):
            cols = pl.ds(pl.multiple_of(tile * TILE, TILE), TILE)
            acc[:, cols] = sum(
                dot(
                    active[quarter * tokens_n : (quarter + 1) * tokens_n, :],
                    w_down[quarter * features : (quarter + 1) * features, cols],
                )
                for quarter in range(quarters)
            )

        def norm_two(at, carry):
            d_gain, d_shift, d_bias = carry
            v = hat[at, :] * gain_one + shift_one + (acc[at, :] + vecs[5:6, :])
            centred = v - jnp.mean(v, axis=-1, keepdims=True)
            over = lax.rsqrt(jnp.mean(centred * centred, axis=-1, keepdims=True) + EPS)
            v = centred * over
            result[at, :] = (v * gain_two + shift_two).astype(LOW)
            d = cot[at, :].astype(F32)
            d_gain += fold(d * v)
            d_shift += fold(d)
            d = d * gain_two
            d = d - jnp.mean(d, axis=-1, keepdims=True) - v * jnp.mean(d * v, axis=-1, keepdims=True)
            d = d * over
            acc[at, :] = d
            d = d.astype(LOW)
            d_low[at, :] = d
            return d_gain, d_shift, d_bias + fold(d.astype(F32))

        blank = jnp.zeros((8, features), F32)
        d_gain, d_shift, d_bias = bands(tokens_n, (blank, blank, blank), norm_two)
        for index, value in ((3, d_bias), (4, d_gain), (5, d_shift)):
            small_out[index : index + 1, :] = jnp.sum(value, axis=0, keepdims=True)

        for quarter in range(quarters):

            def some_down(side):
                at = pl.ds(pl.multiple_of(side * half, LANES), half)
                return dot_tn(active[quarter * tokens_n : (quarter + 1) * tokens_n, at], d_low[...])

            new_chunk(quarter, lambda: some_down(1 - core), lambda: some_down(core))
            tick()
        turned[...] = jnp.transpose(low[...])
        for quarter in range(quarters):
            first = quarter * features

            @pl.loop(0, features // TILE)
            def _(tile):
                rows = pl.ds(pl.multiple_of(first + tile * TILE, TILE), TILE)
                cols = pl.ds(pl.multiple_of(tile * TILE, TILE), TILE)
                d = (dot_nt(d_low[...], w_down[rows, :]) * slope[:, rows]).astype(LOW)
                d_up[:, cols] = d
                small_out[12 + quarter : 13 + quarter, cols] = jnp.sum(
                    d.astype(F32), axis=0, keepdims=True
                )

            tick()
            new_chunk(
                quarters + quarter,
                lambda: dot(turned[give_at, :], d_up[...]),
                lambda: dot(turned[keep_at, :], d_up[...]),
            )
            acc[...] += dot_nt(d_up[...], w_up[:, first : first + features])
            tick()

        def norm_back(at, carry):
            d_gain, d_shift, d_bias = carry
            v, d = hat[at, :], acc[at, :]
            d_gain += fold(d * v)
            d_shift += fold(d)
            d = d * gain_one
            d = d - jnp.mean(d, axis=-1, keepdims=True) - v * jnp.mean(d * v, axis=-1, keepdims=True)
            d = d * spread_one[at, 0:1]
            acc[at, :] = d
            d = d.astype(LOW)
            d_low[at, :] = d
            return d_gain, d_shift, d_bias + fold(d.astype(F32))

        d_gain, d_shift, d_bias = bands(tokens_n, (blank, blank, blank), norm_back)
        for index, value in ((0, d_bias), (1, d_gain), (2, d_shift)):
            small_out[index : index + 1, :] = jnp.sum(value, axis=0, keepdims=True)
        for group in range(4):
            at = slice(group * width, (group + 1) * width)
            d_give[group] = dot_nt(d_low[...], w_out[at, :]).astype(LOW)
        for r in range(rows_n):
            for index in range(3):
                d_copies[index, r].start()
        new_chunk(
            2 * quarters,
            lambda: dot_tn(joined[:, give_at], d_low[...]),
            lambda: dot_tn(joined[:, keep_at], d_low[...]),
        )
        tick()

    square = (tokens_n, features)
    pl.run_scoped(
        dense,
        pltpu.VMEM(square, LOW),
        pltpu.VMEM(square, F32),
        pltpu.VMEM((tokens_n, LANES), F32),
        pltpu.VMEM(square, LOW),
        pltpu.VMEM((features, tokens_n), LOW),
        pltpu.VMEM((tokens_n, inner_n), F32),
        pltpu.VMEM(square, LOW),
        pltpu.VMEM(square, LOW),
    )
    prob = [w_up.at[pl.ds(0, length), pl.ds(head * length, length)] for head in range(heads)]
    d_score = [w_down.at[pl.ds(head * features, length), pl.ds(0, length)] for head in range(heads)]

    def attention(qkv, x_turned, d_heads):
        loads = []
        for index, (src, dst) in enumerate(((qkv_kept, qkv), (turned_kept, x_turned))):
            loads.append(pltpu.make_async_copy(src, dst, load_sem.at[index]))
            loads[-1].start()
        for load in loads:
            load.wait()
        for r in range(rows_n):
            base = r * length
            own_rows = pl.ds(pl.multiple_of(base + me * part, 16), part)
            d_all[own_rows, :] = d_give[me, r * part : (r + 1) * part, :]
            for index in range(3):
                d_copies[index, r].wait_recv()
            d_row = d_all[base : base + length, :]
            for head in range(heads):
                d_heads[head] = d_row[:, head * HEAD_DIM : (head + 1) * HEAD_DIM]

            def scores(block):
                here = pl.ds(pl.multiple_of(base + block * LANES, LANES), LANES)
                local = pl.ds(pl.multiple_of(block * LANES, LANES), LANES)
                same = seg_wide[r] == seg_row[r : r + 1, local]
                for head in range(heads):
                    query = qkv[head, here, :]
                    key = qkv[heads + head, base : base + length, :]
                    value = qkv[2 * heads + head, base : base + length, :]
                    log_total = lse[r * heads + head : r * heads + head + 1, local]
                    p = jnp.exp(jnp.where(same, dot_nt(key, query) - log_total, MASKED))
                    dp = dot_nt(value, d_heads[head, local, :])
                    inner = jnp.sum(dp * p, axis=0, keepdims=True)
                    prob[head][:, local] = p.astype(LOW)
                    d_score[head][:, local] = (p * (dp - inner)).astype(LOW)

            blocks = length // LANES
            pl.loop(0, blocks // 2)(scores)
            tick()
            pl.loop(blocks // 2, blocks)(scores)
            tick()
            for head in range(heads):
                query = qkv[head, base : base + length, :]
                key = qkv[heads + head, base : base + length, :]
                ds = d_score[head][...]
                at = slice(base, base + length)
                left = head * HEAD_DIM
                dq = dot_tn(ds, key) * SCALE
                mine[at, left : left + HEAD_DIM] = dq.astype(LOW)
                left += width
                mine[at, left : left + HEAD_DIM] = dot(ds, query).astype(LOW)
                left += width
                mine[at, left : left + HEAD_DIM] = dot(prob[head][...], d_heads[head]).astype(LOW)
            g_copies[r].start()
            tick()

        def dx_of(r, owner):
            at = pl.ds(pl.multiple_of(r * length + owner * part, 16), part)
            return dot_nt(mine[at, :], w_own[...]) + dot_nt(other[at, :], w_mate[...])

        for r in range(rows_n):
            g_copies[r].wait_recv()
            at = pl.ds(r * part, part)
            dx_give[at, :] = dx_of(r, across).astype(LOW)
            dx_copies[r].start()
            tick()
        for index in range(3):
            left = index * width
            sums = [dot(x_turned[...], chip[side, :, left : left + width]) for side in range(2)]
            late_total[index] = jnp.concatenate(sums, axis=1).astype(LOW)
            chunks[2 * quarters + 1 + index].advance()
            tick()
        token_sums = jnp.sum(mine[...].astype(F32), axis=0, keepdims=True)
        owner = lax.div(lax.broadcasted_iota(jnp.int32, (1, features), 1), width)
        for row, left in ((8, 0), (9, 2 * width)):
            spread = jnp.concatenate([token_sums[:, left : left + width]] * 4, axis=1)
            small_out[row : row + 1, :] = jnp.where(owner == me, spread, 0.0)
        for r in range(rows_n):
            at = pl.ds(r * part, part)
            dx_out[at, :] += dx_of(r, me)
        tick()

    pl.run_scoped(
        attention,
        pltpu.VMEM(qkv_kept.shape, LOW),
        pltpu.VMEM(turned_kept.shape, LOW),
        pltpu.VMEM((heads, length, HEAD_DIM), LOW),
    )
    smalls = [
        remote(
            small_out, small_land.at[number], (small_send, small_recv), number, place.partner(link)
        )
        for number, link in enumerate(links)
    ]
    gap = len(DRAIN) // (len(links) + 1)

    def small_step(number):
        if 0 < number <= len(links):
            smalls[number - 1].wait()
            small_out[...] += small_land[number - 1]
        if number < len(links):
            smalls[number].start()

    for at, index in enumerate(DRAIN):
        if at % gap == 0:
            small_step(at // gap)
        if not chunks[index].done():
            chunks[index].advance()
    for number in range((len(DRAIN) - 1) // gap + 1, len(links) + 1):
        small_step(number)
    while not all(chunk.done() for chunk in chunks):
        for chunk in chunks:
            if not chunk.done():
                chunk.advance()
    for r in range(rows_n):
        dx_copies[r].wait_recv()
        at = pl.ds(r * part, part)
        dx_out[at, :] += dx_land[at, :].astype(F32)
    for copy in dx_copies + g_copies + list(d_copies.values()):
        copy.wait_send()


def layer(mesh_shape, vectors, x_rows, cot, segments, weights):
    row_bits = [("r", bit) for bit in axis_bits(mesh_shape["rows"])]
    pos_bits = [("p", bit) for bit in axis_bits(mesh_shape["pos"])]
    name = dict(zip("cyxzw", pos_bits + row_bits))
    paths = [[name[letter] for letter in path] + row_bits[3:] for path in PATHS]
    late_paths = [row_bits[3:][::-1] + [name[letter] for letter in path] for path in LATE_PATHS]
    links = pos_bits + row_bits
    rows_n, length = segments.shape
    tokens_n, features = x_rows.shape
    inner_n = weights[4].shape[1]
    width = features // 4
    every = rows_n * length
    steps = len(links)
    half = features // 2
    early = landing_shape(features, features, links)
    late = landing_shape(half, half, row_bits)
    vmem = pl.BlockSpec(memory_space=pltpu.VMEM)
    hbm = pl.BlockSpec(memory_space=pl.ANY)
    dma = pltpu.SemaphoreType.DMA
    shape = jax.ShapeDtypeStruct
    square = shape((features, features), LOW)
    return pl.pallas_call(
        partial(layer_kernel, rows_n, paths, late_paths, links),
        out_shape=[
            square,
            square,
            square,
            square,
            shape((features, inner_n), LOW),
            shape((inner_n, features), LOW),
            shape((3 * width // HEAD_DIM, every, HEAD_DIM), LOW),
            shape((half, every), LOW),
            shape((tokens_n, features), LOW),
            shape((tokens_n, features), F32),
            shape((16, features), F32),
        ],
        in_specs=[vmem] * 12 + [hbm] * 6,
        out_specs=[hbm] * 8 + [vmem] * 3,
        scratch_shapes=[
            pltpu.VMEM((every, features), LOW),
            pltpu.VMEM((4, tokens_n, width), LOW),
            pltpu.VMEM((features, features), LOW),
            pltpu.VMEM((features, inner_n), LOW),
            pltpu.VMEM((inner_n, features), LOW),
            pltpu.VMEM((features, 3 * width), LOW),
            pltpu.VMEM((features, 3 * width), LOW),
            pltpu.VMEM((16, length), F32),
            pltpu.VMEM((rows_n, length), F32),
            pltpu.VMEM((rows_n, length, LANES), F32),
            pltpu.VMEM((every, width), LOW),
            pltpu.VMEM((2, every, 3 * width), LOW),
            pltpu.VMEM((tokens_n, features), LOW),
            pltpu.VMEM((tokens_n, features), LOW),
            pltpu.VMEM((SLOTS, half, features), LOW),
            pltpu.VMEM((9, half, features), LOW),
            pltpu.VMEM((3, half, half), LOW),
            pltpu.VMEM((9, *early), LOW),
            pltpu.VMEM((3, *late), LOW),
            pltpu.VMEM((steps, 16, features), F32),
            dma((12, 2 * steps)),
            dma((12, 2 * steps)),
            dma((12,)),
            dma((steps,)),
            dma((steps,)),
            *[dma((3, rows_n))] * 6,
            *[dma((rows_n,))] * 4,
            dma((9,)),
            dma((rows_n + 1,)),
            pltpu.VMEM((16, features), F32),
        ],
        compiler_params=pltpu.CompilerParams(
            collective_id=0, has_side_effects=True, vmem_limit_bytes=VMEM_LIMIT
        ),
        cost_estimate=pl.CostEstimate(
            flops=4 * 10**10, bytes_accessed=8 * 10**7, transcendentals=8 * 10**6
        ),
        name="layer",
    )(*vectors, x_rows, cot, segments, *weights)


def finish_kernel(moved, *refs):
    sources = refs[: moved + 1]
    outs = refs[moved + 1 :]
    for src, dst in zip(sources[:moved], outs[:moved]):
        dst[...] = src[...].astype(dst.dtype)
    small = sources[moved]
    for index, dst in enumerate(outs[moved:-1]):
        dst[...] = small[index, :]
    outs[-1][...] = jnp.concatenate([small[index, :] for index in range(12, 16)])


def finish(blocks, result, grad_tokens, small, steps):
    arrays = [*blocks, result, grad_tokens]
    kinds = [F32] * len(blocks) + [result.dtype, grad_tokens.dtype]
    specs = [pl.BlockSpec((a.shape[0] // steps, a.shape[1]), lambda i: (i, 0)) for a in arrays]
    features = small.shape[1]
    vectors = [features] * 10 + [4 * features]
    shape = jax.ShapeDtypeStruct
    return pl.pallas_call(
        partial(finish_kernel, len(arrays)),
        grid=(steps,),
        out_shape=[shape(a.shape, kind) for a, kind in zip(arrays, kinds)]
        + [shape((size,), F32) for size in vectors],
        in_specs=[*specs, pl.BlockSpec(small.shape, lambda i: (0, 0))],
        out_specs=[*specs, *[pl.BlockSpec((size,), lambda i: (0,)) for size in vectors]],
        compiler_params=pltpu.CompilerParams(vmem_limit_bytes=VMEM_LIMIT),
        cost_estimate=pl.CostEstimate(
            flops=0, bytes_accessed=6 * sum(a.size for a in arrays), transcendentals=0
        ),
        name="finish",
    )(*arrays, small)


def on_device(
    mesh_shape,
    tokens,
    segments,
    w_query,
    b_query,
    w_key,
    w_value,
    b_value,
    w_out,
    b_out,
    gain_one,
    shift_one,
    w_up,
    b_up,
    w_down,
    b_down,
    gain_two,
    shift_two,
    cotangent,
):
    rows_n, part_len, features = tokens.shape
    flat = (rows_n * part_len, features)
    vectors = (b_query, b_value, b_out, gain_one, shift_one, b_down, gain_two, shift_two, b_up)
    outs = layer(
        mesh_shape,
        vectors,
        tokens.reshape(flat),
        cotangent.reshape(flat),
        segments,
        (w_query, w_key, w_value, w_out, w_up, w_down),
    )
    (g_query, g_key, g_value, g_out, g_up, g_down, result, grad_tokens, *vectors) = finish(
        outs[:6], *outs[8:], 3
    )
    shape = (rows_n, part_len, features)
    return (
        result.reshape(shape),
        grad_tokens.reshape(shape),
        g_query,
        vectors[8],
        g_key,
        g_value,
        vectors[9],
        g_out,
        vectors[0],
        vectors[1],
        vectors[2],
        g_up,
        vectors[10],
        g_down,
        vectors[3],
        vectors[4],
        vectors[5],
    )


def solution(mesh):
    tokens = P("rows", "pos", None)
    return jax.shard_map(
        partial(on_device, dict(mesh.shape)),
        mesh=mesh,
        in_specs=(tokens, P("rows", None), *[P()] * 15, tokens),
        out_specs=(tokens, tokens, *[P()] * 15),
        check_vma=False,
    )
```

```python
from functools import partial

import jax
import jax.numpy as jnp
from jax import lax
from jax.experimental import pallas as pl
from jax.experimental.pallas import tpu as pltpu
from jax.sharding import PartitionSpec as P

HEADS = 12
HEAD_DIM = 64
EPS = 1e-05
MASKED = -1000000000.0
SCALE = HEAD_DIM ** (-0.5)
LANES = 128
VMEM_LIMIT = 60 * 2**20
MESH = pl.DeviceIdType.MESH
LOW = jnp.bfloat16
F32 = jnp.float32


def flip(value, bit):
    return value + bit - 2 * bit * lax.rem(lax.div(value, bit), 2)


def bit_of(value, bit):
    return lax.rem(lax.div(value, bit), 2)


def axis_bits(size):
    assert size & (size - 1) == 0
    return [1 << i for i in range(size.bit_length() - 1)]


def dot(a, b):
    return jnp.dot(a, b, preferred_element_type=F32)


def dot_nt(a, b):
    return lax.dot_general(a, b, (((1,), (1,)), ((), ())), preferred_element_type=F32)


def dot_tn(a, b):
    return lax.dot_general(a, b, (((0,), (0,)), ((), ())), preferred_element_type=F32)


class Place:
    def __init__(self):
        self.row = lax.axis_index("rows")
        self.pos = lax.axis_index("pos")

    def partner(self, link):
        axis, bit = link
        if axis == "r":
            return (flip(self.row, bit), self.pos)
        return (self.row, flip(self.pos, bit))

    def side(self, link):
        axis, bit = link
        return bit_of(self.row if axis == "r" else self.pos, bit)


def remote(src, dst, sems, index, device):
    send_sem, recv_sem = sems
    return pltpu.make_async_remote_copy(
        src_ref=src,
        dst_ref=dst,
        send_sem=send_sem.at[index],
        recv_sem=recv_sem.at[index],
        device_id=device,
        device_id_type=MESH,
    )


def greet(devices):
    barrier = pltpu.get_barrier_semaphore()
    for device in devices:
        pl.semaphore_signal(barrier, inc=1, device_id=device, device_id_type=MESH)
    pl.semaphore_wait(barrier, len(devices))


def rows_at(ref, start, size):
    return ref.at[pl.ds(pl.multiple_of(start, 16), size)]


def plan_splits(rows, cols, links):
    kinds = []
    for _ in links:
        if (rows // 2) % 16 == 0:
            rows //= 2
            kinds.append("rows")
        elif (cols // 2) % LANES == 0:
            cols //= 2
            kinds.append("cols")
        else:
            kinds.append("whole")
    return kinds


def shrink(rows, cols, kind):
    return (rows // 2 if kind == "rows" else rows, cols // 2 if kind == "cols" else cols)


def landing_shape(rows, cols, links):
    total, widest = 0, 0
    for kind in plan_splits(rows, cols, links):
        rows, cols = shrink(rows, cols, kind)
        total, widest = total + rows, max(widest, cols)
    return total, widest


def add_into(dst, left, right, rows):
    step = 16 if rows % 48 else 48

    @pl.loop(0, rows // step)
    def _(i):
        at = pl.ds(pl.multiple_of(i * step, step), step)
        dst[at, :] = (left[at, :].astype(F32) + right[at, :].astype(F32)).astype(dst.dtype)


def window(ref, row0, rows, col0, cols):
    if not isinstance(row0, int):
        row0 = pl.multiple_of(row0, 16)
    if not isinstance(col0, int):
        col0 = pl.multiple_of(col0, LANES)
    return ref.at[pl.ds(row0, rows), pl.ds(col0, cols)]


class Chunk:
    def __init__(self, place, fixed, path, gather, give, out, total, landing, sems):
        send_sem, recv_sem, copy_sem = sems
        self.reduces, self.gathers, self.moment, self.gave = [], [], 0, False
        rows, cols = out.shape
        row0, col0, landed, slot = 0, 0, 0, 0
        corner = None
        row_trail, col_trail, kind_of = [], [], {}

        def held(at, rows, cols):
            return window(total, at[0] - corner[0], rows, at[1] - corner[1], cols)

        shape = out.shape
        for _, kind in fixed:
            shape = shrink(*shape, kind)
        kinds = [kind for _, kind in fixed] + plan_splits(*shape, path)
        for number, (link, kind) in enumerate(zip([link for link, _ in fixed] + path, kinds)):
            side = place.side(link)
            kind_of[link] = kind
            keep = other = (row0, col0)
            if kind == "rows":
                row_trail.append((row0, rows))
                rows //= 2
                keep, other = (row0 + side * rows, col0), (row0 + (1 - side) * rows, col0)
            elif kind == "cols":
                col_trail.append((col0, cols))
                cols //= 2
                keep, other = (row0, col0 + side * cols), (row0, col0 + (1 - side) * cols)
            row0, col0 = keep
            if number == max(len(fixed) - 1, 0):
                corner = keep
            if number < len(fixed):
                continue
            land = window(landing, landed, rows, 0, cols)
            landed += rows
            src = give if number == 0 else held(other, rows, cols)
            copy = remote(src, land, (send_sem, recv_sem), slot, place.partner(link))
            slot += 1
            self.reduces.append((copy, held(keep, rows, cols), land, kind == "whole"))
        mine = window(out, row0, rows, col0, cols)
        self.own = pltpu.make_async_copy(held((row0, col0), rows, cols), mine, copy_sem)
        src = held((row0, col0), rows, cols)
        for link in gather:
            kind = kind_of[link]
            if kind == "whole":
                self.gathers.append(None)
                continue
            here = window(out, row0, rows, col0, cols)
            src = here if src is None else src
            self.gathers.append(remote(src, here, (send_sem, recv_sem), slot, place.partner(link)))
            src = None
            slot += 1
            if kind == "rows":
                row0, rows = row_trail.pop()
            else:
                col0, cols = col_trail.pop()

    def done(self):
        return self.moment > len(self.reduces) + len(self.gathers)

    def advance(self):
        count, now = len(self.reduces), self.moment
        if 0 < now <= count:
            copy, keep, land, whole = self.reduces[now - 1]
            copy.wait_recv()
            if whole:
                copy.wait_send()
            add_into(keep, keep, land, land.shape[0])
        elif now > count:
            if now == count + 1:
                self.own.wait()
            if self.gathers[now - count - 1] is not None:
                self.gathers[now - count - 1].wait_recv()
        if now < count:
            self.reduces[now][0].start()
        elif now < count + len(self.gathers):
            if now == count:
                self.own.start()
            if self.gathers[now - count] is not None:
                self.gathers[now - count].start()
        else:
            for index, (copy, _, _, whole) in enumerate(self.reduces):
                if not whole and not (index == 0 and self.gave):
                    copy.wait_send()
            for copy in self.gathers:
                if copy is not None:
                    copy.wait_send()
        self.moment += 1


PATHS = ("cyxzw", "cxyzw", "czwxy", "cyxzw", "czwxy", "cxyzw", "cxyzw", "cyzwx", "cxyzw")
LATE_PATHS = ("wzxyc", "wzxyc", "wyzxc")
TICKS = (
    (),
    (),
    (),
    (),
    (0, 1, 2),
    (),
    (),
    (3, 4),
    (5,),
    (0, 1, 2),
    (6,),
    (),
    (3, 4, 5, 7, 1),
    (0, 2, 8),
    (1,),
    (4, 6, 0),
    (3,),
    (1, 2),
    (5,),
    (0, 3),
    (8, 1),
    (4, 5, 7),
    (),
    (0, 6),
    (1, 2, 3),
    (),
    (4, 5, 8),
    (),
    (0, 7),
)
DRAIN = (3, 6, 9, 5, 8, 10, 3, 7, 11, 6, 9, 8, 5, 0, 10, 3, 6, 1, 11, 7, 2, 9, 4, 8, 10, 5, 6, 11, 9, 8, 1, 7, 10, 0, 2, 11, 1, 9, 4, 0, 10, 3, 7, 5, 3, 6, 5, 9, 8, 2, 11, 10, 7, 4, 6, 9, 2, 6, 9, 11, 2, 8, 10, 8, 10, 4, 7, 4, 11, 7, 11)
TAIL_STEEP = 0.24
TAIL = (
    0.09575598852910579,
    0.09547705164870551,
    0.093198719112773,
    0.06193635630868121,
    0.1216760657292812,
    -0.06984360139735674,
    0.1555215658230106,
    -0.05372215169653546,
)
TILE = 256
WIDE = 768
BAND = 48
SLOTS = 4


def gelu_and_slope(u):
    bell = jnp.exp(u * u * -0.5)
    t = 1.0 / (1.0 + TAIL_STEEP * jnp.abs(u))
    f = TAIL[-1]
    for coefficient in TAIL[-2::-1]:
        f = f * t + coefficient
    below = f * t * bell
    phi = jnp.where(u > 0, 1.0 - below, below)
    return u * phi, phi + u * (bell * 0.3989422804014327)


def fold(v):
    return jnp.sum(v.reshape(v.shape[0] // 8, 8, v.shape[1]), axis=0)


def bands(n, init, body):
    def step(i, carry):
        return body(pl.ds(pl.multiple_of(i * BAND, BAND), BAND), carry)

    return lax.fori_loop(0, n // BAND, step, init)


def layer_kernel(rows_n, paths, late_paths, links, *refs):
    vector_refs, refs = refs[:9], refs[9:]
    (x_in, cot, segments, q_in, k_in, v_in, w_out_in, w_up_in, w_down_in) = refs[:9]
    refs = refs[:2] + refs[1:]
    (q_out, k_out, v_out, o_out, up_out, down_out, qkv_kept, turned_kept) = refs[10:18]
    (result, dx_out, small_out) = refs[18:21]
    (x_all, mixed, w_out, w_up, w_down, w_own, w_mate, lse, seg_row, seg_wide) = refs[21:31]
    (d_all, chip, dx_give, dx_land, gives, total, late_total, landing, late_land) = refs[31:40]
    (small_land, send_sem, recv_sem, copy_sem, small_send, small_recv) = refs[40:46]
    (x_send, x_recv, m_send, m_recv, d_send, d_recv) = refs[46:52]
    (g_send, g_recv, dx_send, dx_recv, load_sem, own_sem, vecs) = refs[52:59]
    d_give = mixed
    place = Place()
    me = place.pos
    mate, across = flip(me, 1), flip(me, 2)
    far = flip(mate, 2)
    peers = [across, far, mate]
    core = bit_of(me, 1)
    tokens_n, features = x_in.shape
    part = tokens_n // rows_n
    length = 4 * part
    width = d_all.shape[1]
    heads = width // HEAD_DIM
    inner_n = w_up.shape[1]
    half = features // 2
    quarters = inner_n // features
    outs = [window(down_out, j * features, features, 0, features) for j in range(inner_n // features)]
    outs += [window(up_out, 0, features, j * features, features) for j in range(inner_n // features)]
    outs += [o_out]
    chunks = []
    for index, out in enumerate(outs + [q_out, k_out, v_out]):
        sems = (send_sem.at[index], recv_sem.at[index], copy_sem.at[index])
        if index < len(outs):
            path = paths[index]
            spaces = (gives.at[index % SLOTS], out, total.at[index], landing.at[index])
            chunks.append(Chunk(place, [], path, path[::-1], *spaces, sems))
        else:
            at = index - len(outs)
            fixed = [(links[0], "rows"), (links[1], "cols")]
            spaces = (None, out, late_total.at[at], late_land.at[at])
            chunks.append(Chunk(place, fixed, links[2:], late_paths[at], *spaces, sems))
    mine, other = chip.at[core], chip.at[1 - core]
    d_copies, g_copies, dx_copies = {}, [], []
    for r in range(rows_n):
        at = pl.ds(r * part, part)
        row = pl.ds(r * length, length)
        for index, peer in enumerate(peers):
            d_copies[index, r] = remote(
                d_give.at[peer, at],
                rows_at(d_all, r * length + me * part, part),
                (d_send, d_recv),
                (index, r),
                (place.row, peer),
            )
        g_copies.append(
            remote(mine.at[row], mine.at[row], (g_send, g_recv), r, (place.row, mate))
        )
        dx_copies.append(
            remote(dx_give.at[at], dx_land.at[at], (dx_send, dx_recv), r, (place.row, across))
        )
    ticks = [0]

    def tick():
        for index in TICKS[ticks[0]]:
            if chunks[index].moment > 0 and not chunks[index].done():
                chunks[index].advance()
        ticks[0] += 1

    def new_chunk(index, give, keep):
        chunk = chunks[index]
        if index >= SLOTS:
            chunks[index - SLOTS].reduces[0][0].wait_send()
            chunks[index - SLOTS].gave = True
        gives[index % SLOTS] = give().astype(LOW)
        chunk.advance()
        total[index] = keep().astype(LOW)

    to_across, to_mate, passed, own, m_copies = [], [], [], [], []

    def x_spot(r, owner):
        return rows_at(x_all, r * length + owner * part, part)

    for r in range(rows_n):
        src = x_in.at[pl.ds(r * part, part)]
        x_sems = (x_send, x_recv)
        to_across.append(remote(src, x_spot(r, me), x_sems, (0, r), (place.row, across)))
        to_mate.append(remote(src, x_spot(r, me), x_sems, (1, r), (place.row, mate)))
        spot = x_spot(r, across)
        passed.append(remote(spot, spot, x_sems, (2, r), (place.row, mate)))
        own.append(pltpu.make_async_copy(src, x_spot(r, me), own_sem.at[r]))
        own[r].start()
    weights = [
        pltpu.make_async_copy(src, dst, load_sem.at[index])
        for index, (src, dst) in enumerate(((w_out_in, w_out), (w_up_in, w_up), (w_down_in, w_down)))
    ]
    greet([place.partner(link) for link in links] + [(place.row, far)])
    for r in range(rows_n):
        to_across[r].start()
        to_mate[r].start()
    give_at = pl.ds(pl.multiple_of((1 - core) * half, LANES), half)
    keep_at = pl.ds(pl.multiple_of(core * half, LANES), half)
    small_out[...] = jnp.zeros_like(small_out)

    def attend(windows, qkv, x_turned, blend, lse_cols):
        loads = []
        for owner in range(2):
            first = lax.div(3 * (me if owner == 0 else mate), 2) * LANES
            for index, src in enumerate((q_in, k_in, v_in)):
                at = 3 * owner + index
                window_of = src.at[:, pl.ds(pl.multiple_of(first, LANES), TILE)]
                loads.append(pltpu.make_async_copy(window_of, windows.at[at], load_sem.at[3 + at]))
                loads[-1].start()
        for copy in weights:
            copy.start()
        for index, ref in enumerate(vector_refs[:8]):
            vecs[index : index + 1, :] = ref[...].astype(F32)[None]
        up_bias = vector_refs[8][...].astype(F32)[None]
        for quarter in range(quarters):
            at = slice(quarter * features, (quarter + 1) * features)
            vecs[8 + quarter : 9 + quarter, :] = up_bias[:, at]
        seg_row[...] = segments[...].astype(F32)
        for r in range(rows_n):
            row = seg_row[r : r + 1, :]
            seg_wide[r] = jnp.transpose(jnp.broadcast_to(row, (LANES, length)))
        for load in loads:
            load.wait()
        for owner, dst in enumerate((w_own, w_mate)):
            for index in range(3):
                at = slice(index * width, (index + 1) * width)
                for odd in range(2):

                    @pl.when(lax.rem(me + owner, 2) == odd)
                    def _():
                        left = odd * HEAD_DIM
                        dst[:, at] = windows[3 * owner + index, :, left : left + width]

        first = pl.ds(pl.multiple_of(lax.div(3 * me, 2) * LANES, LANES), TILE)
        odd = lax.rem(me, 2) == 1
        biases = []
        for index in range(2):
            bias = vecs[index : index + 1, first]
            biases.append(jnp.where(odd, bias[:, HEAD_DIM : HEAD_DIM + width], bias[:, :width]))
        b_own = jnp.concatenate([biases[0], jnp.zeros((1, width), F32), biases[1]], axis=1)
        is_query = lax.broadcasted_iota(jnp.int32, (1, 3 * width), 1) < width
        scale = jnp.where(is_query, SCALE, 1.0)
        kept = []
        for r in range(rows_n):
            if r == 0:
                to_across[r].wait_recv()
                passed[r].start()
            to_mate[r].wait_recv()
            own[r].wait()
            passed[r].wait_recv()
            base = r * length
            x_row = x_all[base : base + length, :]
            made = ((dot(x_row, w_own[...]) + b_own) * scale).astype(LOW)
            for index in range(3 * heads):
                left = index * HEAD_DIM
                qkv[index, base : base + length, :] = made[:, left : left + HEAD_DIM]
            row = pl.ds(base, length)
            kept.append(
                pltpu.make_async_copy(qkv.at[:, row, :], qkv_kept.at[:, row, :], own_sem.at[r])
            )
            kept[-1].start()

            for index, owner in enumerate((*peers, me)):
                here = pl.ds(pl.multiple_of(base + owner * part, 16), part)
                local = pl.ds(pl.multiple_of(owner * part, 16), part)
                seg_q = seg_wide[r, local, :]
                same = jnp.concatenate([seg_q] * (length // LANES), axis=1) == seg_row[r : r + 1, :]
                for head in range(heads):
                    query = qkv[head, here, :]
                    key = qkv[heads + head, base : base + length, :]
                    value = qkv[2 * heads + head, base : base + length, :]
                    scores = jnp.where(same, dot_nt(query, key), MASKED)
                    top = jnp.max(scores, axis=-1, keepdims=True)
                    power = jnp.exp(scores - top)
                    sums = jnp.sum(power, axis=-1, keepdims=True)
                    out = dot(power.astype(LOW), value) / sums
                    blend[here, head * HEAD_DIM : (head + 1) * HEAD_DIM] = out.astype(LOW)
                    column = r * heads + head
                    lse_cols[local, column : column + 1] = top + jnp.log(sums)
                if index < len(peers):
                    copy = remote(
                        blend.at[here],
                        mixed.at[me, pl.ds(r * part, part)],
                        (m_send, m_recv),
                        (index, r),
                        (place.row, owner),
                    )
                    copy.start()
                    m_copies.append(copy)
                else:
                    mixed[me, r * part : (r + 1) * part, :] = blend[here, :]
                if index == 1 and r + 1 < rows_n:
                    to_across[r + 1].wait_recv()
                    passed[r + 1].start()
        lse[...] = jnp.transpose(lse_cols[...])[: lse.shape[0], :]
        mine_half = pl.ds(pl.multiple_of(core * half, LANES), half)
        for r in range(rows_n):
            base = r * length
            x_turned[:, base : base + length] = jnp.transpose(x_all[base : base + length, mine_half])
        kept.append(pltpu.make_async_copy(x_turned, turned_kept, own_sem.at[rows_n]))
        kept[-1].start()
        for copy in to_across + to_mate + passed:
            copy.wait_send()
        for copy in m_copies:
            copy.wait()
        for copy in kept:
            copy.wait()

    every = rows_n * length
    pl.run_scoped(
        attend,
        pltpu.VMEM((6, features, TILE), LOW),
        pltpu.VMEM(qkv_kept.shape, LOW),
        pltpu.VMEM(turned_kept.shape, LOW),
        pltpu.VMEM((every, width), LOW),
        pltpu.VMEM((length, LANES), F32),
    )

    active = x_all

    def dense(joined, hat, spread_one, low, turned, slope, d_low):
        acc = dx_out
        for group in range(4):
            joined[:, group * width : (group + 1) * width] = mixed[group]
        gain_one, shift_one = vecs[3:4, :], vecs[4:5, :]
        gain_two, shift_two = vecs[6:7, :], vecs[7:8, :]
        weights[0].wait()
        acc[...] = dot(joined[...], w_out[...])

        def norm_one(at, carry):
            v = x_in[at, :].astype(F32) + (acc[at, :] + vecs[2:3, :])
            centred = v - jnp.mean(v, axis=-1, keepdims=True)
            over = lax.rsqrt(jnp.mean(centred * centred, axis=-1, keepdims=True) + EPS)
            v = centred * over
            hat[at, :] = v
            spread_one[at, :] = jnp.broadcast_to(over, (BAND, LANES))
            low[at, :] = (v * gain_one + shift_one).astype(LOW)
            return carry

        bands(tokens_n, 0, norm_one)
        weights[1].wait()
        for quarter in range(quarters):

            @pl.loop(0, features // WIDE)
            def _(tile):
                cols = pl.ds(pl.multiple_of(tile * WIDE, WIDE), WIDE)
                wide = pl.ds(pl.multiple_of(quarter * features + tile * WIDE, WIDE), WIDE)
                u = dot(low[...], w_up[:, wide]) + vecs[8 + quarter : 9 + quarter, cols]
                for band in range(tokens_n // BAND):
                    at = slice(band * BAND, (band + 1) * BAND)
                    g, s = gelu_and_slope(u[at])
                    active[quarter * tokens_n + band * BAND : quarter * tokens_n + (band + 1) * BAND, cols] = g.astype(LOW)
                    slope[at, wide] = s

        weights[2].wait()

        @pl.loop(0, features // WIDE)
        def _(tile):
            cols = pl.ds(pl.multiple_of(tile * WIDE, WIDE), WIDE)
            acc[:, cols] = sum(
                dot(
                    active[quarter * tokens_n : (quarter + 1) * tokens_n, :],
                    w_down[quarter * features : (quarter + 1) * features, cols],
                )
                for quarter in range(quarters)
            )

        def norm_two(at, carry):
            d_gain, d_shift, d_bias = carry
            v = hat[at, :] * gain_one + shift_one + (acc[at, :] + vecs[5:6, :])
            centred = v - jnp.mean(v, axis=-1, keepdims=True)
            over = lax.rsqrt(jnp.mean(centred * centred, axis=-1, keepdims=True) + EPS)
            v = centred * over
            result[at, :] = (v * gain_two + shift_two).astype(LOW)
            d = cot[at, :].astype(F32)
            d_gain += fold(d * v)
            d_shift += fold(d)
            d = d * gain_two
            d = d - jnp.mean(d, axis=-1, keepdims=True) - v * jnp.mean(d * v, axis=-1, keepdims=True)
            d = d * over
            acc[at, :] = d
            d = d.astype(LOW)
            d_low[at, :] = d
            return d_gain, d_shift, d_bias + fold(d.astype(F32))

        blank = jnp.zeros((8, features), F32)
        d_gain, d_shift, d_bias = bands(tokens_n, (blank, blank, blank), norm_two)
        for index, value in ((3, d_bias), (4, d_gain), (5, d_shift)):
            small_out[index : index + 1, :] = jnp.sum(value, axis=0, keepdims=True)

        for quarter in range(quarters):

            def some_down(side):
                at = pl.ds(pl.multiple_of(side * half, LANES), half)
                return dot_tn(active[quarter * tokens_n : (quarter + 1) * tokens_n, at], d_low[...])

            new_chunk(quarter, lambda: some_down(1 - core), lambda: some_down(core))
            tick()
        turned[...] = jnp.transpose(low[...])
        for quarter in range(quarters):
            first = quarter * features
            d_up = active.at[pl.ds(quarter * tokens_n, tokens_n)]

            @pl.loop(0, features // WIDE)
            def _(tile):
                rows = pl.ds(pl.multiple_of(first + tile * WIDE, WIDE), WIDE)
                cols = pl.ds(pl.multiple_of(tile * WIDE, WIDE), WIDE)
                d = (dot_nt(d_low[...], w_down[rows, :]) * slope[:, rows]).astype(LOW)
                d_up[:, cols] = d
                small_out[12 + quarter : 13 + quarter, cols] = jnp.sum(
                    d.astype(F32), axis=0, keepdims=True
                )

            tick()
            new_chunk(
                quarters + quarter,
                lambda: dot(turned[give_at, :], d_up[...]),
                lambda: dot(turned[keep_at, :], d_up[...]),
            )
            acc[...] += dot_nt(d_up[...], w_up[:, first : first + features])
            tick()

        def norm_back(at, carry):
            d_gain, d_shift, d_bias = carry
            v, d = hat[at, :], acc[at, :]
            d_gain += fold(d * v)
            d_shift += fold(d)
            d = d * gain_one
            d = d - jnp.mean(d, axis=-1, keepdims=True) - v * jnp.mean(d * v, axis=-1, keepdims=True)
            d = d * spread_one[at, 0:1]
            acc[at, :] = d
            d = d.astype(LOW)
            d_low[at, :] = d
            return d_gain, d_shift, d_bias + fold(d.astype(F32))

        d_gain, d_shift, d_bias = bands(tokens_n, (blank, blank, blank), norm_back)
        for index, value in ((0, d_bias), (1, d_gain), (2, d_shift)):
            small_out[index : index + 1, :] = jnp.sum(value, axis=0, keepdims=True)
        for group in range(4):
            at = slice(group * width, (group + 1) * width)
            d_give[group] = dot_nt(d_low[...], w_out[at, :]).astype(LOW)
        for r in range(rows_n):
            for index in range(3):
                d_copies[index, r].start()
        new_chunk(
            2 * quarters,
            lambda: dot_tn(joined[:, give_at], d_low[...]),
            lambda: dot_tn(joined[:, keep_at], d_low[...]),
        )
        tick()

    square = (tokens_n, features)
    pl.run_scoped(
        dense,
        pltpu.VMEM(square, LOW),
        pltpu.VMEM(square, F32),
        pltpu.VMEM((tokens_n, LANES), F32),
        pltpu.VMEM(square, LOW),
        pltpu.VMEM((features, tokens_n), LOW),
        pltpu.VMEM((tokens_n, inner_n), F32),
        pltpu.VMEM(square, LOW),
    )
    prob = [w_up.at[pl.ds(0, length), pl.ds(head * length, length)] for head in range(heads)]
    d_score = [w_down.at[pl.ds(head * features, length), pl.ds(0, length)] for head in range(heads)]

    def attention(qkv, x_turned, d_heads):
        loads = []
        for index, (src, dst) in enumerate(((qkv_kept, qkv), (turned_kept, x_turned))):
            loads.append(pltpu.make_async_copy(src, dst, load_sem.at[index]))
            loads[-1].start()
        for load in loads:
            load.wait()
        for r in range(rows_n):
            base = r * length
            own_rows = pl.ds(pl.multiple_of(base + me * part, 16), part)
            d_all[own_rows, :] = d_give[me, r * part : (r + 1) * part, :]
            for index in range(3):
                d_copies[index, r].wait_recv()
            d_row = d_all[base : base + length, :]
            for head in range(heads):
                d_heads[head] = d_row[:, head * HEAD_DIM : (head + 1) * HEAD_DIM]

            def scores(block):
                here = pl.ds(pl.multiple_of(base + block * LANES, LANES), LANES)
                local = pl.ds(pl.multiple_of(block * LANES, LANES), LANES)
                same = seg_wide[r] == seg_row[r : r + 1, local]
                for head in range(heads):
                    query = qkv[head, here, :]
                    key = qkv[heads + head, base : base + length, :]
                    value = qkv[2 * heads + head, base : base + length, :]
                    log_total = lse[r * heads + head : r * heads + head + 1, local]
                    p = jnp.exp(jnp.where(same, dot_nt(key, query) - log_total, MASKED))
                    dp = dot_nt(value, d_heads[head, local, :])
                    inner = jnp.sum(dp * p, axis=0, keepdims=True)
                    prob[head][:, local] = p.astype(LOW)
                    d_score[head][:, local] = (p * (dp - inner)).astype(LOW)

            blocks = length // LANES
            pl.loop(0, blocks // 2)(scores)
            tick()
            pl.loop(blocks // 2, blocks)(scores)
            tick()
            for head in range(heads):
                query = qkv[head, base : base + length, :]
                key = qkv[heads + head, base : base + length, :]
                ds = d_score[head][...]
                at = slice(base, base + length)
                left = head * HEAD_DIM
                dq = dot_tn(ds, key) * SCALE
                mine[at, left : left + HEAD_DIM] = dq.astype(LOW)
                left += width
                mine[at, left : left + HEAD_DIM] = dot(ds, query).astype(LOW)
                left += width
                mine[at, left : left + HEAD_DIM] = dot(prob[head][...], d_heads[head]).astype(LOW)
            g_copies[r].start()
            tick()

        def dx_of(r, owner):
            at = pl.ds(pl.multiple_of(r * length + owner * part, 16), part)
            return dot_nt(mine[at, :], w_own[...]) + dot_nt(other[at, :], w_mate[...])

        for r in range(rows_n):
            g_copies[r].wait_recv()
            at = pl.ds(r * part, part)
            dx_give[at, :] = dx_of(r, across).astype(LOW)
            dx_copies[r].start()
            tick()
        for index in range(3):
            left = index * width
            sums = [dot(x_turned[...], chip[side, :, left : left + width]) for side in range(2)]
            late_total[index] = jnp.concatenate(sums, axis=1).astype(LOW)
            chunks[2 * quarters + 1 + index].advance()
            tick()
        token_sums = jnp.sum(mine[...].astype(F32), axis=0, keepdims=True)
        owner = lax.div(lax.broadcasted_iota(jnp.int32, (1, features), 1), width)
        for row, left in ((8, 0), (9, 2 * width)):
            spread = jnp.concatenate([token_sums[:, left : left + width]] * 4, axis=1)
            small_out[row : row + 1, :] = jnp.where(owner == me, spread, 0.0)
        for r in range(rows_n):
            at = pl.ds(r * part, part)
            dx_out[at, :] += dx_of(r, me)
        tick()

    pl.run_scoped(
        attention,
        pltpu.VMEM(qkv_kept.shape, LOW),
        pltpu.VMEM(turned_kept.shape, LOW),
        pltpu.VMEM((heads, length, HEAD_DIM), LOW),
    )
    smalls = [
        remote(
            small_out, small_land.at[number], (small_send, small_recv), number, place.partner(link)
        )
        for number, link in enumerate(links)
    ]
    gap = len(DRAIN) // (len(links) + 1)

    def small_step(number):
        if 0 < number <= len(links):
            smalls[number - 1].wait()
            small_out[...] += small_land[number - 1]
        if number < len(links):
            smalls[number].start()

    for at, index in enumerate(DRAIN):
        if at % gap == 0:
            small_step(at // gap)
        if not chunks[index].done():
            chunks[index].advance()
    for number in range((len(DRAIN) - 1) // gap + 1, len(links) + 1):
        small_step(number)
    while not all(chunk.done() for chunk in chunks):
        for chunk in chunks:
            if not chunk.done():
                chunk.advance()
    for r in range(rows_n):
        dx_copies[r].wait_recv()
        at = pl.ds(r * part, part)
        dx_out[at, :] += dx_land[at, :].astype(F32)
    for copy in dx_copies + g_copies + list(d_copies.values()):
        copy.wait_send()


def layer(mesh_shape, vectors, x_rows, cot, segments, weights):
    row_bits = [("r", bit) for bit in axis_bits(mesh_shape["rows"])]
    pos_bits = [("p", bit) for bit in axis_bits(mesh_shape["pos"])]
    name = dict(zip("cyxzw", pos_bits + row_bits))
    paths = [[name[letter] for letter in path] + row_bits[3:] for path in PATHS]
    late_paths = [row_bits[3:][::-1] + [name[letter] for letter in path] for path in LATE_PATHS]
    links = pos_bits + row_bits
    rows_n, length = segments.shape
    tokens_n, features = x_rows.shape
    inner_n = weights[4].shape[1]
    width = features // 4
    every = rows_n * length
    steps = len(links)
    half = features // 2
    early = landing_shape(features, features, links)
    late = landing_shape(half, half, row_bits)
    vmem = pl.BlockSpec(memory_space=pltpu.VMEM)
    hbm = pl.BlockSpec(memory_space=pl.ANY)
    dma = pltpu.SemaphoreType.DMA
    shape = jax.ShapeDtypeStruct
    square = shape((features, features), LOW)
    return pl.pallas_call(
        partial(layer_kernel, rows_n, paths, late_paths, links),
        out_shape=[
            square,
            square,
            square,
            square,
            shape((features, inner_n), LOW),
            shape((inner_n, features), LOW),
            shape((3 * width // HEAD_DIM, every, HEAD_DIM), LOW),
            shape((half, every), LOW),
            shape((tokens_n, features), LOW),
            shape((tokens_n, features), F32),
            shape((16, features), F32),
        ],
        in_specs=[vmem] * 12 + [hbm] * 6,
        out_specs=[hbm] * 8 + [vmem] * 3,
        scratch_shapes=[
            pltpu.VMEM((every, features), LOW),
            pltpu.VMEM((4, tokens_n, width), LOW),
            pltpu.VMEM((features, features), LOW),
            pltpu.VMEM((features, inner_n), LOW),
            pltpu.VMEM((inner_n, features), LOW),
            pltpu.VMEM((features, 3 * width), LOW),
            pltpu.VMEM((features, 3 * width), LOW),
            pltpu.VMEM((16, length), F32),
            pltpu.VMEM((rows_n, length), F32),
            pltpu.VMEM((rows_n, length, LANES), F32),
            pltpu.VMEM((every, width), LOW),
            pltpu.VMEM((2, every, 3 * width), LOW),
            pltpu.VMEM((tokens_n, features), LOW),
            pltpu.VMEM((tokens_n, features), LOW),
            pltpu.VMEM((SLOTS, half, features), LOW),
            pltpu.VMEM((9, half, features), LOW),
            pltpu.VMEM((3, half, half), LOW),
            pltpu.VMEM((9, *early), LOW),
            pltpu.VMEM((3, *late), LOW),
            pltpu.VMEM((steps, 16, features), F32),
            dma((12, 2 * steps)),
            dma((12, 2 * steps)),
            dma((12,)),
            dma((steps,)),
            dma((steps,)),
            *[dma((3, rows_n))] * 6,
            *[dma((rows_n,))] * 4,
            dma((9,)),
            dma((rows_n + 1,)),
            pltpu.VMEM((16, features), F32),
        ],
        compiler_params=pltpu.CompilerParams(
            collective_id=0, has_side_effects=True, vmem_limit_bytes=VMEM_LIMIT
        ),
        cost_estimate=pl.CostEstimate(
            flops=4 * 10**10, bytes_accessed=8 * 10**7, transcendentals=8 * 10**6
        ),
        name="layer",
    )(*vectors, x_rows, cot, segments, *weights)


def finish_kernel(moved, *refs):
    sources = refs[: moved + 1]
    outs = refs[moved + 1 :]
    for src, dst in zip(sources[:moved], outs[:moved]):
        dst[...] = src[...].astype(dst.dtype)
    small = sources[moved]
    for index, dst in enumerate(outs[moved:-1]):
        dst[...] = small[index, :]
    outs[-1][...] = jnp.concatenate([small[index, :] for index in range(12, 16)])


def finish(blocks, result, grad_tokens, small, steps):
    arrays = [*blocks, result, grad_tokens]
    kinds = [F32] * len(blocks) + [result.dtype, grad_tokens.dtype]
    specs = [pl.BlockSpec((a.shape[0] // steps, a.shape[1]), lambda i: (i, 0)) for a in arrays]
    features = small.shape[1]
    vectors = [features] * 10 + [4 * features]
    shape = jax.ShapeDtypeStruct
    return pl.pallas_call(
        partial(finish_kernel, len(arrays)),
        grid=(steps,),
        out_shape=[shape(a.shape, kind) for a, kind in zip(arrays, kinds)]
        + [shape((size,), F32) for size in vectors],
        in_specs=[*specs, pl.BlockSpec(small.shape, lambda i: (0, 0))],
        out_specs=[*specs, *[pl.BlockSpec((size,), lambda i: (0,)) for size in vectors]],
        compiler_params=pltpu.CompilerParams(vmem_limit_bytes=VMEM_LIMIT),
        cost_estimate=pl.CostEstimate(
            flops=0, bytes_accessed=6 * sum(a.size for a in arrays), transcendentals=0
        ),
        name="finish",
    )(*arrays, small)


def on_device(
    mesh_shape,
    tokens,
    segments,
    w_query,
    b_query,
    w_key,
    w_value,
    b_value,
    w_out,
    b_out,
    gain_one,
    shift_one,
    w_up,
    b_up,
    w_down,
    b_down,
    gain_two,
    shift_two,
    cotangent,
):
    rows_n, part_len, features = tokens.shape
    flat = (rows_n * part_len, features)
    vectors = (b_query, b_value, b_out, gain_one, shift_one, b_down, gain_two, shift_two, b_up)
    outs = layer(
        mesh_shape,
        vectors,
        tokens.reshape(flat),
        cotangent.reshape(flat),
        segments,
        (w_query, w_key, w_value, w_out, w_up, w_down),
    )
    (g_query, g_key, g_value, g_out, g_up, g_down, result, grad_tokens, *vectors) = finish(
        outs[:6], *outs[8:], 3
    )
    shape = (rows_n, part_len, features)
    return (
        result.reshape(shape),
        grad_tokens.reshape(shape),
        g_query,
        vectors[8],
        g_key,
        g_value,
        vectors[9],
        g_out,
        vectors[0],
        vectors[1],
        vectors[2],
        g_up,
        vectors[10],
        g_down,
        vectors[3],
        vectors[4],
        vectors[5],
    )


def solution(mesh):
    tokens = P("rows", "pos", None)
    return jax.shard_map(
        partial(on_device, dict(mesh.shape)),
        mesh=mesh,
        in_specs=(tokens, P("rows", None), *[P()] * 15, tokens),
        out_specs=(tokens, tokens, *[P()] * 15),
        check_vma=False,
    )
```

```python
from functools import partial

import jax
import jax.numpy as jnp
from jax import lax
from jax.experimental import pallas as pl
from jax.experimental.pallas import tpu as pltpu
from jax.sharding import PartitionSpec as P

HEADS = 12
HEAD_DIM = 64
EPS = 1e-05
MASKED = -1000000000.0
SCALE = HEAD_DIM ** (-0.5)
LANES = 128
VMEM_LIMIT = 60 * 2**20
MESH = pl.DeviceIdType.MESH
LOW = jnp.bfloat16
F32 = jnp.float32


def flip(value, bit):
    return value + bit - 2 * bit * lax.rem(lax.div(value, bit), 2)


def bit_of(value, bit):
    return lax.rem(lax.div(value, bit), 2)


def axis_bits(size):
    assert size & (size - 1) == 0
    return [1 << i for i in range(size.bit_length() - 1)]


def dot(a, b):
    return jnp.dot(a, b, preferred_element_type=F32)


def dot_nt(a, b):
    return lax.dot_general(a, b, (((1,), (1,)), ((), ())), preferred_element_type=F32)


def dot_tn(a, b):
    return lax.dot_general(a, b, (((0,), (0,)), ((), ())), preferred_element_type=F32)


class Place:
    def __init__(self):
        self.row = lax.axis_index("rows")
        self.pos = lax.axis_index("pos")

    def partner(self, link):
        axis, bit = link
        if axis == "r":
            return (flip(self.row, bit), self.pos)
        return (self.row, flip(self.pos, bit))

    def side(self, link):
        axis, bit = link
        return bit_of(self.row if axis == "r" else self.pos, bit)


def remote(src, dst, sems, index, device):
    send_sem, recv_sem = sems
    return pltpu.make_async_remote_copy(
        src_ref=src,
        dst_ref=dst,
        send_sem=send_sem.at[index],
        recv_sem=recv_sem.at[index],
        device_id=device,
        device_id_type=MESH,
    )


def greet(devices):
    barrier = pltpu.get_barrier_semaphore()
    for device in devices:
        pl.semaphore_signal(barrier, inc=1, device_id=device, device_id_type=MESH)
    pl.semaphore_wait(barrier, len(devices))


def rows_at(ref, start, size):
    return ref.at[pl.ds(pl.multiple_of(start, 16), size)]


def plan_splits(rows, cols, links):
    kinds = []
    for _ in links:
        if (rows // 2) % 16 == 0:
            rows //= 2
            kinds.append("rows")
        elif (cols // 2) % LANES == 0:
            cols //= 2
            kinds.append("cols")
        else:
            kinds.append("whole")
    return kinds


def shrink(rows, cols, kind):
    return (rows // 2 if kind == "rows" else rows, cols // 2 if kind == "cols" else cols)


def landing_shape(rows, cols, links):
    total, widest = 0, 0
    for kind in plan_splits(rows, cols, links):
        rows, cols = shrink(rows, cols, kind)
        total, widest = total + rows, max(widest, cols)
    return total, widest


def add_into(dst, left, right, rows):
    step = 16 if rows % 48 else 48

    @pl.loop(0, rows // step)
    def _(i):
        at = pl.ds(pl.multiple_of(i * step, step), step)
        dst[at, :] = (left[at, :].astype(F32) + right[at, :].astype(F32)).astype(dst.dtype)


def window(ref, row0, rows, col0, cols):
    if not isinstance(row0, int):
        row0 = pl.multiple_of(row0, 16)
    if not isinstance(col0, int):
        col0 = pl.multiple_of(col0, LANES)
    return ref.at[pl.ds(row0, rows), pl.ds(col0, cols)]


class Chunk:
    def __init__(self, place, fixed, path, gather, give, out, total, landing, sems):
        send_sem, recv_sem, copy_sem = sems
        self.reduces, self.gathers, self.moment, self.gave = [], [], 0, False
        rows, cols = out.shape
        row0, col0, landed, slot = 0, 0, 0, 0
        corner = None
        row_trail, col_trail, kind_of = [], [], {}

        def held(at, rows, cols):
            return window(total, at[0] - corner[0], rows, at[1] - corner[1], cols)

        shape = out.shape
        for _, kind in fixed:
            shape = shrink(*shape, kind)
        kinds = [kind for _, kind in fixed] + plan_splits(*shape, path)
        for number, (link, kind) in enumerate(zip([link for link, _ in fixed] + path, kinds)):
            side = place.side(link)
            kind_of[link] = kind
            keep = other = (row0, col0)
            if kind == "rows":
                row_trail.append((row0, rows))
                rows //= 2
                keep, other = (row0 + side * rows, col0), (row0 + (1 - side) * rows, col0)
            elif kind == "cols":
                col_trail.append((col0, cols))
                cols //= 2
                keep, other = (row0, col0 + side * cols), (row0, col0 + (1 - side) * cols)
            row0, col0 = keep
            if number == max(len(fixed) - 1, 0):
                corner = keep
            if number < len(fixed):
                continue
            land = window(landing, landed, rows, 0, cols)
            landed += rows
            src = give if number == 0 else held(other, rows, cols)
            copy = remote(src, land, (send_sem, recv_sem), slot, place.partner(link))
            slot += 1
            self.reduces.append((copy, held(keep, rows, cols), land, kind == "whole"))
        mine = window(out, row0, rows, col0, cols)
        self.own = pltpu.make_async_copy(held((row0, col0), rows, cols), mine, copy_sem)
        src = held((row0, col0), rows, cols)
        for link in gather:
            kind = kind_of[link]
            if kind == "whole":
                self.gathers.append(None)
                continue
            here = window(out, row0, rows, col0, cols)
            src = here if src is None else src
            self.gathers.append(remote(src, here, (send_sem, recv_sem), slot, place.partner(link)))
            src = None
            slot += 1
            if kind == "rows":
                row0, rows = row_trail.pop()
            else:
                col0, cols = col_trail.pop()

    def done(self):
        return self.moment > len(self.reduces) + len(self.gathers)

    def advance(self):
        count, now = len(self.reduces), self.moment
        if 0 < now <= count:
            copy, keep, land, whole = self.reduces[now - 1]
            copy.wait_recv()
            if whole:
                copy.wait_send()
            add_into(keep, keep, land, land.shape[0])
        elif now > count:
            if now == count + 1:
                self.own.wait()
            if self.gathers[now - count - 1] is not None:
                self.gathers[now - count - 1].wait_recv()
        if now < count:
            self.reduces[now][0].start()
        elif now < count + len(self.gathers):
            if now == count:
                self.own.start()
            if self.gathers[now - count] is not None:
                self.gathers[now - count].start()
        else:
            for index, (copy, _, _, whole) in enumerate(self.reduces):
                if not whole and not (index == 0 and self.gave):
                    copy.wait_send()
            for copy in self.gathers:
                if copy is not None:
                    copy.wait_send()
        self.moment += 1


PATHS = ("cyxzw", "cxyzw", "czwxy", "cyxzw", "czwxy", "cxyzw", "cxyzw", "cyzwx", "cxyzw")
LATE_PATHS = ("wzxyc", "wzxyc", "wyzxc")
TICKS = (
    (),
    (),
    (),
    (),
    (0, 1, 2),
    (),
    (),
    (3, 4),
    (5,),
    (0, 1, 2),
    (6,),
    (),
    (3, 4, 5, 7, 1),
    (0, 2, 8),
    (1,),
    (4, 6, 0),
    (3,),
    (1, 2),
    (5,),
    (0, 3),
    (8, 1),
    (4, 5, 7),
    (),
    (0, 6),
    (1, 2, 3),
    (),
    (4, 5, 8),
    (),
    (0, 7),
)
DRAIN = (3, 6, 9, 5, 8, 10, 3, 7, 11, 6, 9, 8, 5, 0, 10, 3, 6, 1, 11, 7, 2, 9, 4, 8, 10, 5, 6, 11, 9, 8, 1, 7, 10, 0, 2, 11, 1, 9, 4, 0, 10, 3, 7, 5, 3, 6, 5, 9, 8, 2, 11, 10, 7, 4, 6, 9, 2, 6, 9, 11, 2, 8, 10, 8, 10, 4, 7, 4, 11, 7, 11)
TAIL_STEEP = 0.24
TAIL = (
    0.09575598852910579,
    0.09547705164870551,
    0.093198719112773,
    0.06193635630868121,
    0.1216760657292812,
    -0.06984360139735674,
    0.1555215658230106,
    -0.05372215169653546,
)
TILE = 256
WIDE = 768
BAND = 96
SLOTS = 4


def gelu_and_slope(u):
    bell = jnp.exp(u * u * -0.5)
    t = 1.0 / (1.0 + TAIL_STEEP * jnp.abs(u))
    f = TAIL[-1]
    for coefficient in TAIL[-2::-1]:
        f = f * t + coefficient
    below = f * t * bell
    phi = jnp.where(u > 0, 1.0 - below, below)
    return u * phi, phi + u * (bell * 0.3989422804014327)


def fold(v):
    return jnp.sum(v.reshape(v.shape[0] // 8, 8, v.shape[1]), axis=0)


def bands(n, init, body):
    def step(i, carry):
        return body(pl.ds(pl.multiple_of(i * BAND, BAND), BAND), carry)

    return lax.fori_loop(0, n // BAND, step, init)


def layer_kernel(rows_n, paths, late_paths, links, *refs):
    vector_refs, refs = refs[:9], refs[9:]
    (x_in, cot, segments, q_in, k_in, v_in, w_out_in, w_up_in, w_down_in) = refs[:9]
    refs = refs[:2] + refs[1:]
    (q_out, k_out, v_out, o_out, up_out, down_out, qkv_kept, turned_kept) = refs[10:18]
    (result, dx_out, small_out) = refs[18:21]
    (x_all, mixed, w_out, w_up, w_down, w_own, w_mate, lse, seg_row, seg_wide) = refs[21:31]
    (d_all, chip, dx_give, dx_land, gives, total, late_total, landing, late_land) = refs[31:40]
    (small_land, send_sem, recv_sem, copy_sem, small_send, small_recv) = refs[40:46]
    (x_send, x_recv, m_send, m_recv, d_send, d_recv) = refs[46:52]
    (g_send, g_recv, dx_send, dx_recv, load_sem, own_sem, vecs) = refs[52:59]
    d_give = mixed
    place = Place()
    me = place.pos
    mate, across = flip(me, 1), flip(me, 2)
    far = flip(mate, 2)
    peers = [across, far, mate]
    core = bit_of(me, 1)
    tokens_n, features = x_in.shape
    part = tokens_n // rows_n
    length = 4 * part
    width = d_all.shape[1]
    heads = width // HEAD_DIM
    inner_n = w_up.shape[1]
    half = features // 2
    quarters = inner_n // features
    outs = [window(down_out, j * features, features, 0, features) for j in range(inner_n // features)]
    outs += [window(up_out, 0, features, j * features, features) for j in range(inner_n // features)]
    outs += [o_out]
    chunks = []
    for index, out in enumerate(outs + [q_out, k_out, v_out]):
        sems = (send_sem.at[index], recv_sem.at[index], copy_sem.at[index])
        if index < len(outs):
            path = paths[index]
            spaces = (gives.at[index % SLOTS], out, total.at[index], landing.at[index])
            chunks.append(Chunk(place, [], path, path[::-1], *spaces, sems))
        else:
            at = index - len(outs)
            fixed = [(links[0], "rows"), (links[1], "cols")]
            spaces = (None, out, late_total.at[at], late_land.at[at])
            chunks.append(Chunk(place, fixed, links[2:], late_paths[at], *spaces, sems))
    mine, other = chip.at[core], chip.at[1 - core]
    d_copies, g_copies, dx_copies = {}, [], []
    for r in range(rows_n):
        at = pl.ds(r * part, part)
        row = pl.ds(r * length, length)
        for index, peer in enumerate(peers):
            d_copies[index, r] = remote(
                d_give.at[peer, at],
                rows_at(d_all, r * length + me * part, part),
                (d_send, d_recv),
                (index, r),
                (place.row, peer),
            )
        g_copies.append(
            remote(mine.at[row], mine.at[row], (g_send, g_recv), r, (place.row, mate))
        )
        dx_copies.append(
            remote(dx_give.at[at], dx_land.at[at], (dx_send, dx_recv), r, (place.row, across))
        )
    ticks = [0]

    def tick():
        for index in TICKS[ticks[0]]:
            if chunks[index].moment > 0 and not chunks[index].done():
                chunks[index].advance()
        ticks[0] += 1

    def new_chunk(index, give, keep):
        chunk = chunks[index]
        if index >= SLOTS:
            chunks[index - SLOTS].reduces[0][0].wait_send()
            chunks[index - SLOTS].gave = True
        gives[index % SLOTS] = give().astype(LOW)
        chunk.advance()
        total[index] = keep().astype(LOW)

    to_across, to_mate, passed, own, m_copies = [], [], [], [], []

    def x_spot(r, owner):
        return rows_at(x_all, r * length + owner * part, part)

    for r in range(rows_n):
        src = x_in.at[pl.ds(r * part, part)]
        x_sems = (x_send, x_recv)
        to_across.append(remote(src, x_spot(r, me), x_sems, (0, r), (place.row, across)))
        to_mate.append(remote(src, x_spot(r, me), x_sems, (1, r), (place.row, mate)))
        spot = x_spot(r, across)
        passed.append(remote(spot, spot, x_sems, (2, r), (place.row, mate)))
        own.append(pltpu.make_async_copy(src, x_spot(r, me), own_sem.at[r]))
        own[r].start()
    weights = [
        pltpu.make_async_copy(src, dst, load_sem.at[index])
        for index, (src, dst) in enumerate(((w_out_in, w_out), (w_up_in, w_up), (w_down_in, w_down)))
    ]
    greet([place.partner(link) for link in links] + [(place.row, far)])
    for r in range(rows_n):
        to_across[r].start()
        to_mate[r].start()
    give_at = pl.ds(pl.multiple_of((1 - core) * half, LANES), half)
    keep_at = pl.ds(pl.multiple_of(core * half, LANES), half)
    small_out[...] = jnp.zeros_like(small_out)

    def attend(windows, qkv, x_turned, blend, lse_cols):
        loads = []
        for owner in range(2):
            first = lax.div(3 * (me if owner == 0 else mate), 2) * LANES
            for index, src in enumerate((q_in, k_in, v_in)):
                at = 3 * owner + index
                window_of = src.at[:, pl.ds(pl.multiple_of(first, LANES), TILE)]
                loads.append(pltpu.make_async_copy(window_of, windows.at[at], load_sem.at[3 + at]))
                loads[-1].start()
        for copy in weights:
            copy.start()
        for index, ref in enumerate(vector_refs[:8]):
            vecs[index : index + 1, :] = ref[...].astype(F32)[None]
        up_bias = vector_refs[8][...].astype(F32)[None]
        for quarter in range(quarters):
            at = slice(quarter * features, (quarter + 1) * features)
            vecs[8 + quarter : 9 + quarter, :] = up_bias[:, at]
        seg_row[...] = segments[...].astype(F32)
        for r in range(rows_n):
            row = seg_row[r : r + 1, :]
            seg_wide[r] = jnp.transpose(jnp.broadcast_to(row, (LANES, length)))
        for load in loads:
            load.wait()
        for owner, dst in enumerate((w_own, w_mate)):
            for index in range(3):
                at = slice(index * width, (index + 1) * width)
                for odd in range(2):

                    @pl.when(lax.rem(me + owner, 2) == odd)
                    def _():
                        left = odd * HEAD_DIM
                        dst[:, at] = windows[3 * owner + index, :, left : left + width]

        first = pl.ds(pl.multiple_of(lax.div(3 * me, 2) * LANES, LANES), TILE)
        odd = lax.rem(me, 2) == 1
        biases = []
        for index in range(2):
            bias = vecs[index : index + 1, first]
            biases.append(jnp.where(odd, bias[:, HEAD_DIM : HEAD_DIM + width], bias[:, :width]))
        b_own = jnp.concatenate([biases[0], jnp.zeros((1, width), F32), biases[1]], axis=1)
        is_query = lax.broadcasted_iota(jnp.int32, (1, 3 * width), 1) < width
        scale = jnp.where(is_query, SCALE, 1.0)
        kept = []
        for r in range(rows_n):
            if r == 0:
                to_across[r].wait_recv()
                passed[r].start()
            to_mate[r].wait_recv()
            own[r].wait()
            passed[r].wait_recv()
            base = r * length
            x_row = x_all[base : base + length, :]
            made = ((dot(x_row, w_own[...]) + b_own) * scale).astype(LOW)
            for index in range(3 * heads):
                left = index * HEAD_DIM
                qkv[index, base : base + length, :] = made[:, left : left + HEAD_DIM]
            row = pl.ds(base, length)
            kept.append(
                pltpu.make_async_copy(qkv.at[:, row, :], qkv_kept.at[:, row, :], own_sem.at[r])
            )
            kept[-1].start()

            for index, owner in enumerate((*peers, me)):
                here = pl.ds(pl.multiple_of(base + owner * part, 16), part)
                local = pl.ds(pl.multiple_of(owner * part, 16), part)
                seg_q = seg_wide[r, local, :]
                same = jnp.concatenate([seg_q] * (length // LANES), axis=1) == seg_row[r : r + 1, :]
                for head in range(heads):
                    query = qkv[head, here, :]
                    key = qkv[heads + head, base : base + length, :]
                    value = qkv[2 * heads + head, base : base + length, :]
                    scores = jnp.where(same, dot_nt(query, key), MASKED)
                    top = jnp.max(scores, axis=-1, keepdims=True)
                    power = jnp.exp(scores - top)
                    sums = jnp.sum(power, axis=-1, keepdims=True)
                    out = dot(power.astype(LOW), value) / sums
                    blend[here, head * HEAD_DIM : (head + 1) * HEAD_DIM] = out.astype(LOW)
                    column = r * heads + head
                    lse_cols[local, column : column + 1] = top + jnp.log(sums)
                if index < len(peers):
                    copy = remote(
                        blend.at[here],
                        mixed.at[me, pl.ds(r * part, part)],
                        (m_send, m_recv),
                        (index, r),
                        (place.row, owner),
                    )
                    copy.start()
                    m_copies.append(copy)
                else:
                    mixed[me, r * part : (r + 1) * part, :] = blend[here, :]
                if index == 1 and r + 1 < rows_n:
                    to_across[r + 1].wait_recv()
                    passed[r + 1].start()
        lse[...] = jnp.transpose(lse_cols[...])[: lse.shape[0], :]
        mine_half = pl.ds(pl.multiple_of(core * half, LANES), half)
        for r in range(rows_n):
            base = r * length
            x_turned[:, base : base + length] = jnp.transpose(x_all[base : base + length, mine_half])
        kept.append(pltpu.make_async_copy(x_turned, turned_kept, own_sem.at[rows_n]))
        kept[-1].start()
        for copy in to_across + to_mate + passed:
            copy.wait_send()
        for copy in m_copies:
            copy.wait()
        for copy in kept:
            copy.wait()

    every = rows_n * length
    pl.run_scoped(
        attend,
        pltpu.VMEM((6, features, TILE), LOW),
        pltpu.VMEM(qkv_kept.shape, LOW),
        pltpu.VMEM(turned_kept.shape, LOW),
        pltpu.VMEM((every, width), LOW),
        pltpu.VMEM((length, LANES), F32),
    )

    active = x_all

    def dense(joined, hat, spread_one, low, turned, slope, d_low):
        acc = dx_out
        for group in range(4):
            joined[:, group * width : (group + 1) * width] = mixed[group]
        gain_one, shift_one = vecs[3:4, :], vecs[4:5, :]
        gain_two, shift_two = vecs[6:7, :], vecs[7:8, :]
        weights[0].wait()
        acc[...] = dot(joined[...], w_out[...])

        def norm_one(at, carry):
            v = x_in[at, :].astype(F32) + (acc[at, :] + vecs[2:3, :])
            centred = v - jnp.mean(v, axis=-1, keepdims=True)
            over = lax.rsqrt(jnp.mean(centred * centred, axis=-1, keepdims=True) + EPS)
            v = centred * over
            hat[at, :] = v
            spread_one[at, :] = jnp.broadcast_to(over, (BAND, LANES))
            low[at, :] = (v * gain_one + shift_one).astype(LOW)
            return carry

        bands(tokens_n, 0, norm_one)
        weights[1].wait()
        for quarter in range(quarters):

            @pl.loop(0, features // WIDE)
            def _(tile):
                cols = pl.ds(pl.multiple_of(tile * WIDE, WIDE), WIDE)
                wide = pl.ds(pl.multiple_of(quarter * features + tile * WIDE, WIDE), WIDE)
                u = dot(low[...], w_up[:, wide]) + vecs[8 + quarter : 9 + quarter, cols]
                for band in range(tokens_n // BAND):
                    at = slice(band * BAND, (band + 1) * BAND)
                    g, s = gelu_and_slope(u[at])
                    active[quarter * tokens_n + band * BAND : quarter * tokens_n + (band + 1) * BAND, cols] = g.astype(LOW)
                    slope[at, wide] = s

        weights[2].wait()

        @pl.loop(0, features // WIDE)
        def _(tile):
            cols = pl.ds(pl.multiple_of(tile * WIDE, WIDE), WIDE)
            acc[:, cols] = sum(
                dot(
                    active[quarter * tokens_n : (quarter + 1) * tokens_n, :],
                    w_down[quarter * features : (quarter + 1) * features, cols],
                )
                for quarter in range(quarters)
            )

        def norm_two(at, carry):
            d_gain, d_shift, d_bias = carry
            v = hat[at, :] * gain_one + shift_one + (acc[at, :] + vecs[5:6, :])
            centred = v - jnp.mean(v, axis=-1, keepdims=True)
            over = lax.rsqrt(jnp.mean(centred * centred, axis=-1, keepdims=True) + EPS)
            v = centred * over
            result[at, :] = (v * gain_two + shift_two).astype(LOW)
            d = cot[at, :].astype(F32)
            d_gain += fold(d * v)
            d_shift += fold(d)
            d = d * gain_two
            d = d - jnp.mean(d, axis=-1, keepdims=True) - v * jnp.mean(d * v, axis=-1, keepdims=True)
            d = d * over
            acc[at, :] = d
            d = d.astype(LOW)
            d_low[at, :] = d
            return d_gain, d_shift, d_bias + fold(d.astype(F32))

        blank = jnp.zeros((8, features), F32)
        d_gain, d_shift, d_bias = bands(tokens_n, (blank, blank, blank), norm_two)
        for index, value in ((3, d_bias), (4, d_gain), (5, d_shift)):
            small_out[index : index + 1, :] = jnp.sum(value, axis=0, keepdims=True)

        for quarter in range(quarters):

            def some_down(side):
                at = pl.ds(pl.multiple_of(side * half, LANES), half)
                return dot_tn(active[quarter * tokens_n : (quarter + 1) * tokens_n, at], d_low[...])

            new_chunk(quarter, lambda: some_down(1 - core), lambda: some_down(core))
            tick()
        turned[...] = jnp.transpose(low[...])
        for quarter in range(quarters):
            first = quarter * features
            d_up = active.at[pl.ds(quarter * tokens_n, tokens_n)]

            @pl.loop(0, features // WIDE)
            def _(tile):
                rows = pl.ds(pl.multiple_of(first + tile * WIDE, WIDE), WIDE)
                cols = pl.ds(pl.multiple_of(tile * WIDE, WIDE), WIDE)
                d = (dot_nt(d_low[...], w_down[rows, :]) * slope[:, rows]).astype(LOW)
                d_up[:, cols] = d
                small_out[12 + quarter : 13 + quarter, cols] = jnp.sum(
                    d.astype(F32), axis=0, keepdims=True
                )

            tick()
            new_chunk(
                quarters + quarter,
                lambda: dot(turned[give_at, :], d_up[...]),
                lambda: dot(turned[keep_at, :], d_up[...]),
            )
            acc[...] += dot_nt(d_up[...], w_up[:, first : first + features])
            tick()

        def norm_back(at, carry):
            d_gain, d_shift, d_bias = carry
            v, d = hat[at, :], acc[at, :]
            d_gain += fold(d * v)
            d_shift += fold(d)
            d = d * gain_one
            d = d - jnp.mean(d, axis=-1, keepdims=True) - v * jnp.mean(d * v, axis=-1, keepdims=True)
            d = d * spread_one[at, 0:1]
            acc[at, :] = d
            d = d.astype(LOW)
            d_low[at, :] = d
            return d_gain, d_shift, d_bias + fold(d.astype(F32))

        d_gain, d_shift, d_bias = bands(tokens_n, (blank, blank, blank), norm_back)
        for index, value in ((0, d_bias), (1, d_gain), (2, d_shift)):
            small_out[index : index + 1, :] = jnp.sum(value, axis=0, keepdims=True)
        for group in range(4):
            at = slice(group * width, (group + 1) * width)
            d_give[group] = dot_nt(d_low[...], w_out[at, :]).astype(LOW)
        for r in range(rows_n):
            for index in range(3):
                d_copies[index, r].start()
        new_chunk(
            2 * quarters,
            lambda: dot_tn(joined[:, give_at], d_low[...]),
            lambda: dot_tn(joined[:, keep_at], d_low[...]),
        )
        tick()

    square = (tokens_n, features)
    pl.run_scoped(
        dense,
        pltpu.VMEM(square, LOW),
        pltpu.VMEM(square, F32),
        pltpu.VMEM((tokens_n, LANES), F32),
        pltpu.VMEM(square, LOW),
        pltpu.VMEM((features, tokens_n), LOW),
        pltpu.VMEM((tokens_n, inner_n), F32),
        pltpu.VMEM(square, LOW),
    )
    prob = [w_up.at[pl.ds(0, length), pl.ds(head * length, length)] for head in range(heads)]
    d_score = [w_down.at[pl.ds(head * features, length), pl.ds(0, length)] for head in range(heads)]

    def attention(qkv, x_turned, d_heads):
        loads = []
        for index, (src, dst) in enumerate(((qkv_kept, qkv), (turned_kept, x_turned))):
            loads.append(pltpu.make_async_copy(src, dst, load_sem.at[index]))
            loads[-1].start()
        for load in loads:
            load.wait()
        for r in range(rows_n):
            base = r * length
            own_rows = pl.ds(pl.multiple_of(base + me * part, 16), part)
            d_all[own_rows, :] = d_give[me, r * part : (r + 1) * part, :]
            for index in range(3):
                d_copies[index, r].wait_recv()
            d_row = d_all[base : base + length, :]
            for head in range(heads):
                d_heads[head] = d_row[:, head * HEAD_DIM : (head + 1) * HEAD_DIM]

            def scores(block):
                here = pl.ds(pl.multiple_of(base + block * LANES, LANES), LANES)
                local = pl.ds(pl.multiple_of(block * LANES, LANES), LANES)
                same = seg_wide[r] == seg_row[r : r + 1, local]
                for head in range(heads):
                    query = qkv[head, here, :]
                    key = qkv[heads + head, base : base + length, :]
                    value = qkv[2 * heads + head, base : base + length, :]
                    log_total = lse[r * heads + head : r * heads + head + 1, local]
                    p = jnp.exp(jnp.where(same, dot_nt(key, query) - log_total, MASKED))
                    dp = dot_nt(value, d_heads[head, local, :])
                    inner = jnp.sum(dp * p, axis=0, keepdims=True)
                    prob[head][:, local] = p.astype(LOW)
                    d_score[head][:, local] = (p * (dp - inner)).astype(LOW)

            blocks = length // LANES
            pl.loop(0, blocks // 2)(scores)
            tick()
            pl.loop(blocks // 2, blocks)(scores)
            tick()
            for head in range(heads):
                query = qkv[head, base : base + length, :]
                key = qkv[heads + head, base : base + length, :]
                ds = d_score[head][...]
                at = slice(base, base + length)
                left = head * HEAD_DIM
                dq = dot_tn(ds, key) * SCALE
                mine[at, left : left + HEAD_DIM] = dq.astype(LOW)
                left += width
                mine[at, left : left + HEAD_DIM] = dot(ds, query).astype(LOW)
                left += width
                mine[at, left : left + HEAD_DIM] = dot(prob[head][...], d_heads[head]).astype(LOW)
            g_copies[r].start()
            tick()

        def dx_of(r, owner):
            at = pl.ds(pl.multiple_of(r * length + owner * part, 16), part)
            return dot_nt(mine[at, :], w_own[...]) + dot_nt(other[at, :], w_mate[...])

        for r in range(rows_n):
            g_copies[r].wait_recv()
            at = pl.ds(r * part, part)
            dx_give[at, :] = dx_of(r, across).astype(LOW)
            dx_copies[r].start()
            tick()
        for index in range(3):
            left = index * width
            sums = [dot(x_turned[...], chip[side, :, left : left + width]) for side in range(2)]
            late_total[index] = jnp.concatenate(sums, axis=1).astype(LOW)
            chunks[2 * quarters + 1 + index].advance()
            tick()
        token_sums = jnp.sum(mine[...].astype(F32), axis=0, keepdims=True)
        owner = lax.div(lax.broadcasted_iota(jnp.int32, (1, features), 1), width)
        for row, left in ((8, 0), (9, 2 * width)):
            spread = jnp.concatenate([token_sums[:, left : left + width]] * 4, axis=1)
            small_out[row : row + 1, :] = jnp.where(owner == me, spread, 0.0)
        for r in range(rows_n):
            at = pl.ds(r * part, part)
            dx_out[at, :] += dx_of(r, me)
        tick()

    pl.run_scoped(
        attention,
        pltpu.VMEM(qkv_kept.shape, LOW),
        pltpu.VMEM(turned_kept.shape, LOW),
        pltpu.VMEM((heads, length, HEAD_DIM), LOW),
    )
    smalls = [
        remote(
            small_out, small_land.at[number], (small_send, small_recv), number, place.partner(link)
        )
        for number, link in enumerate(links)
    ]
    gap = len(DRAIN) // (len(links) + 1)

    def small_step(number):
        if 0 < number <= len(links):
            smalls[number - 1].wait()
            small_out[...] += small_land[number - 1]
        if number < len(links):
            smalls[number].start()

    for at, index in enumerate(DRAIN):
        if at % gap == 0:
            small_step(at // gap)
        if not chunks[index].done():
            chunks[index].advance()
    for number in range((len(DRAIN) - 1) // gap + 1, len(links) + 1):
        small_step(number)
    while not all(chunk.done() for chunk in chunks):
        for chunk in chunks:
            if not chunk.done():
                chunk.advance()
    for r in range(rows_n):
        dx_copies[r].wait_recv()
        at = pl.ds(r * part, part)
        dx_out[at, :] += dx_land[at, :].astype(F32)
    for copy in dx_copies + g_copies + list(d_copies.values()):
        copy.wait_send()


def layer(mesh_shape, vectors, x_rows, cot, segments, weights):
    row_bits = [("r", bit) for bit in axis_bits(mesh_shape["rows"])]
    pos_bits = [("p", bit) for bit in axis_bits(mesh_shape["pos"])]
    name = dict(zip("cyxzw", pos_bits + row_bits))
    paths = [[name[letter] for letter in path] + row_bits[3:] for path in PATHS]
    late_paths = [row_bits[3:][::-1] + [name[letter] for letter in path] for path in LATE_PATHS]
    links = pos_bits + row_bits
    rows_n, length = segments.shape
    tokens_n, features = x_rows.shape
    inner_n = weights[4].shape[1]
    width = features // 4
    every = rows_n * length
    steps = len(links)
    half = features // 2
    early = landing_shape(features, features, links)
    late = landing_shape(half, half, row_bits)
    vmem = pl.BlockSpec(memory_space=pltpu.VMEM)
    hbm = pl.BlockSpec(memory_space=pl.ANY)
    dma = pltpu.SemaphoreType.DMA
    shape = jax.ShapeDtypeStruct
    square = shape((features, features), LOW)
    return pl.pallas_call(
        partial(layer_kernel, rows_n, paths, late_paths, links),
        out_shape=[
            square,
            square,
            square,
            square,
            shape((features, inner_n), LOW),
            shape((inner_n, features), LOW),
            shape((3 * width // HEAD_DIM, every, HEAD_DIM), LOW),
            shape((half, every), LOW),
            shape((tokens_n, features), LOW),
            shape((tokens_n, features), F32),
            shape((16, features), F32),
        ],
        in_specs=[vmem] * 12 + [hbm] * 6,
        out_specs=[hbm] * 8 + [vmem] * 3,
        scratch_shapes=[
            pltpu.VMEM((every, features), LOW),
            pltpu.VMEM((4, tokens_n, width), LOW),
            pltpu.VMEM((features, features), LOW),
            pltpu.VMEM((features, inner_n), LOW),
            pltpu.VMEM((inner_n, features), LOW),
            pltpu.VMEM((features, 3 * width), LOW),
            pltpu.VMEM((features, 3 * width), LOW),
            pltpu.VMEM((16, length), F32),
            pltpu.VMEM((rows_n, length), F32),
            pltpu.VMEM((rows_n, length, LANES), F32),
            pltpu.VMEM((every, width), LOW),
            pltpu.VMEM((2, every, 3 * width), LOW),
            pltpu.VMEM((tokens_n, features), LOW),
            pltpu.VMEM((tokens_n, features), LOW),
            pltpu.VMEM((SLOTS, half, features), LOW),
            pltpu.VMEM((9, half, features), LOW),
            pltpu.VMEM((3, half, half), LOW),
            pltpu.VMEM((9, *early), LOW),
            pltpu.VMEM((3, *late), LOW),
            pltpu.VMEM((steps, 16, features), F32),
            dma((12, 2 * steps)),
            dma((12, 2 * steps)),
            dma((12,)),
            dma((steps,)),
            dma((steps,)),
            *[dma((3, rows_n))] * 6,
            *[dma((rows_n,))] * 4,
            dma((9,)),
            dma((rows_n + 1,)),
            pltpu.VMEM((16, features), F32),
        ],
        compiler_params=pltpu.CompilerParams(
            collective_id=0, has_side_effects=True, vmem_limit_bytes=VMEM_LIMIT
        ),
        cost_estimate=pl.CostEstimate(
            flops=4 * 10**10, bytes_accessed=8 * 10**7, transcendentals=8 * 10**6
        ),
        name="layer",
    )(*vectors, x_rows, cot, segments, *weights)


def finish_kernel(moved, *refs):
    sources = refs[: moved + 1]
    outs = refs[moved + 1 :]
    for src, dst in zip(sources[:moved], outs[:moved]):
        dst[...] = src[...].astype(dst.dtype)
    small = sources[moved]
    for index, dst in enumerate(outs[moved:-1]):
        dst[...] = small[index, :]
    outs[-1][...] = jnp.concatenate([small[index, :] for index in range(12, 16)])


def finish(blocks, result, grad_tokens, small, steps):
    arrays = [*blocks, result, grad_tokens]
    kinds = [F32] * len(blocks) + [result.dtype, grad_tokens.dtype]
    specs = [pl.BlockSpec((a.shape[0] // steps, a.shape[1]), lambda i: (i, 0)) for a in arrays]
    features = small.shape[1]
    vectors = [features] * 10 + [4 * features]
    shape = jax.ShapeDtypeStruct
    return pl.pallas_call(
        partial(finish_kernel, len(arrays)),
        grid=(steps,),
        out_shape=[shape(a.shape, kind) for a, kind in zip(arrays, kinds)]
        + [shape((size,), F32) for size in vectors],
        in_specs=[*specs, pl.BlockSpec(small.shape, lambda i: (0, 0))],
        out_specs=[*specs, *[pl.BlockSpec((size,), lambda i: (0,)) for size in vectors]],
        compiler_params=pltpu.CompilerParams(vmem_limit_bytes=VMEM_LIMIT),
        cost_estimate=pl.CostEstimate(
            flops=0, bytes_accessed=6 * sum(a.size for a in arrays), transcendentals=0
        ),
        name="finish",
    )(*arrays, small)


def on_device(
    mesh_shape,
    tokens,
    segments,
    w_query,
    b_query,
    w_key,
    w_value,
    b_value,
    w_out,
    b_out,
    gain_one,
    shift_one,
    w_up,
    b_up,
    w_down,
    b_down,
    gain_two,
    shift_two,
    cotangent,
):
    rows_n, part_len, features = tokens.shape
    flat = (rows_n * part_len, features)
    vectors = (b_query, b_value, b_out, gain_one, shift_one, b_down, gain_two, shift_two, b_up)
    outs = layer(
        mesh_shape,
        vectors,
        tokens.reshape(flat),
        cotangent.reshape(flat),
        segments,
        (w_query, w_key, w_value, w_out, w_up, w_down),
    )
    (g_query, g_key, g_value, g_out, g_up, g_down, result, grad_tokens, *vectors) = finish(
        outs[:6], *outs[8:], 3
    )
    shape = (rows_n, part_len, features)
    return (
        result.reshape(shape),
        grad_tokens.reshape(shape),
        g_query,
        vectors[8],
        g_key,
        g_value,
        vectors[9],
        g_out,
        vectors[0],
        vectors[1],
        vectors[2],
        g_up,
        vectors[10],
        g_down,
        vectors[3],
        vectors[4],
        vectors[5],
    )


def solution(mesh):
    tokens = P("rows", "pos", None)
    return jax.shard_map(
        partial(on_device, dict(mesh.shape)),
        mesh=mesh,
        in_specs=(tokens, P("rows", None), *[P()] * 15, tokens),
        out_specs=(tokens, tokens, *[P()] * 15),
        check_vma=False,
    )
```
